128 devices in a mesh: grp: 8 (over z, core), mem: 16 (over x, y).
Axes of the slice: x: 4, y: 4, z: 4, core: 2. Of those that a mesh axis runs over, the one named last changes fastest.
Arguments:
- send_rows: bfloat16 [128, 128, 16, 512], P(('grp', 'mem')), may hold values from -6 to 6
- slot_pos: int32 [128, 128, 16], P(('grp', 'mem')), may hold values from -1 to 1023, as said below
- lengths: int32 [128, 8], P(('grp', 'mem')), may hold values from 1 to 512, 1024 in all within a row
- candidates: bfloat16 [16384, 512], P(('grp', 'mem')), may hold values from -6 to 6
- target_ids: int32 [1024, 16], P(('grp', 'mem')), may hold values from 0 to 2047
- w_proj: bfloat16 [512, 2048], replicated, may hold values from -0.25 to 0.25
- w_out: bfloat16 [512, 512], replicated, may hold values from -0.25 to 0.25
- grad_hist_out: bfloat16 [131072, 512], P(('grp', 'mem')), may hold values from -6 to 6
- grad_tgt_out: bfloat16 [16384, 512], P(('grp', 'mem')), may hold values from -6 to 6
Outputs:
- out_hist: bfloat16 [131072, 512], P(('grp', 'mem'))
- out_tgt: bfloat16 [16384, 512], P(('grp', 'mem'))
- d_send: bfloat16 [128, 128, 16, 512], P(('grp', 'mem'))
- d_cand: float32 [16384, 512], P(('grp', 'mem'))
- d_w_proj: float32 [512, 2048], replicated
- d_w_out: float32 [512, 512], replicated
The draws below stay inside these ranges and needn't reach their ends.
Inputs may be any that keep to these rules, and one draw needn't show every extreme that they name: For each destination d the entries of slot_pos[d] that are not -1 are each of 0 to 1023 once; in slot_pos[d, s] the live slots come first; at most 16 slots are live for a pair, and every destination has a source with all 16 live. `lengths`: each row sums to 1024 and its largest entry is 512.
All inputs are finite; a program needn't handle non-finite values.
Results may differ from the reference program's by a relative error of at most 0.019.
Values may be sent and summed in bfloat16 or wider, within the bound.
No kernel may reach another device: no remote copies, remote signals or barrier semaphores. Data moves between devices by JAX's collectives and lax.ppermute only.
A program may use at most 192 MiB of HBM per device.

```python
import math
import jax
import jax.numpy as jnp
import numpy as np
from jax import lax

D = 512
HEADS = 8
ROWS_DEV = 1024
UPD = 8
NT = 16
RANKS = 128
LMAX = 512
CAP = 16
TOTAL = 131072
USERS = 1024
TARGETS = 16384
CAND_GRP = 2048
CANDS = 16384
N_GRP = 8
N_MEM = 16


def draw_slot_pos(key, part):
    key = jax.random.fold_in(key, 7)
    pair_key, force_key, order_key = jax.random.split(key, 3)
    half_cap = CAP // 2
    pair_count = RANKS // 2
    imbalance = jax.random.randint(pair_key, (RANKS, pair_count), -half_cap, half_cap + 1)
    forced = jax.random.randint(force_key, (RANKS, 1), 0, pair_count)
    imbalance = jnp.where(jnp.arange(pair_count)[None, :] == forced, half_cap, imbalance)
    counts = jnp.stack([half_cap + imbalance, half_cap - imbalance], axis=2).reshape(RANKS, RANKS)
    starts = jnp.cumsum(counts, axis=1) - counts
    orders = jax.vmap(lambda sub_key: jax.random.permutation(sub_key, ROWS_DEV))(jax.random.split(order_key, RANKS))
    slot_index = jnp.arange(CAP)
    wanted = starts[:, :, None] + slot_index[None, None, :]
    is_live = slot_index[None, None, :] < counts[:, :, None]
    picked = jnp.take_along_axis(orders, jnp.clip(wanted, 0, ROWS_DEV - 1).reshape(RANKS, RANKS * CAP), axis=1)
    return jnp.where(is_live, picked.reshape(RANKS, RANKS, CAP), -1).astype(jnp.int32)


def place_ends(drawn, rng, least, top_value):
    longest = drawn.shape.index(max(drawn.shape))
    spots = []
    for shift in (0, 1):
        where = [jax.random.randint(jax.random.fold_in(rng, axis), (), 0, length) for axis, length in enumerate(drawn.shape)]
        where[longest] = (where[longest] + shift) % drawn.shape[longest]
        spots.append(tuple(where))
    return drawn.at[spots[0]].set(least).at[spots[1]].set(top_value)


def level_of(own_key, dims, cuts, low, largest):
    def one(axis_at, parts):
        steps = jax.random.uniform(jax.random.fold_in(jax.random.fold_in(own_key, 6), axis_at), (parts,), jnp.float32, low / len(cuts), largest / len(cuts))
        return jnp.repeat(jnp.exp(steps), dims[axis_at] // parts).reshape((-1,) + (1,) * (len(dims) - axis_at - 1))

    factor_of = one(*cuts[0])
    for cut in cuts[1:]:
        factor_of = factor_of * one(*cut)
    return factor_of


def split_up(number_of, total, reach, skew):
    loads = [(1 << 20) // math.isqrt(standing ** skew) + 1 for standing in range(2, number_of + 1)]
    spare, holding = total - reach - (number_of - 1), [1] * (number_of - 1)
    while spare > 0:
        movable = [i for i in range(number_of - 1) if holding[i] < reach]
        pool, remaining = sum([loads[i] for i in movable]), spare
        for i in movable:
            addition = min(reach - holding[i], max(1, remaining * loads[i] // pool), spare)
            holding[i] = holding[i] + addition
            spare = spare - addition
    return np.array([reach] + holding)


def ragged(key, number_of, total, most, slope):
    if number_of == 2:
        one = jax.random.randint(key, (), max(1, total - most), min(most, total - 1) + 1)
        return jnp.stack([one, total - one])
    sizes = jnp.asarray(split_up(number_of, total, most, slope), jnp.int32)
    pairs = (number_of - 1) // 2
    giver, sink = sizes[1:1 + 2 * pairs:2], sizes[2:2 + 2 * pairs:2]
    room = jnp.minimum(giver - 1, most - sink)
    moved = jax.random.randint(jax.random.fold_in(key, 1), (pairs,), 0, 1 << 20) % (room + 1)
    sizes = sizes.at[1:1 + 2 * pairs:2].set(giver - moved).at[2:2 + 2 * pairs:2].set(sink + moved)
    return sizes[jax.random.permutation(jax.random.fold_in(key, 2), number_of)]


def noise(rng, shape, scale, limit, cuts=(), kind=jnp.bfloat16):
    values = scale * jax.random.normal(rng, shape, jnp.float32)
    if cuts:
        values = values * level_of(rng, shape, cuts, -0.22, 0.18)
    return jnp.clip(values, -limit, limit).astype(kind)


def setup_inputs(seed: int = 0) -> dict:
    key_list = jax.random.split(jax.random.key(seed), 10)
    send_rows = noise(key_list[0], (RANKS, RANKS, CAP, D), 1.0, 6.0, ((0, 128),))
    slot_pos = draw_slot_pos(jax.random.fold_in(key_list[9], 71), 0)
    lengths = jax.vmap(lambda own: ragged(own, UPD, ROWS_DEV, LMAX, 2))(jax.random.split(key_list[2], RANKS)).reshape((RANKS, UPD)).astype(jnp.int32)
    candidates = noise(key_list[3], (CANDS, D), 1.0, 6.0, ((0, 128),))
    target_ids = place_ends(jax.random.randint(key_list[4], (USERS, NT), 0, CAND_GRP), jax.random.fold_in(key_list[4], 1), 0, CAND_GRP - 1).astype(jnp.int32)
    w_proj = noise(key_list[5], (D, 4 * D), D ** -0.5, 0.25)
    w_out = noise(key_list[6], (D, D), D ** -0.5, 0.25)
    grad_hist_out = noise(key_list[7], (TOTAL, D), 1.0, 6.0, ((0, 128),))
    grad_tgt_out = noise(key_list[8], (TARGETS, D), 1.0, 6.0, ((0, 128),))
    return {"send_rows": send_rows, "slot_pos": slot_pos, "lengths": lengths, "candidates": candidates, "target_ids": target_ids, "w_proj": w_proj, "w_out": w_out, "grad_hist_out": grad_hist_out, "grad_tgt_out": grad_tgt_out}


norm_epsilon = 1e-05

def norm_rows(values):
    row_mean = lax.optimization_barrier(jnp.mean(values, axis=-1, keepdims=True))
    centred = values - row_mean
    variance = lax.optimization_barrier(jnp.mean(centred * centred, axis=-1, keepdims=True))
    return centred * lax.rsqrt(variance + norm_epsilon)

def attend_block(queries, key_rows, val_rows, allowed, score_scale):
    scores = jnp.einsum('qhe,khe->hqk', queries.astype(jnp.float32), key_rows.astype(jnp.float32)) * score_scale
    weights = jnp.where(allowed[None], jax.nn.silu(scores), 0.0).astype(queries.dtype)
    return jnp.einsum('hqk,khe->qhe', weights.astype(jnp.float32), val_rows.astype(jnp.float32))

def segment_ids(user_lengths, row_count):
    ends = jnp.cumsum(user_lengths)
    return lax.optimization_barrier(jnp.sum((jnp.arange(row_count)[:, None] >= ends[None, :]).astype(jnp.int32), axis=1))

def sequence_layer(x_hist, x_tgt, w_proj, w_out, seg_hist, seg_tgt):
    hist_rows = x_hist.shape[0]
    feature = x_hist.shape[1]
    head_size = feature // HEADS
    score_scale = 1.0 / head_size ** 0.5
    joined = jnp.concatenate([x_hist, x_tgt], axis=0)
    normed = norm_rows(joined.astype(jnp.float32)).astype(x_hist.dtype)
    projected = jax.nn.silu(jnp.dot(normed, w_proj, preferred_element_type=jnp.float32)).astype(x_hist.dtype)
    gate_rows = projected[:, :feature]
    val_rows = projected[:, feature:2 * feature].reshape(-1, HEADS, head_size)
    queries = projected[:, 2 * feature:3 * feature].reshape(-1, HEADS, head_size)
    key_rows = projected[:, 3 * feature:].reshape(-1, HEADS, head_size)
    row_block = min(512, hist_rows)
    positions = jnp.arange(hist_rows)
    outputs = []
    for first_row in range(0, hist_rows, row_block):
        last_row = first_row + row_block
        allowed = (seg_hist[first_row:last_row, None] == seg_hist[None, :last_row]) & (positions[first_row:last_row, None] >= positions[None, :last_row])
        outputs.append(attend_block(queries[first_row:last_row], key_rows[:last_row], val_rows[:last_row], allowed, score_scale))
    target_queries = queries[hist_rows:]
    target_allowed = seg_tgt[:, None] == seg_hist[None, :]
    target_out = attend_block(target_queries, key_rows[:hist_rows], val_rows[:hist_rows], target_allowed, score_scale)
    self_score = lax.optimization_barrier(jnp.sum(target_queries.astype(jnp.float32) * key_rows[hist_rows:].astype(jnp.float32), axis=-1)) * score_scale
    self_weight = jax.nn.silu(self_score).astype(x_hist.dtype)
    target_out = target_out + self_weight.astype(jnp.float32)[..., None] * val_rows[hist_rows:].astype(jnp.float32)
    outputs.append(target_out)
    attended = jnp.concatenate(outputs, axis=0).reshape(-1, feature)
    mixed_rows = (norm_rows(attended) * gate_rows.astype(jnp.float32)).astype(x_hist.dtype)
    result = (joined.astype(jnp.float32) + jnp.dot(mixed_rows, w_out, preferred_element_type=jnp.float32)).astype(x_hist.dtype)
    return (result[:hist_rows], result[hist_rows:])

def reference(send_rows, slot_pos, lengths, candidates, target_ids, w_proj, w_out, grad_hist_out, grad_tgt_out):
    by_target = jnp.swapaxes(send_rows, 0, 1)
    group_tables = candidates.reshape(N_GRP, CAND_GRP, D)
    tgt_count = UPD * NT
    seg_tgt = (jnp.arange(tgt_count) // NT).astype(jnp.int32)

    def one_device(carry, inputs):
        sum_proj, sum_out, cand_sums = carry
        arrived, positions_in, user_lengths, chosen, hist_tangent, tgt_tangent, device = inputs
        flat_rows = arrived.reshape(RANKS * CAP, D)
        flat_pos = positions_in.reshape(-1)
        landing = jnp.where(flat_pos < 0, ROWS_DEV, flat_pos)
        x_hist = jnp.zeros((ROWS_DEV + 1, D), send_rows.dtype).at[landing].set(flat_rows)[:ROWS_DEV]
        group_index = device // N_MEM
        group_table = lax.dynamic_index_in_dim(group_tables, group_index, 0, keepdims=False)
        x_tgt = jnp.take(group_table, chosen, axis=0)
        seg_hist = segment_ids(user_lengths, ROWS_DEV)

        def local_layer(hist_in, tgt_in, proj_in, out_in):
            return sequence_layer(hist_in, tgt_in, proj_in, out_in, seg_hist, seg_tgt)
        (out_hist, out_tgt), backward = jax.vjp(local_layer, x_hist, x_tgt, w_proj, w_out)
        grad_hist, grad_tgt, grad_proj, grad_out = backward((hist_tangent, tgt_tangent))
        fetched = jnp.take(grad_hist, jnp.clip(flat_pos, 0, ROWS_DEV - 1), axis=0)
        slot_grads = jnp.where(flat_pos[:, None] >= 0, fetched, jnp.zeros_like(fetched)).reshape(RANKS, CAP, D)
        partial_table = jax.ops.segment_sum(grad_tgt.astype(jnp.float32), chosen, num_segments=CAND_GRP)
        cand_sums = cand_sums.at[group_index].add(partial_table)
        sum_proj = sum_proj + grad_proj.astype(jnp.float32)
        sum_out = sum_out + grad_out.astype(jnp.float32)
        return ((sum_proj, sum_out, cand_sums), (out_hist, out_tgt, slot_grads))
    initial = (jnp.zeros((D, 4 * D), jnp.float32), jnp.zeros((D, D), jnp.float32), jnp.zeros((N_GRP, CAND_GRP, D), jnp.float32))
    inputs = (by_target, slot_pos, lengths, target_ids.reshape(RANKS, tgt_count), grad_hist_out.reshape(RANKS, ROWS_DEV, D), grad_tgt_out.reshape(RANKS, tgt_count, D), jnp.arange(RANKS, dtype=jnp.int32))
    (sum_proj, sum_out, cand_sums), (outs_hist, outs_tgt, slots_all) = lax.scan(one_device, initial, inputs)
    return (outs_hist.reshape(TOTAL, D), outs_tgt.reshape(TARGETS, D), jnp.swapaxes(slots_all, 0, 1), cand_sums.reshape(CANDS, D), sum_proj, sum_out)
```

```python
import jax
import jax.numpy as jnp
from jax import lax
from jax.experimental import pallas as pl
from jax.experimental.pallas import tpu as pltpu
from jax.sharding import PartitionSpec as P

HEADS = 8
EPS = 1e-05
BLK = 256
MASKED = -1e9
F32 = jnp.float32
BF16 = jnp.bfloat16
BOTH = ("grp", "mem")
NN = (((1,), (0,)), ((), ()))
NT = (((1,), (1,)), ((), ()))


def mm(left, right, dims=NN):
    return lax.dot_general(left, right, dims, preferred_element_type=F32)


def moments(values):
    centred = values - jnp.mean(values, axis=-1, keepdims=True)
    variance = jnp.mean(centred * centred, axis=-1, keepdims=True)
    return centred, lax.rsqrt(variance + EPS)


def layer_kernel(
    first_ref,
    arrived,
    pos_row,
    cand,
    tid_col,
    lo,
    hi,
    w_proj,
    w_out,
    g_hist,
    g_tgt,
    out_hist,
    out_tgt,
    normed_o,
    normed_t,
    mixed_t,
    rstd_o,
    d_pre,
    x_s,
    gate_s,
    q_s,
    km,
    vm,
    w_s,
    s_s,
    bias_s,
    a_acc,
    dq_acc,
    da_s,
    da_t,
    q_t,
    dk_t,
    dv_t,
):
    hist_rows = out_hist.shape[0]
    tgt_rows = out_tgt.shape[0]
    feature = out_hist.shape[1]
    blocks = hist_rows // BLK
    lane = lax.broadcasted_iota(jnp.int32, (1, 128), 1)
    low_half = jnp.where(lane < 64, 1.0, 0.0).astype(F32)
    halves = (low_half, 1.0 - low_half)

    def project(r0, size, table, hits):
        rows = pl.ds(r0, size)
        onehot = jnp.where(hits, 1.0, 0.0).astype(BF16)
        x = mm(onehot, table[...])
        x_s[rows, :] = x.astype(BF16)
        centred, rstd = moments(x)
        normed = centred * rstd
        rstd_o[rows, :] = rstd
        normed_t[:, rows] = normed.T.astype(BF16)
        normed = normed.astype(BF16)
        normed_o[rows, :] = normed
        for part in range(4):
            half = mm(normed, w_proj[:, part * feature : (part + 1) * feature]) * 0.5
            t = jnp.tanh(half)
            u = 1.0 + t
            act = half * u
            slope = 0.5 * u * (1.0 + half * (1.0 - t))
            d_pre[rows, part * feature : (part + 1) * feature] = slope.astype(BF16)
            if part == 0:
                gate_s[rows, :] = act.astype(BF16)
            elif part == 2:
                q_s[rows, :] = (act.astype(BF16) * 0.0625).astype(BF16)
            else:
                dest = vm if part == 1 else km
                for head in range(HEADS):
                    pair = act[:, (head // 2) * 128 : (head // 2 + 1) * 128]
                    dest[head, rows, :] = (pair * halves[head % 2]).astype(BF16)

    def project_hist(i, carry):
        r0 = pl.multiple_of(i * BLK, BLK)
        row = r0 + lax.broadcasted_iota(jnp.int32, (BLK, 1), 0)
        project(r0, BLK, arrived, pos_row[...] == row)
        return carry

    lax.fori_loop(0, blocks, project_hist, 0)
    col = lax.broadcasted_iota(jnp.int32, (1, cand.shape[0]), 1)
    project(hist_rows, tgt_rows, cand, tid_col[...] == col)
    dk_t[...] = jnp.zeros_like(dk_t)
    dv_t[...] = jnp.zeros_like(dv_t)

    def forward(r0, size, slot, k0, width, bias):
        rows, keys = pl.ds(r0, size), pl.ds(k0, width)
        bias_s[:size, :width] = bias
        for pair in range(HEADS // 2):
            cols = slice(pair * 128, (pair + 1) * 128)
            total = a_acc[:size, cols]
            for head in (2 * pair, 2 * pair + 1):
                half = mm(q_s[rows, cols], km[head, keys, :], NT) + bias_s[:size, :width]
                t = jnp.tanh(half)
                u = 1.0 + t
                weight = (half * u).astype(BF16)
                w_s[slot, head, :size, :width] = weight
                slope = 0.5 * u * (1.0 + half * (1.0 - t))
                s_s[slot, head, :size, :width] = slope.astype(BF16)
                total = total + mm(weight, vm[head, keys, :])
            a_acc[:size, cols] = total

    def backward(size, slot, k0, width):
        keys = pl.ds(k0, width)
        for pair in range(HEADS // 2):
            cols = slice(pair * 128, (pair + 1) * 128)
            total = dq_acc[:size, cols]
            for head in (2 * pair, 2 * pair + 1):
                d_weight = mm(da_s[:size, cols], vm[head, keys, :], NT)
                d_score = d_weight * s_s[slot, head, :size, :width].astype(F32)
                d_score = d_score.astype(BF16)
                total = total + mm(d_score, km[head, keys, :])
                own = slice(head * 64, (head + 1) * 64)
                dv_t[own, keys] += mm(da_t[own, :size], w_s[slot, head, :size, :width])
                dk_t[own, keys] += mm(q_t[own, :size], d_score)
            dq_acc[:size, cols] = total

    def middle(r0, size, out_ref, g_ref, o0):
        rows, own = pl.ds(r0, size), pl.ds(o0, size)
        centred, rstd = moments(a_acc[:size, :])
        normed = centred * rstd
        gate = gate_s[rows, :].astype(F32)
        mixed = normed * gate
        mixed_t[:, rows] = mixed.T.astype(BF16)
        update = mm(mixed.astype(BF16), w_out[...])
        out_ref[own, :] = (x_s[rows, :].astype(F32) + update).astype(BF16)
        d_mixed = mm(g_ref[own, :], w_out[...], NT)
        d_gate = d_mixed * normed * d_pre[rows, :feature].astype(F32)
        d_pre[rows, :feature] = d_gate.astype(BF16)
        d_normed = d_mixed * gate
        mean_d = jnp.mean(d_normed, axis=-1, keepdims=True)
        mean_dn = jnp.mean(d_normed * normed, axis=-1, keepdims=True)
        d_att = rstd * (d_normed - mean_d - normed * mean_dn)
        da_s[:size, :] = d_att.astype(BF16)
        da_t[:, :size] = d_att.T.astype(BF16)
        q_t[:, :size] = q_s[rows, :].astype(F32).T.astype(BF16)

    def finish(r0, size):
        rows, cols = pl.ds(r0, size), slice(2 * feature, 3 * feature)
        d_q = dq_acc[:size, :] * 0.125 * d_pre[rows, cols].astype(F32)
        d_pre[rows, cols] = d_q.astype(BF16)

    def bias_of(r0, size, k0):
        rows = pl.ds(r0, size)
        key = k0 + lax.broadcasted_iota(jnp.int32, (1, BLK), 1)
        allowed = (key >= lo[rows, :]) & (key <= hi[rows, :])
        return jnp.where(allowed, 0.0, MASKED).astype(F32)

    def hist_block(i, carry):
        r0 = pl.multiple_of(i * BLK, BLK)
        first = first_ref[i]
        a_acc[...] = jnp.zeros_like(a_acc)
        dq_acc[...] = jnp.zeros_like(dq_acc)

        def fwd(j, c):
            k0 = pl.multiple_of(j * BLK, BLK)
            forward(r0, BLK, j, k0, BLK, bias_of(r0, BLK, k0))
            return c

        def bwd(j, c):
            backward(BLK, j, pl.multiple_of(j * BLK, BLK), BLK)
            return c

        lax.fori_loop(first, i + 1, fwd, 0)
        middle(r0, BLK, out_hist, g_hist, r0)
        lax.fori_loop(first, i + 1, bwd, 0)
        finish(r0, BLK)
        return carry

    lax.fori_loop(0, blocks, hist_block, 0)

    a_acc[...] = jnp.zeros_like(a_acc)
    dq_acc[...] = jnp.zeros_like(dq_acc)

    def fwd_tgt(j, c):
        k0 = pl.multiple_of(j * BLK, BLK)
        forward(hist_rows, tgt_rows, j, k0, BLK, bias_of(hist_rows, tgt_rows, k0))
        return c

    def bwd_tgt(j, c):
        backward(tgt_rows, j, pl.multiple_of(j * BLK, BLK), BLK)
        return c

    lax.fori_loop(0, blocks, fwd_tgt, 0)
    same = lax.broadcasted_iota(jnp.int32, (tgt_rows, tgt_rows), 0) == lax.broadcasted_iota(
        jnp.int32, (tgt_rows, tgt_rows), 1
    )
    forward(
        hist_rows, tgt_rows, blocks, hist_rows, tgt_rows, jnp.where(same, 0.0, MASKED).astype(F32)
    )
    middle(hist_rows, tgt_rows, out_tgt, g_tgt, 0)
    lax.fori_loop(0, blocks, bwd_tgt, 0)
    backward(tgt_rows, blocks, hist_rows, tgt_rows)
    finish(hist_rows, tgt_rows)

    def spread(r0, size):
        rows = pl.ds(r0, size)
        vals, keys = slice(feature, 2 * feature), slice(3 * feature, 4 * feature)
        d_val = dv_t[:, rows].T * d_pre[rows, vals].astype(F32)
        d_pre[rows, vals] = d_val.astype(BF16)
        d_key = dk_t[:, rows].T * 2.0 * d_pre[rows, keys].astype(F32)
        d_pre[rows, keys] = d_key.astype(BF16)

    def spread_hist(i, carry):
        spread(pl.multiple_of(i * BLK, BLK), BLK)
        return carry

    lax.fori_loop(0, blocks, spread_hist, 0)
    spread(hist_rows, tgt_rows)


def weights_kernel(normed_t, mixed_t, d_pre, g_hist, g_tgt, d_proj, d_out):
    hist_rows = g_hist.shape[0]
    for part in range(d_proj.shape[1] // 512):
        cols = slice(part * 512, (part + 1) * 512)
        d_proj[:, cols] = mm(normed_t[...], d_pre[:, cols]).astype(BF16)
    total = mm(mixed_t[:, :hist_rows], g_hist[...])
    total = total + mm(mixed_t[:, hist_rows:], g_tgt[...])
    d_out[...] = total.astype(BF16)


def rows_kernel(
    d_pre, w_proj, normed, rstd, g_hist, g_tgt, pos_col, slot_grads, d_tgt, d_hist
):
    hist_rows = g_hist.shape[0]
    tgt_rows = g_tgt.shape[0]

    def back(r0, size, g_ref, out_ref, o0):
        rows, own = pl.ds(r0, size), pl.ds(o0, size)
        d_normed = mm(d_pre[rows, :], w_proj[...], NT)
        unit = normed[rows, :].astype(F32)
        mean_d = jnp.mean(d_normed, axis=-1, keepdims=True)
        mean_dn = jnp.mean(d_normed * unit, axis=-1, keepdims=True)
        d_x = rstd[rows, :] * (d_normed - mean_d - unit * mean_dn)
        out_ref[own, :] = (d_x + g_ref[own, :].astype(F32)).astype(BF16)

    back(hist_rows, tgt_rows, g_tgt, d_tgt, 0)

    def back_hist(i, carry):
        r0 = pl.multiple_of(i * BLK, BLK)
        back(r0, BLK, g_hist, d_hist, r0)
        return carry

    lax.fori_loop(0, hist_rows // BLK, back_hist, 0)

    def pick(i, carry):
        r0 = pl.multiple_of(i * BLK, BLK)
        row = lax.broadcasted_iota(jnp.int32, (1, hist_rows), 1)
        onehot = jnp.where(pos_col[pl.ds(r0, BLK), :] == row, 1.0, 0.0).astype(BF16)
        slot_grads[pl.ds(r0, BLK), :] = mm(onehot, d_hist[...]).astype(BF16)
        return carry

    lax.fori_loop(0, slot_grads.shape[0] // BLK, pick, 0)


def cand_kernel(own_ids, picked, rows, out):
    hits = own_ids[...] == picked[...]
    out[...] = mm(jnp.where(hits, 1.0, 0.0).astype(BF16), rows[...])


VMEM = pl.BlockSpec(memory_space=pltpu.VMEM)
SMEM = pl.BlockSpec(memory_space=pltpu.SMEM)


def params(mib):
    return pltpu.CompilerParams(vmem_limit_bytes=mib << 20)


AXES = {"z": (4, 32), "c": (2, 16), "x": (4, 4), "y": (4, 1)}


def local(
    send_rows, slot_pos, lengths, candidates, target_ids, w_proj, w_out, g_hist, g_tgt
):
    peers, capacity, feature = send_rows.shape[1:]
    slots = peers * capacity
    hist_rows, tgt_rows = g_hist.shape[0], g_tgt.shape[0]
    all_rows = hist_rows + tgt_rows
    users, tgt_each = target_ids.shape
    table = lax.all_gather(candidates, "mem", axis=0, tiled=True)
    arrived = lax.all_to_all(send_rows, BOTH, split_axis=1, concat_axis=0, tiled=True)
    arrived = arrived.reshape(slots, feature)

    pos_row = slot_pos.reshape(1, slots)
    pos_col = slot_pos.reshape(slots, 1)
    ends = jnp.cumsum(lengths[0])
    starts = ends - lengths[0]
    row = jnp.arange(hist_rows)[:, None]
    hist_lo = jnp.max(jnp.where(row >= starts[None, :], starts[None, :], 0), axis=1)
    lo = jnp.concatenate([hist_lo, jnp.repeat(starts, tgt_each)]).astype(jnp.int32)[:, None]
    hi = jnp.concatenate([jnp.arange(hist_rows), jnp.repeat(ends - 1, tgt_each)])
    hi = hi.astype(jnp.int32)[:, None]
    first = (hist_lo[::BLK] // BLK).astype(jnp.int32)

    sds = jax.ShapeDtypeStruct
    out_hist, out_tgt, normed, normed_t, mixed_t, rstd, d_pre = pl.pallas_call(
        layer_kernel,
        out_shape=(
            sds((hist_rows, feature), BF16),
            sds((tgt_rows, feature), BF16),
            sds((all_rows, feature), BF16),
            sds((feature, all_rows), BF16),
            sds((feature, all_rows), BF16),
            sds((all_rows, 1), F32),
            sds((all_rows, 4 * feature), BF16),
        ),
        in_specs=[SMEM] + [VMEM] * 10,
        out_specs=(VMEM,) * 7,
        scratch_shapes=[
            pltpu.VMEM((all_rows, feature), BF16),
            pltpu.VMEM((all_rows, feature), BF16),
            pltpu.VMEM((all_rows, feature), BF16),
            pltpu.VMEM((HEADS, all_rows, 128), BF16),
            pltpu.VMEM((HEADS, all_rows, 128), BF16),
            pltpu.VMEM((hist_rows // BLK + 1, HEADS, BLK, BLK), BF16),
            pltpu.VMEM((hist_rows // BLK + 1, HEADS, BLK, BLK), BF16),
            pltpu.VMEM((BLK, BLK), F32),
            pltpu.VMEM((BLK, feature), F32),
            pltpu.VMEM((BLK, feature), F32),
            pltpu.VMEM((BLK, feature), BF16),
            pltpu.VMEM((feature, BLK), BF16),
            pltpu.VMEM((feature, BLK), BF16),
            pltpu.VMEM((feature, all_rows), F32),
            pltpu.VMEM((feature, all_rows), F32),
        ],
        compiler_params=params(58),
        name="layer",
    )(
        first,
        arrived,
        pos_row,
        table,
        target_ids.reshape(tgt_rows, 1),
        lo,
        hi,
        w_proj,
        w_out,
        g_hist,
        g_tgt,
    )

    d_proj, d_out = pl.pallas_call(
        weights_kernel,
        out_shape=(sds(w_proj.shape, BF16), sds(w_out.shape, BF16)),
        in_specs=[VMEM] * 5,
        out_specs=(VMEM, VMEM),
        compiler_params=params(40),
        name="weights",
    )(normed_t, mixed_t, d_pre, g_hist, g_tgt)

    slot_grads, d_tgt = pl.pallas_call(
        rows_kernel,
        out_shape=(sds((slots, feature), BF16), sds((tgt_rows, feature), BF16)),
        in_specs=[VMEM] * 7,
        out_specs=(VMEM, VMEM),
        scratch_shapes=[pltpu.VMEM((hist_rows, feature), BF16)],
        compiler_params=params(40),
        name="rows",
    )(d_pre, w_proj, normed, rstd, g_hist, g_tgt, pos_col)

    sum_proj, sum_out = reduce_weights(d_proj, d_out)

    returned = lax.all_to_all(
        slot_grads.reshape(peers, 1, capacity, feature),
        BOTH,
        split_axis=0,
        concat_axis=1,
        tiled=True,
    )

    picked = lax.all_gather(target_ids.reshape(1, tgt_rows), "mem", axis=1, tiled=True)
    tgt_grads = lax.all_gather(d_tgt, "mem", axis=0, tiled=True)
    mine = lax.axis_index("mem") * candidates.shape[0] + jnp.arange(
        candidates.shape[0], dtype=jnp.int32
    )
    d_cand = pl.pallas_call(
        cand_kernel,
        out_shape=sds(candidates.shape, F32),
        in_specs=[VMEM] * 3,
        out_specs=VMEM,
        name="cand",
    )(mine.astype(jnp.int32)[:, None], picked, tgt_grads)
    return (out_hist, out_tgt, returned, d_cand, sum_proj, sum_out)


def reduce_weights(d_proj, d_out):
    both = jnp.concatenate([d_proj.reshape(2048, 512), d_out], axis=0).reshape(128, 16, 1280 // 2)
    both = lax.all_to_all(both, BOTH, split_axis=0, concat_axis=0, tiled=True)
    total = jnp.sum(both.astype(F32), axis=0).astype(BF16)
    gathered = lax.all_gather(total, "mem", axis=0, tiled=True)
    gathered = lax.all_gather(gathered, "grp", axis=0, tiled=True)
    gathered = gathered.reshape(2560, 512).astype(F32)
    return gathered[:2048].reshape(512, 2048), gathered[2048:]


def solution(mesh):
    placed = (
        P(BOTH, None, None, None),
        P(BOTH, None, None),
        P(BOTH, None),
        P(BOTH, None),
        P(BOTH, None),
        P(),
        P(),
        P(BOTH, None),
        P(BOTH, None),
    )
    return jax.shard_map(
        local,
        mesh=mesh,
        in_specs=placed,
        out_specs=(
            P(BOTH, None),
            P(BOTH, None),
            P(BOTH, None, None, None),
            P(BOTH, None),
            P(),
            P(),
        ),
        check_vma=False,
    )
```

```python
import jax
import jax.numpy as jnp
from jax import lax
from jax.experimental import pallas as pl
from jax.experimental.pallas import tpu as pltpu
from jax.sharding import PartitionSpec as P

HEADS = 8
EPS = 1e-05
BLK = 256
MASKED = -1e9
F32 = jnp.float32
BF16 = jnp.bfloat16
BOTH = ("grp", "mem")
NN = (((1,), (0,)), ((), ()))
NT = (((1,), (1,)), ((), ()))


def mm(left, right, dims=NN):
    return lax.dot_general(left, right, dims, preferred_element_type=F32)


def moments(values):
    centred = values - jnp.mean(values, axis=-1, keepdims=True)
    variance = jnp.mean(centred * centred, axis=-1, keepdims=True)
    return centred, lax.rsqrt(variance + EPS)


def head_masks():
    lane = lax.broadcasted_iota(jnp.int32, (1, 128), 1)
    low_half = jnp.where(lane < 64, 1.0, 0.0).astype(F32)
    return (low_half, 1.0 - low_half)


def silu_parts(half):
    t = jnp.tanh(half)
    u = 1.0 + t
    return half * u, 0.5 * u * (1.0 + half * (1.0 - t))


def one_hot(hits):
    return jnp.where(hits, 1.0, 0.0).astype(BF16)


def split_heads(act, dest, rows):
    halves = head_masks()
    for head in range(HEADS):
        pair = act[:, (head // 2) * 128 : (head // 2 + 1) * 128]
        dest[head, rows, :] = (pair * halves[head % 2]).astype(BF16)


def score_bias(lo, hi, k0):
    key = k0 + lax.broadcasted_iota(jnp.int32, (1, BLK), 1)
    allowed = (key >= lo) & (key <= hi)
    return jnp.where(allowed, 0.0, MASKED).astype(F32)


def forward(q_ref, rows, size, km, vm, keys, width, w_s, s_s, slot, bias_s, a_acc):
    for pair in range(HEADS // 2):
        cols = slice(pair * 128, (pair + 1) * 128)
        total = a_acc[:size, cols]
        for head in (2 * pair, 2 * pair + 1):
            half = mm(q_ref[rows, cols], km[head, keys, :], NT) + bias_s[:size, :width]
            weight, slope = silu_parts(half)
            weight = weight.astype(BF16)
            w_s[slot, head, :size, :width] = weight
            s_s[slot, head, :size, :width] = slope.astype(BF16)
            total = total + mm(weight, vm[head, keys, :])
        a_acc[:size, cols] = total


def backward(size, km, vm, keys, width, w_s, s_s, slot, da_s, da_t, q_t, dq_acc, dk_t, dv_t):
    for pair in range(HEADS // 2):
        cols = slice(pair * 128, (pair + 1) * 128)
        total = dq_acc[:size, cols]
        for head in (2 * pair, 2 * pair + 1):
            d_weight = mm(da_s[:size, cols], vm[head, keys, :], NT)
            d_score = d_weight * s_s[slot, head, :size, :width].astype(F32)
            d_score = d_score.astype(BF16)
            total = total + mm(d_score, km[head, keys, :])
            own = slice(head * 64, (head + 1) * 64)
            dv_t[own, keys] += mm(da_t[own, :size], w_s[slot, head, :size, :width])
            dk_t[own, keys] += mm(q_t[own, :size], d_score)
        dq_acc[:size, cols] = total


def middle(attended, x, gate, g, w_out):
    centred, rstd = moments(attended)
    normed = centred * rstd
    mixed = normed * gate
    out = (x + mm(mixed.astype(BF16), w_out)).astype(BF16)
    d_mixed = mm(g, w_out, NT)
    d_normed = d_mixed * gate
    mean_d = jnp.mean(d_normed, axis=-1, keepdims=True)
    mean_dn = jnp.mean(d_normed * normed, axis=-1, keepdims=True)
    d_att = rstd * (d_normed - mean_d - normed * mean_dn)
    return out, mixed, d_mixed * normed, d_att


def hist_kernel(
    first_ref,
    arrived,
    pos_row,
    lo,
    hi,
    w_proj,
    w_out,
    g_hist,
    out_hist,
    normed_o,
    rstd_o,
    normed_t,
    mixed_t,
    km,
    vm,
    dk_t,
    dv_t,
    d_gq,
    sl_vk,
    x_s,
    gate_s,
    q_s,
    w_s,
    s_s,
    bias_s,
    a_acc,
    dq_acc,
    da_s,
    da_t,
    q_t,
):
    hist_rows, feature = out_hist.shape
    blocks = hist_rows // BLK
    first_cols, last_cols = slice(0, feature), slice(feature, 2 * feature)

    def project(i, carry):
        r0 = pl.multiple_of(i * BLK, BLK)
        rows = pl.ds(r0, BLK)
        row = r0 + lax.broadcasted_iota(jnp.int32, (BLK, 1), 0)
        x = mm(one_hot(pos_row[...] == row), arrived[...])
        x_s[rows, :] = x.astype(BF16)
        centred, rstd = moments(x)
        normed = centred * rstd
        rstd_o[rows, :] = rstd
        normed_t[:, rows] = normed.T.astype(BF16)
        normed = normed.astype(BF16)
        normed_o[rows, :] = normed
        for part in range(4):
            half = mm(normed, w_proj[:, part * feature : (part + 1) * feature]) * 0.5
            act, slope = silu_parts(half)
            slope = slope.astype(BF16)
            if part == 0:
                gate_s[rows, :] = act.astype(BF16)
                d_gq[rows, first_cols] = slope
            elif part == 1:
                split_heads(act, vm, rows)
                sl_vk[rows, first_cols] = slope
            elif part == 2:
                q_s[rows, :] = (act.astype(BF16) * 0.0625).astype(BF16)
                d_gq[rows, last_cols] = slope
            else:
                split_heads(act, km, rows)
                sl_vk[rows, last_cols] = slope
        return carry

    lax.fori_loop(0, blocks, project, 0)
    dk_t[...] = jnp.zeros_like(dk_t)
    dv_t[...] = jnp.zeros_like(dv_t)

    def hist_block(i, carry):
        r0 = pl.multiple_of(i * BLK, BLK)
        rows = pl.ds(r0, BLK)
        first = first_ref[i]
        a_acc[...] = jnp.zeros_like(a_acc)
        dq_acc[...] = jnp.zeros_like(dq_acc)

        def fwd(j, c):
            k0 = pl.multiple_of(j * BLK, BLK)
            keys = pl.ds(k0, BLK)
            bias_s[...] = score_bias(lo[rows, :], hi[rows, :], k0)
            forward(q_s, rows, BLK, km, vm, keys, BLK, w_s, s_s, j, bias_s, a_acc)
            return c

        def bwd(j, c):
            keys = pl.ds(pl.multiple_of(j * BLK, BLK), BLK)
            backward(
                BLK, km, vm, keys, BLK, w_s, s_s, j, da_s, da_t, q_t, dq_acc, dk_t, dv_t
            )
            return c

        lax.fori_loop(first, i + 1, fwd, 0)
        out, mixed, d_gate, d_att = middle(
            a_acc[...], x_s[rows, :].astype(F32), gate_s[rows, :].astype(F32), g_hist[rows, :], w_out[...]
        )
        out_hist[rows, :] = out
        mixed_t[:, rows] = mixed.T.astype(BF16)
        d_gq[rows, first_cols] = (d_gate * d_gq[rows, first_cols].astype(F32)).astype(BF16)
        da_s[...] = d_att.astype(BF16)
        da_t[...] = d_att.T.astype(BF16)
        q_t[...] = q_s[rows, :].astype(F32).T.astype(BF16)
        lax.fori_loop(first, i + 1, bwd, 0)
        d_q = dq_acc[...] * 0.125 * d_gq[rows, last_cols].astype(F32)
        d_gq[rows, last_cols] = d_q.astype(BF16)
        return carry

    lax.fori_loop(0, blocks, hist_block, 0)


def tgt_kernel(
    core_ref,
    cand,
    tid_col,
    tid_row,
    lo,
    hi,
    w_proj,
    w_out,
    g_tgt,
    km,
    vm,
    dk_in,
    dv_in,
    d_gq,
    sl_vk,
    normed_t,
    mixed_t,
    g_hist,
    out_tgt,
    d_tgt,
    d_vk,
    keep,
    give,
    gate_s,
    q_s,
    km_own,
    vm_own,
    d_pre,
    w_s,
    s_s,
    bias_s,
    a_acc,
    dq_acc,
    da_s,
    da_t,
    q_t,
    dk_t,
    dv_t,
    dk_own,
    dv_own,
    tgt_t,
):
    tgt_rows, feature = out_tgt.shape
    hist_rows = g_hist.shape[0]
    blocks = hist_rows // BLK
    every = slice(0, tgt_rows)
    part_cols = [slice(part * feature, (part + 1) * feature) for part in range(4)]
    col = lax.broadcasted_iota(jnp.int32, (1, cand.shape[0]), 1)
    x = mm(one_hot(tid_col[...] == col), cand[...])
    centred, rstd = moments(x)
    unit = centred * rstd
    normed = unit.astype(BF16)
    tgt_t[0] = unit.T.astype(BF16)
    for part in range(4):
        half = mm(normed, w_proj[:, part_cols[part]]) * 0.5
        act, slope = silu_parts(half)
        d_pre[:, part_cols[part]] = slope.astype(BF16)
        if part == 0:
            gate_s[...] = act.astype(BF16)
        elif part == 1:
            split_heads(act, vm_own, every)
        elif part == 2:
            q_s[...] = (act.astype(BF16) * 0.0625).astype(BF16)
        else:
            split_heads(act, km_own, every)

    a_acc[...] = jnp.zeros_like(a_acc)
    dq_acc[...] = jnp.zeros_like(dq_acc)
    dk_own[...] = jnp.zeros_like(dk_own)
    dv_own[...] = jnp.zeros_like(dv_own)
    dk_t[...] = dk_in[...]
    dv_t[...] = dv_in[...]

    def fwd(j, c):
        k0 = pl.multiple_of(j * BLK, BLK)
        keys = pl.ds(k0, BLK)
        bias_s[...] = score_bias(lo[...], hi[...], k0)
        forward(q_s, every, tgt_rows, km, vm, keys, BLK, w_s, s_s, j, bias_s, a_acc)
        return c

    def bwd(j, c):
        keys = pl.ds(pl.multiple_of(j * BLK, BLK), BLK)
        backward(
            tgt_rows, km, vm, keys, BLK, w_s, s_s, j, da_s, da_t, q_t, dq_acc, dk_t, dv_t
        )
        return c

    lax.fori_loop(0, blocks, fwd, 0)
    same = lax.broadcasted_iota(jnp.int32, (tgt_rows, tgt_rows), 0) == lax.broadcasted_iota(
        jnp.int32, (tgt_rows, tgt_rows), 1
    )
    bias_s[:, :tgt_rows] = jnp.where(same, 0.0, MASKED).astype(F32)
    forward(
        q_s, every, tgt_rows, km_own, vm_own, every, tgt_rows, w_s, s_s, blocks, bias_s, a_acc
    )
    out, mixed, d_gate, d_att = middle(
        a_acc[...], x, gate_s[...].astype(F32), g_tgt[...], w_out[...]
    )
    out_tgt[...] = out
    tgt_t[1] = mixed.T.astype(BF16)
    d_pre[:, part_cols[0]] = (d_gate * d_pre[:, part_cols[0]].astype(F32)).astype(BF16)
    da_s[...] = d_att.astype(BF16)
    da_t[...] = d_att.T.astype(BF16)
    q_t[...] = q_s[...].astype(F32).T.astype(BF16)
    lax.fori_loop(0, blocks, bwd, 0)
    backward(
        tgt_rows, km_own, vm_own, every, tgt_rows, w_s, s_s, blocks,
        da_s, da_t, q_t, dq_acc, dk_own, dv_own,
    )
    grads = (None, dv_own[...].T, dq_acc[...] * 0.125, dk_own[...].T * 2.0)
    for part in (1, 2, 3):
        d_part = grads[part] * d_pre[:, part_cols[part]].astype(F32)
        d_pre[:, part_cols[part]] = d_part.astype(BF16)

    d_normed = mm(d_pre[...], w_proj[...], NT)
    mean_d = jnp.mean(d_normed, axis=-1, keepdims=True)
    mean_dn = jnp.mean(d_normed * unit, axis=-1, keepdims=True)
    d_x = rstd * (d_normed - mean_d - unit * mean_dn) + g_tgt[...].astype(F32)
    d_tgt[every, :] = d_x.astype(BF16)
    ids = tid_row[...]
    high = lax.shift_right_logical(ids, 6)
    low = ids - high * 64
    d_tgt[tgt_rows:, :] = jnp.zeros((d_tgt.shape[0] - tgt_rows, feature), BF16)
    wide = (d_tgt.shape[0] - tgt_rows, tgt_rows)
    d_tgt[tgt_rows:, :tgt_rows] = jnp.broadcast_to(high.astype(F32), wide).astype(BF16)
    d_tgt[tgt_rows:, tgt_rows : 2 * tgt_rows] = jnp.broadcast_to(low.astype(F32), wide).astype(BF16)

    def spread(i, carry):
        rows = pl.ds(pl.multiple_of(i * BLK, BLK), BLK)
        vals, keys = slice(0, feature), slice(feature, 2 * feature)
        d_vk[rows, vals] = (dv_t[:, rows].T * sl_vk[rows, vals].astype(F32)).astype(BF16)
        d_vk[rows, keys] = (dk_t[:, rows].T * 2.0 * sl_vk[rows, keys].astype(F32)).astype(BF16)
        return carry

    lax.fori_loop(0, blocks, spread, 0)

    core = core_ref[0]
    half_rows = feature // 2
    for dest, half in ((give, 1 - core), (keep, core)):
        rows = pl.ds(pl.multiple_of(half * half_rows, half_rows), half_rows)
        for part in range(5):
            if part < 4:
                source = (d_gq, d_vk)[part % 2]
                cols = slice((part // 2) * feature, (part // 2 + 1) * feature)
                total = mm(normed_t[rows, :], source[:, cols])
                total = total + mm(tgt_t[0, rows, :], d_pre[:, part_cols[part]])
            else:
                total = mm(mixed_t[rows, :], g_hist[...]) + mm(tgt_t[1, rows, :], g_tgt[...])
            for group, dest_cols, cols in segments(part, feature):
                piece = total[:, cols].reshape(16, 16, cols.stop - cols.start)
                dest[:, group, :, dest_cols] = piece.astype(BF16)


def segments(part, feature):
    found, begin = [], part * feature
    while begin < (part + 1) * feature:
        group = begin // 640
        end = min((part + 1) * feature, (group + 1) * 640)
        found.append(
            (group, slice(begin - group * 640, end - group * 640), slice(begin - part * feature, end - part * feature))
        )
        begin = end
    return found


def rows_kernel(d_gq, d_vk, w_proj, normed, rstd, g_hist, pos_col, slot_grads, d_hist):
    hist_rows, feature = g_hist.shape

    def back(i, carry):
        rows = pl.ds(pl.multiple_of(i * BLK, BLK), BLK)
        d_normed = jnp.zeros((BLK, feature), F32)
        for part in range(4):
            cols = slice((part // 2) * feature, (part // 2 + 1) * feature)
            source = (d_gq, d_vk)[part % 2]
            weights = w_proj[:, part * feature : (part + 1) * feature]
            d_normed = d_normed + mm(source[rows, cols], weights, NT)
        unit = normed[rows, :].astype(F32)
        mean_d = jnp.mean(d_normed, axis=-1, keepdims=True)
        mean_dn = jnp.mean(d_normed * unit, axis=-1, keepdims=True)
        d_x = rstd[rows, :] * (d_normed - mean_d - unit * mean_dn)
        d_hist[rows, :] = (d_x + g_hist[rows, :].astype(F32)).astype(BF16)
        return carry

    lax.fori_loop(0, hist_rows // BLK, back, 0)

    def pick(i, carry):
        rows = pl.ds(pl.multiple_of(i * BLK, BLK), BLK)
        row = lax.broadcasted_iota(jnp.int32, (1, hist_rows), 1)
        onehot = one_hot(pos_col[rows, :] == row)
        slot_grads[rows, :] = mm(onehot, d_hist[...]).astype(BF16)
        return carry

    lax.fori_loop(0, slot_grads.shape[0] // BLK, pick, 0)


def cand_kernel(first_ref, rows, out):
    count, feature = out.shape
    own = first_ref[0] + lax.broadcasted_iota(jnp.int32, (count, 1), 0)
    total = jnp.zeros((count, feature), F32)
    for peer in range(rows.shape[0]):
        high = rows[peer, count : count + 16, :count].astype(F32)[:1]
        low = rows[peer, count : count + 16, count : 2 * count].astype(F32)[:1]
        ids = (high * 64.0 + low).astype(jnp.int32)
        total = total + mm(one_hot(own == ids), rows[peer, :count, :])
    out[...] = total


def sums_kernel(core_ref, own, other, d_proj, d_out):
    half_rows, feature = d_proj.shape[0] // 2, d_out.shape[1]
    for source, half in ((own, core_ref[0]), (other, 1 - core_ref[0])):
        rows = pl.ds(pl.multiple_of(half * half_rows, half_rows), half_rows)
        for part in range(5):
            for group, source_cols, cols in segments(part, feature):
                piece = source[:, group, :, source_cols].astype(F32)
                piece = piece.reshape(half_rows, cols.stop - cols.start)
                if part < 4:
                    d_proj[rows, part * feature + cols.start : part * feature + cols.stop] = piece
                else:
                    d_out[rows, cols] = piece


VMEM = pl.BlockSpec(memory_space=pltpu.VMEM)
SMEM = pl.BlockSpec(memory_space=pltpu.SMEM)


def params(mib):
    return pltpu.CompilerParams(vmem_limit_bytes=mib << 20)


def cost(flops, nbytes):
    return pl.CostEstimate(flops=flops, bytes_accessed=nbytes, transcendentals=0)


def local(
    send_rows, slot_pos, lengths, candidates, target_ids, w_proj, w_out, g_hist, g_tgt
):
    peers, capacity, feature = send_rows.shape[1:]
    slots = peers * capacity
    hist_rows, tgt_rows = g_hist.shape[0], g_tgt.shape[0]
    blocks = hist_rows // BLK
    each = target_ids.shape[1]
    table = lax.all_gather(candidates, "mem", axis=0, tiled=True)
    arrived = lax.all_to_all(send_rows, BOTH, split_axis=1, concat_axis=0, tiled=True)
    arrived = arrived.reshape(slots, feature)

    pos_row = slot_pos.reshape(1, slots)
    pos_col = slot_pos.reshape(slots, 1)
    ends = jnp.cumsum(lengths[0])
    starts = ends - lengths[0]
    row = jnp.arange(hist_rows, dtype=jnp.int32)[:, None]
    hist_lo = jnp.max(jnp.where(row >= starts[None, :], starts[None, :], 0), axis=1)
    first = (hist_lo[::BLK] // BLK).astype(jnp.int32)
    tgt_lo = jnp.repeat(starts, each).astype(jnp.int32)[:, None]
    tgt_hi = jnp.repeat(ends - 1, each).astype(jnp.int32)[:, None]
    core = lax.rem(lax.axis_index("grp"), 2).astype(jnp.int32)[None]

    sds = jax.ShapeDtypeStruct
    heads_shape = (HEADS, hist_rows, 128)
    out_hist, normed, rstd, normed_t, mixed_t, km, vm, dk_t, dv_t, d_gq, sl_vk = pl.pallas_call(
        hist_kernel,
        out_shape=(
            sds((hist_rows, feature), BF16),
            sds((hist_rows, feature), BF16),
            sds((hist_rows, 1), F32),
            sds((feature, hist_rows), BF16),
            sds((feature, hist_rows), BF16),
            sds(heads_shape, BF16),
            sds(heads_shape, BF16),
            sds((feature, hist_rows), F32),
            sds((feature, hist_rows), F32),
            sds((hist_rows, 2 * feature), BF16),
            sds((hist_rows, 2 * feature), BF16),
        ),
        in_specs=[SMEM] + [VMEM] * 7,
        out_specs=(VMEM,) * 11,
        scratch_shapes=[
            pltpu.VMEM((hist_rows, feature), BF16),
            pltpu.VMEM((hist_rows, feature), BF16),
            pltpu.VMEM((hist_rows, feature), BF16),
            pltpu.VMEM((blocks, HEADS, BLK, BLK), BF16),
            pltpu.VMEM((blocks, HEADS, BLK, BLK), BF16),
            pltpu.VMEM((BLK, BLK), F32),
            pltpu.VMEM((BLK, feature), F32),
            pltpu.VMEM((BLK, feature), F32),
            pltpu.VMEM((BLK, feature), BF16),
            pltpu.VMEM((feature, BLK), BF16),
            pltpu.VMEM((feature, BLK), BF16),
        ],
        compiler_params=params(HIST_MIB),
        cost_estimate=cost(16 << 30, 24 << 20),
        name="hist",
    )(first, arrived, pos_row, hist_lo.astype(jnp.int32)[:, None], row, w_proj, w_out, g_hist)

    pieces = (16, 4, 16, 640)
    out_tgt, d_tgt, d_vk, keep, give = pl.pallas_call(
        tgt_kernel,
        out_shape=(
            sds((tgt_rows, feature), BF16),
            sds((tgt_rows + 16, feature), BF16),
            sds((hist_rows, 2 * feature), BF16),
            sds(pieces, BF16),
            sds(pieces, BF16),
        ),
        in_specs=[SMEM] + [VMEM] * 17,
        out_specs=(VMEM,) * 5,
        scratch_shapes=[
            pltpu.VMEM((tgt_rows, feature), BF16),
            pltpu.VMEM((tgt_rows, feature), BF16),
            pltpu.VMEM((HEADS, tgt_rows, 128), BF16),
            pltpu.VMEM((HEADS, tgt_rows, 128), BF16),
            pltpu.VMEM((tgt_rows, 4 * feature), BF16),
            pltpu.VMEM((blocks + 1, HEADS, tgt_rows, BLK), BF16),
            pltpu.VMEM((blocks + 1, HEADS, tgt_rows, BLK), BF16),
            pltpu.VMEM((tgt_rows, BLK), F32),
            pltpu.VMEM((tgt_rows, feature), F32),
            pltpu.VMEM((tgt_rows, feature), F32),
            pltpu.VMEM((tgt_rows, feature), BF16),
            pltpu.VMEM((feature, tgt_rows), BF16),
            pltpu.VMEM((feature, tgt_rows), BF16),
            pltpu.VMEM((feature, hist_rows), F32),
            pltpu.VMEM((feature, hist_rows), F32),
            pltpu.VMEM((feature, tgt_rows), F32),
            pltpu.VMEM((feature, tgt_rows), F32),
            pltpu.VMEM((2, feature, tgt_rows), BF16),
        ],
        compiler_params=params(TGT_MIB),
        cost_estimate=cost(6 << 30, 28 << 20),
        name="tgt",
    )(
        core,
        table,
        target_ids.reshape(tgt_rows, 1),
        target_ids.reshape(1, tgt_rows),
        tgt_lo,
        tgt_hi,
        w_proj,
        w_out,
        g_tgt,
        km,
        vm,
        dk_t,
        dv_t,
        d_gq,
        sl_vk,
        normed_t,
        mixed_t,
        g_hist,
    )

    swap = core_swap()
    swapped = lax.ppermute(give, BOTH, swap)
    chip_sum = (keep.astype(F32) + swapped.astype(F32)).astype(BF16)
    chip_sum = chip_sum.reshape(64, 1, 16, 640)
    scattered = lax.all_to_all(
        chip_sum, BOTH, split_axis=0, concat_axis=1, tiled=True, axis_index_groups=same_core()
    )
    slot_grads = pl.pallas_call(
        rows_kernel,
        out_shape=sds((slots, feature), BF16),
        in_specs=[VMEM] * 7,
        out_specs=VMEM,
        scratch_shapes=[pltpu.VMEM((hist_rows, feature), BF16)],
        compiler_params=params(ROWS_MIB),
        cost_estimate=cost(5 << 30, 16 << 20),
        name="rows",
    )(d_gq, d_vk, w_proj, normed, rstd, g_hist, pos_col)
    total = jnp.sum(scattered.reshape(64, 16, 640).astype(F32), axis=0).astype(BF16)

    returned = lax.all_to_all(
        slot_grads.reshape(peers, 1, capacity, feature),
        BOTH,
        split_axis=0,
        concat_axis=1,
        tiled=True,
    )
    own = lax.all_to_all(
        jnp.broadcast_to(total[None, None], (64, 1, 16, 640)),
        BOTH,
        split_axis=0,
        concat_axis=1,
        tiled=True,
        axis_index_groups=same_core(),
    ).reshape(pieces)
    other = lax.ppermute(own, BOTH, swap)
    sum_proj, sum_out = pl.pallas_call(
        sums_kernel,
        out_shape=(sds(w_proj.shape, F32), sds(w_out.shape, F32)),
        in_specs=[SMEM, VMEM, VMEM],
        out_specs=(VMEM, VMEM),
        compiler_params=params(16),
        name="sums",
    )(core, own, other)

    tgt_grads = lax.all_gather(d_tgt, "mem", axis=0, tiled=False)
    mine = (lax.axis_index("mem") * candidates.shape[0]).astype(jnp.int32)[None]
    d_cand = pl.pallas_call(
        cand_kernel,
        out_shape=sds(candidates.shape, F32),
        in_specs=[SMEM, VMEM],
        out_specs=VMEM,
        compiler_params=params(16),
        name="cand",
    )(mine, tgt_grads)
    return (out_hist, out_tgt, returned, d_cand, sum_proj, sum_out)


HIST_MIB, TGT_MIB, ROWS_MIB = 44, 44, 24


def core_swap():
    return [(i, i + 16 if (i // 16) % 2 == 0 else i - 16) for i in range(128)]


def same_core():
    return [[i for i in range(128) if (i // 16) % 2 == core] for core in (0, 1)]


def solution(mesh):
    placed = (
        P(BOTH, None, None, None),
        P(BOTH, None, None),
        P(BOTH, None),
        P(BOTH, None),
        P(BOTH, None),
        P(),
        P(),
        P(BOTH, None),
        P(BOTH, None),
    )
    return jax.shard_map(
        local,
        mesh=mesh,
        in_specs=placed,
        out_specs=(
            P(BOTH, None),
            P(BOTH, None),
            P(BOTH, None, None, None),
            P(BOTH, None),
            P(),
            P(),
        ),
        check_vma=False,
    )
```

```python
import jax
import jax.numpy as jnp
from jax import lax
from jax.experimental import pallas as pl
from jax.experimental.pallas import tpu as pltpu
from jax.sharding import PartitionSpec as P

HEADS = 8
EPS = 1e-05
BLK = 256
MASKED = -1e9
F32 = jnp.float32
BF16 = jnp.bfloat16
BOTH = ("grp", "mem")
NN = (((1,), (0,)), ((), ()))
NT = (((1,), (1,)), ((), ()))


def mm(left, right, dims=NN):
    return lax.dot_general(left, right, dims, preferred_element_type=F32)


def moments(values):
    centred = values - jnp.mean(values, axis=-1, keepdims=True)
    variance = jnp.mean(centred * centred, axis=-1, keepdims=True)
    return centred, lax.rsqrt(variance + EPS)


def head_masks():
    lane = lax.broadcasted_iota(jnp.int32, (1, 128), 1)
    low_half = jnp.where(lane < 64, 1.0, 0.0).astype(F32)
    return (low_half, 1.0 - low_half)


def silu_parts(half):
    t = jnp.tanh(half)
    u = 1.0 + t
    return half * u, 0.5 * u * (1.0 + half * (1.0 - t))


def one_hot(hits):
    return jnp.where(hits, 1.0, 0.0).astype(BF16)


def split_heads(act, dest, rows):
    halves = head_masks()
    for head in range(HEADS):
        pair = act[:, (head // 2) * 128 : (head // 2 + 1) * 128]
        dest[head, rows, :] = (pair * halves[head % 2]).astype(BF16)


def score_bias(lo, hi, k0):
    key = k0 + lax.broadcasted_iota(jnp.int32, (1, BLK), 1)
    allowed = (key >= lo) & (key <= hi)
    return jnp.where(allowed, 0.0, MASKED).astype(F32)


def forward(q_ref, rows, size, km, vm, keys, width, w_s, s_s, slot, bias_s, a_acc):
    for pair in range(HEADS // 2):
        cols = slice(pair * 128, (pair + 1) * 128)
        total = a_acc[:size, cols]
        for head in (2 * pair, 2 * pair + 1):
            half = mm(q_ref[rows, cols], km[head, keys, :], NT) + bias_s[:size, :width]
            weight, slope = silu_parts(half)
            weight = weight.astype(BF16)
            w_s[slot, head, :size, :width] = weight
            s_s[slot, head, :size, :width] = slope.astype(BF16)
            total = total + mm(weight, vm[head, keys, :])
        a_acc[:size, cols] = total


def backward(size, km, vm, keys, width, w_s, s_s, slot, da_s, da_t, q_t, dq_acc, dk_t, dv_t):
    for pair in range(HEADS // 2):
        cols = slice(pair * 128, (pair + 1) * 128)
        total = dq_acc[:size, cols]
        for head in (2 * pair, 2 * pair + 1):
            d_weight = mm(da_s[:size, cols], vm[head, keys, :], NT)
            d_score = d_weight * s_s[slot, head, :size, :width].astype(F32)
            d_score = d_score.astype(BF16)
            total = total + mm(d_score, km[head, keys, :])
            own = slice(head * 64, (head + 1) * 64)
            dv_t[own, keys] += mm(da_t[own, :size], w_s[slot, head, :size, :width])
            dk_t[own, keys] += mm(q_t[own, :size], d_score)
        dq_acc[:size, cols] = total


def middle(attended, x, gate, g, w_out):
    centred, rstd = moments(attended)
    normed = centred * rstd
    mixed = normed * gate
    out = (x + mm(mixed.astype(BF16), w_out)).astype(BF16)
    d_mixed = mm(g, w_out, NT)
    d_normed = d_mixed * gate
    mean_d = jnp.mean(d_normed, axis=-1, keepdims=True)
    mean_dn = jnp.mean(d_normed * normed, axis=-1, keepdims=True)
    d_att = rstd * (d_normed - mean_d - normed * mean_dn)
    return out, mixed, d_mixed * normed, d_att


def project_kernel(
    arrived, pos_row, w_proj, x_o, normed_o, rstd_o, normed_t, gate_qry, km, vm, slopes
):
    size, feature = x_o.shape
    every = slice(0, size)
    row = pl.program_id(0) * size + lax.broadcasted_iota(jnp.int32, (size, 1), 0)
    x = mm(one_hot(pos_row[...] == row), arrived[...])
    x_o[...] = x.astype(BF16)
    centred, rstd = moments(x)
    normed = centred * rstd
    rstd_o[...] = rstd
    normed_t[...] = normed.T.astype(BF16)
    normed = normed.astype(BF16)
    normed_o[...] = normed
    for part in range(4):
        cols = slice(part * feature, (part + 1) * feature)
        act, slope = silu_parts(mm(normed, w_proj[:, cols]) * 0.5)
        slopes[:, cols] = slope.astype(BF16)
        if part == 0:
            gate_qry[:, :feature] = act.astype(BF16)
        elif part == 1:
            split_heads(act, vm, every)
        elif part == 2:
            gate_qry[:, feature:] = (act.astype(BF16) * 0.0625).astype(BF16)
        else:
            split_heads(act, km, every)


def fetch(pairs, sems):
    copies = [pltpu.make_async_copy(src, dst, sems.at[i]) for i, (src, dst) in enumerate(pairs)]
    for copy in copies:
        copy.start()
    return copies


def tgt_kernel(
    cand,
    tid_col,
    tid_row,
    lo,
    hi,
    w_proj,
    w_out,
    g_tgt,
    km_in,
    vm_in,
    out_tgt,
    d_tgt,
    dk_t,
    dv_t,
    tgt_t,
    d_pre,
    km,
    vm,
    sems,
    gate_s,
    q_s,
    km_own,
    vm_own,
    w_s,
    s_s,
    bias_s,
    a_acc,
    dq_acc,
    da_s,
    da_t,
    q_t,
    dk_own,
    dv_own,
):
    copies = fetch([(km_in, km), (vm_in, vm)], sems)
    tgt_rows, feature = out_tgt.shape
    blocks = km.shape[1] // BLK
    every = slice(0, tgt_rows)
    part_cols = [slice(part * feature, (part + 1) * feature) for part in range(4)]
    col = lax.broadcasted_iota(jnp.int32, (1, cand.shape[0]), 1)
    x = mm(one_hot(tid_col[...] == col), cand[...])
    centred, rstd = moments(x)
    unit = centred * rstd
    normed = unit.astype(BF16)
    tgt_t[0] = unit.T.astype(BF16)
    for part in range(4):
        half = mm(normed, w_proj[:, part_cols[part]]) * 0.5
        act, slope = silu_parts(half)
        d_pre[:, part_cols[part]] = slope.astype(BF16)
        if part == 0:
            gate_s[...] = act.astype(BF16)
        elif part == 1:
            split_heads(act, vm_own, every)
        elif part == 2:
            q_s[...] = (act.astype(BF16) * 0.0625).astype(BF16)
        else:
            split_heads(act, km_own, every)

    a_acc[...] = jnp.zeros_like(a_acc)
    dq_acc[...] = jnp.zeros_like(dq_acc)
    dk_own[...] = jnp.zeros_like(dk_own)
    dv_own[...] = jnp.zeros_like(dv_own)
    dk_t[...] = jnp.zeros_like(dk_t)
    dv_t[...] = jnp.zeros_like(dv_t)
    for copy in copies:
        copy.wait()

    def fwd(j, c):
        k0 = pl.multiple_of(j * BLK, BLK)
        keys = pl.ds(k0, BLK)
        bias_s[...] = score_bias(lo[...], hi[...], k0)
        forward(q_s, every, tgt_rows, km, vm, keys, BLK, w_s, s_s, j, bias_s, a_acc)
        return c

    def bwd(j, c):
        keys = pl.ds(pl.multiple_of(j * BLK, BLK), BLK)
        backward(
            tgt_rows, km, vm, keys, BLK, w_s, s_s, j, da_s, da_t, q_t, dq_acc, dk_t, dv_t
        )
        return c

    lax.fori_loop(0, blocks, fwd, 0)
    same = lax.broadcasted_iota(jnp.int32, (tgt_rows, tgt_rows), 0) == lax.broadcasted_iota(
        jnp.int32, (tgt_rows, tgt_rows), 1
    )
    bias_s[:, :tgt_rows] = jnp.where(same, 0.0, MASKED).astype(F32)
    forward(
        q_s, every, tgt_rows, km_own, vm_own, every, tgt_rows, w_s, s_s, blocks, bias_s, a_acc
    )
    out, mixed, d_gate, d_att = middle(
        a_acc[...], x, gate_s[...].astype(F32), g_tgt[...], w_out[...]
    )
    out_tgt[...] = out
    tgt_t[1] = mixed.T.astype(BF16)
    d_pre[:, part_cols[0]] = (d_gate * d_pre[:, part_cols[0]].astype(F32)).astype(BF16)
    da_s[...] = d_att.astype(BF16)
    da_t[...] = d_att.T.astype(BF16)
    q_t[...] = q_s[...].astype(F32).T.astype(BF16)
    lax.fori_loop(0, blocks, bwd, 0)
    backward(
        tgt_rows, km_own, vm_own, every, tgt_rows, w_s, s_s, blocks,
        da_s, da_t, q_t, dq_acc, dk_own, dv_own,
    )
    grads = (None, dv_own[...].T, dq_acc[...] * 0.125, dk_own[...].T * 2.0)
    for part in (1, 2, 3):
        d_part = grads[part] * d_pre[:, part_cols[part]].astype(F32)
        d_pre[:, part_cols[part]] = d_part.astype(BF16)

    d_normed = mm(d_pre[...], w_proj[...], NT)
    mean_d = jnp.mean(d_normed, axis=-1, keepdims=True)
    mean_dn = jnp.mean(d_normed * unit, axis=-1, keepdims=True)
    d_x = rstd * (d_normed - mean_d - unit * mean_dn) + g_tgt[...].astype(F32)
    d_tgt[every, :] = d_x.astype(BF16)
    ids = tid_row[...]
    high = lax.shift_right_logical(ids, 6)
    low = ids - high * 64
    d_tgt[tgt_rows:, :] = jnp.zeros((d_tgt.shape[0] - tgt_rows, feature), BF16)
    wide = (d_tgt.shape[0] - tgt_rows, tgt_rows)
    d_tgt[tgt_rows:, :tgt_rows] = jnp.broadcast_to(high.astype(F32), wide).astype(BF16)
    d_tgt[tgt_rows:, tgt_rows : 2 * tgt_rows] = jnp.broadcast_to(low.astype(F32), wide).astype(BF16)


def hist_kernel(
    core_ref,
    first_ref,
    lo,
    hi,
    w_out,
    g_hist,
    g_tgt,
    tgt_t,
    tgt_pre,
    gate_qry_in,
    km_in,
    vm_in,
    x_in,
    slopes_in,
    dv_in,
    dk_in,
    normed_t_in,
    out_hist,
    keep,
    give,
    d_pre_o,
    gate_qry,
    km,
    vm,
    x_s,
    d_pre,
    dv_t,
    dk_t,
    normed_t,
    mixed_t,
    sems,
    w_s,
    s_s,
    bias_s,
    a_acc,
    dq_acc,
    da_s,
    da_t,
    q_t,
):
    copies = fetch(
        [
            (gate_qry_in, gate_qry),
            (km_in, km),
            (vm_in, vm),
            (x_in, x_s),
            (slopes_in, d_pre),
            (dv_in, dv_t),
            (dk_in, dk_t),
            (normed_t_in, normed_t),
        ],
        sems,
    )
    hist_rows, feature = out_hist.shape
    blocks = hist_rows // BLK
    part_cols = [slice(part * feature, (part + 1) * feature) for part in range(4)]
    qry = slice(feature, 2 * feature)
    q_ref = gate_qry.at[:, qry]
    for copy in copies[:3]:
        copy.wait()

    def hist_block(i, carry):
        r0 = pl.multiple_of(i * BLK, BLK)
        rows = pl.ds(r0, BLK)
        first = first_ref[i]
        a_acc[...] = jnp.zeros_like(a_acc)
        dq_acc[...] = jnp.zeros_like(dq_acc)

        def fwd(j, c):
            k0 = pl.multiple_of(j * BLK, BLK)
            keys = pl.ds(k0, BLK)
            bias_s[...] = score_bias(lo[rows, :], hi[rows, :], k0)
            forward(q_ref, rows, BLK, km, vm, keys, BLK, w_s, s_s, j, bias_s, a_acc)
            return c

        def bwd(j, c):
            keys = pl.ds(pl.multiple_of(j * BLK, BLK), BLK)
            backward(
                BLK, km, vm, keys, BLK, w_s, s_s, j, da_s, da_t, q_t, dq_acc, dk_t, dv_t
            )
            return c

        lax.fori_loop(first, i + 1, fwd, 0)

        @pl.when(i == 0)
        def _():
            for copy in copies[3:]:
                copy.wait()

        out, mixed, d_gate, d_att = middle(
            a_acc[...],
            x_s[rows, :].astype(F32),
            gate_qry[rows, :feature].astype(F32),
            g_hist[rows, :],
            w_out[...],
        )
        out_hist[rows, :] = out
        mixed_t[:, rows] = mixed.T.astype(BF16)
        d_pre[rows, part_cols[0]] = (d_gate * d_pre[rows, part_cols[0]].astype(F32)).astype(BF16)
        da_s[...] = d_att.astype(BF16)
        da_t[...] = d_att.T.astype(BF16)
        q_t[...] = gate_qry[rows, qry].astype(F32).T.astype(BF16)
        lax.fori_loop(first, i + 1, bwd, 0)
        d_q = dq_acc[...] * 0.125 * d_pre[rows, part_cols[2]].astype(F32)
        d_pre[rows, part_cols[2]] = d_q.astype(BF16)
        return carry

    lax.fori_loop(0, blocks, hist_block, 0)

    def spread(i, carry):
        rows = pl.ds(pl.multiple_of(i * BLK, BLK), BLK)
        vals, keys = part_cols[1], part_cols[3]
        d_pre[rows, vals] = (dv_t[:, rows].T * d_pre[rows, vals].astype(F32)).astype(BF16)
        d_pre[rows, keys] = (dk_t[:, rows].T * 2.0 * d_pre[rows, keys].astype(F32)).astype(BF16)
        return carry

    lax.fori_loop(0, blocks, spread, 0)
    sent = pltpu.make_async_copy(d_pre, d_pre_o, sems.at[len(copies)])
    sent.start()

    core = core_ref[0]
    half_rows = feature // 2
    for dest, half in ((give, 1 - core), (keep, core)):
        rows = pl.ds(pl.multiple_of(half * half_rows, half_rows), half_rows)
        for part in range(5):
            if part < 4:
                total = mm(normed_t[rows, :], d_pre[:, part_cols[part]])
                total = total + mm(tgt_t[0, rows, :], tgt_pre[:, part_cols[part]])
            else:
                total = mm(mixed_t[rows, :], g_hist[...]) + mm(tgt_t[1, rows, :], g_tgt[...])
            for group, dest_cols, cols in segments(part, feature):
                piece = total[:, cols].reshape(16, 16, cols.stop - cols.start)
                dest[:, group, :, dest_cols] = piece.astype(BF16)
    sent.wait()


def segments(part, feature):
    found, begin = [], part * feature
    while begin < (part + 1) * feature:
        group = begin // 640
        end = min((part + 1) * feature, (group + 1) * 640)
        found.append(
            (group, slice(begin - group * 640, end - group * 640), slice(begin - part * feature, end - part * feature))
        )
        begin = end
    return found


def rows_kernel(d_pre, w_proj, normed, rstd, g_hist, pos_col, slot_grads, d_hist):
    hist_rows, feature = g_hist.shape

    def back(i, carry):
        rows = pl.ds(pl.multiple_of(i * BLK, BLK), BLK)
        d_normed = mm(d_pre[rows, :], w_proj[...], NT)
        unit = normed[rows, :].astype(F32)
        mean_d = jnp.mean(d_normed, axis=-1, keepdims=True)
        mean_dn = jnp.mean(d_normed * unit, axis=-1, keepdims=True)
        d_x = rstd[rows, :] * (d_normed - mean_d - unit * mean_dn)
        d_hist[rows, :] = (d_x + g_hist[rows, :].astype(F32)).astype(BF16)
        return carry

    lax.fori_loop(0, hist_rows // BLK, back, 0)

    def pick(i, carry):
        rows = pl.ds(pl.multiple_of(i * BLK, BLK), BLK)
        row = lax.broadcasted_iota(jnp.int32, (1, hist_rows), 1)
        onehot = one_hot(pos_col[rows, :] == row)
        slot_grads[rows, :] = mm(onehot, d_hist[...]).astype(BF16)
        return carry

    lax.fori_loop(0, slot_grads.shape[0] // BLK, pick, 0)


def cand_kernel(first_ref, rows, out):
    count, feature = out.shape
    own = first_ref[0] + lax.broadcasted_iota(jnp.int32, (count, 1), 0)
    total = jnp.zeros((count, feature), F32)
    for peer in range(rows.shape[0]):
        high = rows[peer, count : count + 16, :count].astype(F32)[:1]
        low = rows[peer, count : count + 16, count : 2 * count].astype(F32)[:1]
        ids = (high * 64.0 + low).astype(jnp.int32)
        total = total + mm(one_hot(own == ids), rows[peer, :count, :])
    out[...] = total


def reduce_kernel(pieces, slot_grads, copies):
    del slot_grads
    total = jnp.sum(pieces[...].astype(F32), axis=0).astype(BF16)
    for peer in range(copies.shape[0]):
        copies[peer] = total


def sums_kernel(pieces, d_proj, d_out):
    quarter, feature = d_out.shape
    for part in range(5):
        for group, source_cols, cols in segments(part, feature):
            piece = pieces[0, :, group, :, source_cols].astype(F32)
            piece = piece.reshape(quarter, cols.stop - cols.start)
            if part < 4:
                base = part * feature
                d_proj[:, base + cols.start : base + cols.stop] = piece
            else:
                d_out[:, cols] = piece


VMEM = pl.BlockSpec(memory_space=pltpu.VMEM)
SMEM = pl.BlockSpec(memory_space=pltpu.SMEM)
ANY = pl.BlockSpec(memory_space=pl.ANY)


def params(mib):
    return pltpu.CompilerParams(vmem_limit_bytes=mib << 20)


def cost(flops, nbytes):
    return pl.CostEstimate(flops=flops, bytes_accessed=nbytes, transcendentals=0)


def local(
    send_rows, slot_pos, lengths, candidates, target_ids, w_proj, w_out, g_hist, g_tgt
):
    peers, capacity, feature = send_rows.shape[1:]
    slots = peers * capacity
    hist_rows, tgt_rows = g_hist.shape[0], g_tgt.shape[0]
    blocks = hist_rows // BLK
    each = target_ids.shape[1]
    table = lax.all_gather(candidates, "mem", axis=0, tiled=True)
    arrived = lax.all_to_all(send_rows, BOTH, split_axis=1, concat_axis=0, tiled=True)
    arrived = arrived.reshape(slots, feature)

    pos_row = slot_pos.reshape(1, slots)
    pos_col = slot_pos.reshape(slots, 1)
    ends = jnp.cumsum(lengths[0])
    starts = ends - lengths[0]
    row = jnp.arange(hist_rows, dtype=jnp.int32)[:, None]
    hist_lo = jnp.max(jnp.where(row >= starts[None, :], starts[None, :], 0), axis=1)
    first = (hist_lo[::BLK] // BLK).astype(jnp.int32)
    tgt_lo = jnp.repeat(starts, each).astype(jnp.int32)[:, None]
    tgt_hi = jnp.repeat(ends - 1, each).astype(jnp.int32)[:, None]
    core = lax.rem(lax.axis_index("grp"), 2).astype(jnp.int32)[None]

    sds = jax.ShapeDtypeStruct

    def by_rows(width):
        return pl.BlockSpec((BLK, width), lambda i: (i, 0))

    def whole(*shape):
        return pl.BlockSpec(shape, lambda i: (0,) * len(shape))

    per_head = pl.BlockSpec((HEADS, BLK, 128), lambda i: (0, i, 0))
    x_hist, normed, rstd, normed_t, gate_qry, km, vm, slopes = pl.pallas_call(
        project_kernel,
        grid=(blocks,),
        out_shape=(
            sds((hist_rows, feature), BF16),
            sds((hist_rows, feature), BF16),
            sds((hist_rows, 1), F32),
            sds((feature, hist_rows), BF16),
            sds((hist_rows, 2 * feature), BF16),
            sds((HEADS, hist_rows, 128), BF16),
            sds((HEADS, hist_rows, 128), BF16),
            sds((hist_rows, 4 * feature), BF16),
        ),
        in_specs=[whole(slots, feature), whole(1, slots), whole(feature, 4 * feature)],
        out_specs=(
            by_rows(feature),
            by_rows(feature),
            by_rows(1),
            pl.BlockSpec((feature, BLK), lambda i: (0, i)),
            by_rows(2 * feature),
            per_head,
            per_head,
            by_rows(4 * feature),
        ),
        compiler_params=params(56),
        cost_estimate=cost(5 << 30, 20 << 20),
        name="project",
    )(arrived, pos_row, w_proj)

    scratch = pltpu.VMEM
    out_tgt, d_tgt, dk_t, dv_t, tgt_t, tgt_pre = pl.pallas_call(
        tgt_kernel,
        out_shape=(
            sds((tgt_rows, feature), BF16),
            sds((tgt_rows + 16, feature), BF16),
            sds((feature, hist_rows), F32),
            sds((feature, hist_rows), F32),
            sds((2, feature, tgt_rows), BF16),
            sds((tgt_rows, 4 * feature), BF16),
        ),
        in_specs=[VMEM] * 8 + [ANY] * 2,
        out_specs=(VMEM,) * 6,
        scratch_shapes=[
            scratch((HEADS, hist_rows, 128), BF16),
            scratch((HEADS, hist_rows, 128), BF16),
            pltpu.SemaphoreType.DMA((2,)),
            scratch((tgt_rows, feature), BF16),
            scratch((tgt_rows, feature), BF16),
            scratch((HEADS, tgt_rows, 128), BF16),
            scratch((HEADS, tgt_rows, 128), BF16),
            scratch((blocks + 1, HEADS, tgt_rows, BLK), BF16),
            scratch((blocks + 1, HEADS, tgt_rows, BLK), BF16),
            scratch((tgt_rows, BLK), F32),
            scratch((tgt_rows, feature), F32),
            scratch((tgt_rows, feature), F32),
            scratch((tgt_rows, feature), BF16),
            scratch((feature, tgt_rows), BF16),
            scratch((feature, tgt_rows), BF16),
            scratch((feature, tgt_rows), F32),
            scratch((feature, tgt_rows), F32),
        ],
        compiler_params=params(56),
        cost_estimate=cost(6 << 30, 16 << 20),
        name="tgt",
    )(
        table,
        target_ids.reshape(tgt_rows, 1),
        target_ids.reshape(1, tgt_rows),
        tgt_lo,
        tgt_hi,
        w_proj,
        w_out,
        g_tgt,
        km,
        vm,
    )
    tgt_grads = lax.all_gather(d_tgt, "mem", axis=0, tiled=False)

    pieces = (16, 4, 16, 640)
    out_hist, keep, give, d_pre = pl.pallas_call(
        hist_kernel,
        out_shape=(
            sds((hist_rows, feature), BF16),
            sds(pieces, BF16),
            sds(pieces, BF16),
            sds((hist_rows, 4 * feature), BF16),
        ),
        in_specs=[SMEM] * 2 + [VMEM] * 7 + [ANY] * 8,
        out_specs=(VMEM, VMEM, VMEM, ANY),
        scratch_shapes=[
            scratch((hist_rows, 2 * feature), BF16),
            scratch((HEADS, hist_rows, 128), BF16),
            scratch((HEADS, hist_rows, 128), BF16),
            scratch((hist_rows, feature), BF16),
            scratch((hist_rows, 4 * feature), BF16),
            scratch((feature, hist_rows), F32),
            scratch((feature, hist_rows), F32),
            scratch((feature, hist_rows), BF16),
            scratch((feature, hist_rows), BF16),
            pltpu.SemaphoreType.DMA((9,)),
            scratch((blocks, HEADS, BLK, BLK), BF16),
            scratch((blocks, HEADS, BLK, BLK), BF16),
            scratch((BLK, BLK), F32),
            scratch((BLK, feature), F32),
            scratch((BLK, feature), F32),
            scratch((BLK, feature), BF16),
            scratch((feature, BLK), BF16),
            scratch((feature, BLK), BF16),
        ],
        compiler_params=params(56),
        cost_estimate=cost(18 << 30, 24 << 20),
        name="hist",
    )(
        core,
        first,
        hist_lo.astype(jnp.int32)[:, None],
        row,
        w_out,
        g_hist,
        g_tgt,
        tgt_t,
        tgt_pre,
        gate_qry,
        km,
        vm,
        x_hist,
        slopes,
        dv_t,
        dk_t,
        normed_t,
    )

    swapped = lax.ppermute(give, BOTH, core_swap())
    chip_sum = (keep.astype(F32) + swapped.astype(F32)).astype(BF16)
    chip_sum = chip_sum.reshape(64, 1, 16, 640)
    scattered = lax.all_to_all(
        chip_sum, BOTH, split_axis=0, concat_axis=1, tiled=True, axis_index_groups=same_core()
    )
    slot_grads = pl.pallas_call(
        rows_kernel,
        out_shape=sds((slots, feature), BF16),
        in_specs=[VMEM] * 6,
        out_specs=VMEM,
        scratch_shapes=[scratch((hist_rows, feature), BF16)],
        compiler_params=params(56),
        cost_estimate=cost(5 << 30, 16 << 20),
        name="rows",
    )(d_pre, w_proj, normed, rstd, g_hist, pos_col)
    copies = pl.pallas_call(
        reduce_kernel,
        out_shape=sds((16, 16, 640), BF16),
        in_specs=[VMEM, ANY],
        out_specs=VMEM,
        compiler_params=params(56),
        name="reduce",
    )(scattered.reshape(64, 16, 640), slot_grads)
    level = lax.all_to_all(
        copies.reshape(16, 1, 16, 640), "mem", split_axis=0, concat_axis=1, tiled=True
    ).reshape(256, 640)
    everything = lax.all_gather(level, "grp", axis=0, tiled=True)

    returned = lax.all_to_all(
        slot_grads.reshape(peers, 1, capacity, feature),
        BOTH,
        split_axis=0,
        concat_axis=1,
        tiled=True,
    )
    sum_proj, sum_out = pl.pallas_call(
        sums_kernel,
        out_shape=(sds(w_proj.shape, F32), sds(w_out.shape, F32)),
        grid=(2, 4),
        in_specs=[pl.BlockSpec((1, 4, 4, 16, 640), lambda c, z: (2 * z + c, 0, 0, 0, 0))],
        out_specs=(
            pl.BlockSpec((64, 4 * feature), lambda c, z: (4 * c + z, 0)),
            pl.BlockSpec((64, feature), lambda c, z: (4 * c + z, 0)),
        ),
        compiler_params=params(56),
        name="sums",
    )(everything.reshape(8, 4, 4, 16, 640))

    mine = (lax.axis_index("mem") * candidates.shape[0]).astype(jnp.int32)[None]
    d_cand = pl.pallas_call(
        cand_kernel,
        out_shape=sds(candidates.shape, F32),
        in_specs=[SMEM, VMEM],
        out_specs=VMEM,
        compiler_params=params(56),
        name="cand",
    )(mine, tgt_grads)
    return (out_hist, out_tgt, returned, d_cand, sum_proj, sum_out)


def core_swap():
    return [(i, i + 16 if (i // 16) % 2 == 0 else i - 16) for i in range(128)]


def same_core():
    return [[i for i in range(128) if (i // 16) % 2 == core] for core in (0, 1)]


def solution(mesh):
    placed = (
        P(BOTH, None, None, None),
        P(BOTH, None, None),
        P(BOTH, None),
        P(BOTH, None),
        P(BOTH, None),
        P(),
        P(),
        P(BOTH, None),
        P(BOTH, None),
    )
    return jax.shard_map(
        local,
        mesh=mesh,
        in_specs=placed,
        out_specs=(
            P(BOTH, None),
            P(BOTH, None),
            P(BOTH, None, None, None),
            P(BOTH, None),
            P(),
            P(),
        ),
        check_vma=False,
    )
```

```python
import jax
import jax.numpy as jnp
from jax import lax
from jax.experimental import pallas as pl
from jax.experimental.pallas import tpu as pltpu
from jax.sharding import PartitionSpec as P

HEADS = 8
PAIRS = HEADS // 2
EPS = 1e-05
BLK = 256
MASKED = -1e9
F32 = jnp.float32
BF16 = jnp.bfloat16
BOTH = ("grp", "mem")
NN = (((1,), (0,)), ((), ()))
NT = (((1,), (1,)), ((), ()))


def mm(left, right, dims=NN):
    return lax.dot_general(left, right, dims, preferred_element_type=F32)


def moments(values):
    centred = values - jnp.mean(values, axis=-1, keepdims=True)
    variance = jnp.mean(centred * centred, axis=-1, keepdims=True)
    return centred, lax.rsqrt(variance + EPS)


def head_masks():
    lane = lax.broadcasted_iota(jnp.int32, (1, 128), 1)
    low_half = jnp.where(lane < 64, 1.0, 0.0).astype(F32)
    return (low_half, 1.0 - low_half)


def silu_parts(half):
    t = jnp.tanh(half)
    u = 1.0 + t
    return half * u, 0.5 * u * (1.0 + half * (1.0 - t))


def one_hot(hits):
    return jnp.where(hits, 1.0, 0.0).astype(BF16)


def score_bias(lo, hi, k0):
    key = k0 + lax.broadcasted_iota(jnp.int32, (1, BLK), 1)
    allowed = (key >= lo) & (key <= hi)
    return jnp.where(allowed, 0.0, MASKED).astype(F32)


def stack_heads(rows, dest, size):
    for pair in range(PAIRS):
        both = rows[:, pair * 128 : (pair + 1) * 128]
        for place, keep in enumerate(head_masks()):
            dest[pair, place * size : (place + 1) * size, :] = (both * keep).astype(BF16)


def stack_columns(rows_t, dest, size):
    for head in range(HEADS):
        pair, place = head // 2, head % 2
        own = rows_t[head * 64 : (head + 1) * 64, :].astype(BF16)
        dest[pair, place * 64 : (place + 1) * 64, place * size : (place + 1) * size] = own


def merge_heads(acc, size):
    first, second = head_masks()
    return jnp.concatenate(
        [acc[pair, :size, :] * first + acc[pair, size:, :] * second for pair in range(PAIRS)],
        axis=1,
    )


def forward(q_st, k_ref, v_ref, keys, w_s, s_s, slot, bias, a_acc):
    size, width = bias.shape
    for pair in range(PAIRS):
        cols = slice(pair * 128, (pair + 1) * 128)
        half = mm(q_st[pair], k_ref[keys, cols], NT).reshape(2, size, width)
        weight, slope = silu_parts((half + bias[...][None]).reshape(2 * size, width))
        weight = weight.astype(BF16)
        w_s[slot, pair, :, :width] = weight
        s_s[slot, pair, :, :width] = slope.astype(BF16)
        a_acc[pair] += mm(weight, v_ref[keys, cols])


def backward(q_t, k_ref, v_ref, keys, width, w_s, s_s, slot, da_st, da_t, dq_acc, dk_t, dv_t):
    for pair in range(PAIRS):
        cols = slice(pair * 128, (pair + 1) * 128)
        d_weight = mm(da_st[pair], v_ref[keys, cols], NT)
        d_score = (d_weight * s_s[slot, pair, :, :width].astype(F32)).astype(BF16)
        dq_acc[pair] += mm(d_score, k_ref[keys, cols])
        dv_t[cols, keys] += mm(da_t[pair], w_s[slot, pair, :, :width])
        dk_t[cols, keys] += mm(q_t[pair], d_score)


def middle(attended, x, gate, g, w_out):
    centred, rstd = moments(attended)
    normed = centred * rstd
    mixed = normed * gate
    out = (x + mm(mixed.astype(BF16), w_out)).astype(BF16)
    d_mixed = mm(g, w_out, NT)
    d_normed = d_mixed * gate
    mean_d = jnp.mean(d_normed, axis=-1, keepdims=True)
    mean_dn = jnp.mean(d_normed * normed, axis=-1, keepdims=True)
    d_att = rstd * (d_normed - mean_d - normed * mean_dn)
    return out, mixed, d_mixed * normed, d_att


def project_kernel(
    arrived, pos_row, w_proj, x_o, normed_o, rstd_o, normed_t, acts, slopes
):
    size, feature = x_o.shape
    row = pl.program_id(0) * size + lax.broadcasted_iota(jnp.int32, (size, 1), 0)
    x = mm(one_hot(pos_row[...] == row), arrived[...])
    x_o[...] = x.astype(BF16)
    centred, rstd = moments(x)
    normed = centred * rstd
    rstd_o[...] = rstd
    normed_t[...] = normed.T.astype(BF16)
    normed = normed.astype(BF16)
    normed_o[...] = normed
    for part in range(4):
        cols = slice(part * feature, (part + 1) * feature)
        act, slope = silu_parts(mm(normed, w_proj[:, cols]) * 0.5)
        slopes[:, cols] = slope.astype(BF16)
        act = act.astype(BF16)
        acts[:, cols] = (act * 0.0625).astype(BF16) if part == 2 else act


def fetch(pairs, sems):
    copies = [pltpu.make_async_copy(src, dst, sems.at[i]) for i, (src, dst) in enumerate(pairs)]
    for copy in copies:
        copy.start()
    return copies


def tgt_kernel(
    cand,
    tid_col,
    tid_row,
    lo,
    hi,
    w_proj,
    w_out,
    g_tgt,
    acts_in,
    out_tgt,
    d_tgt,
    dk_t,
    dv_t,
    tgt_t,
    d_pre,
    k_s,
    v_s,
    sems,
    acts,
    w_s,
    s_s,
    bias_s,
    own_bias,
    a_acc,
    dq_acc,
    q_st,
    da_st,
    q_t,
    da_t,
    dk_own,
    dv_own,
):
    feature = out_tgt.shape[1]
    copies = fetch(
        [(acts_in.at[:, 3 * feature :], k_s), (acts_in.at[:, feature : 2 * feature], v_s)], sems
    )
    tgt_rows = out_tgt.shape[0]
    blocks = k_s.shape[0] // BLK
    every = slice(0, tgt_rows)
    part_cols = [slice(part * feature, (part + 1) * feature) for part in range(4)]
    col = lax.broadcasted_iota(jnp.int32, (1, cand.shape[0]), 1)
    x = mm(one_hot(tid_col[...] == col), cand[...])
    centred, rstd = moments(x)
    unit = centred * rstd
    normed = unit.astype(BF16)
    tgt_t[0] = unit.T.astype(BF16)
    for part in range(4):
        half = mm(normed, w_proj[:, part_cols[part]]) * 0.5
        act, slope = silu_parts(half)
        d_pre[:, part_cols[part]] = slope.astype(BF16)
        act = act.astype(BF16)
        acts[:, part_cols[part]] = (act * 0.0625).astype(BF16) if part == 2 else act
    qry = acts[:, part_cols[2]].astype(F32)
    q_t[...] = jnp.zeros_like(q_t)
    da_t[...] = jnp.zeros_like(da_t)
    stack_heads(qry, q_st, tgt_rows)
    stack_columns(qry.T, q_t, tgt_rows)

    a_acc[...] = jnp.zeros_like(a_acc)
    dq_acc[...] = jnp.zeros_like(dq_acc)
    dk_own[...] = jnp.zeros_like(dk_own)
    dv_own[...] = jnp.zeros_like(dv_own)
    dk_t[...] = jnp.zeros_like(dk_t)
    dv_t[...] = jnp.zeros_like(dv_t)
    for copy in copies:
        copy.wait()

    def fwd(j, c):
        k0 = pl.multiple_of(j * BLK, BLK)
        bias_s[...] = score_bias(lo[...], hi[...], k0)
        forward(q_st, k_s, v_s, pl.ds(k0, BLK), w_s, s_s, j, bias_s, a_acc)
        return c

    def bwd(j, c):
        keys = pl.ds(pl.multiple_of(j * BLK, BLK), BLK)
        backward(q_t, k_s, v_s, keys, BLK, w_s, s_s, j, da_st, da_t, dq_acc, dk_t, dv_t)
        return c

    lax.fori_loop(0, blocks, fwd, 0)
    same = lax.broadcasted_iota(jnp.int32, (tgt_rows, tgt_rows), 0) == lax.broadcasted_iota(
        jnp.int32, (tgt_rows, tgt_rows), 1
    )
    own_bias[...] = jnp.where(same, 0.0, MASKED).astype(F32)
    k_own, v_own = acts.at[:, part_cols[3]], acts.at[:, part_cols[1]]
    forward(q_st, k_own, v_own, every, w_s, s_s, blocks, own_bias, a_acc)
    gate = acts[:, part_cols[0]].astype(F32)
    out, mixed, d_gate, d_att = middle(merge_heads(a_acc, tgt_rows), x, gate, g_tgt[...], w_out[...])
    out_tgt[...] = out
    tgt_t[1] = mixed.T.astype(BF16)
    d_pre[:, part_cols[0]] = (d_gate * d_pre[:, part_cols[0]].astype(F32)).astype(BF16)
    stack_heads(d_att, da_st, tgt_rows)
    stack_columns(d_att.T, da_t, tgt_rows)
    lax.fori_loop(0, blocks, bwd, 0)
    backward(
        q_t, k_own, v_own, every, tgt_rows, w_s, s_s, blocks, da_st, da_t, dq_acc, dk_own, dv_own
    )
    d_q = merge_heads(dq_acc, tgt_rows) * 0.125
    grads = (None, dv_own[...].T, d_q, dk_own[...].T * 2.0)
    for part in (1, 2, 3):
        d_part = grads[part] * d_pre[:, part_cols[part]].astype(F32)
        d_pre[:, part_cols[part]] = d_part.astype(BF16)

    d_normed = mm(d_pre[...], w_proj[...], NT)
    mean_d = jnp.mean(d_normed, axis=-1, keepdims=True)
    mean_dn = jnp.mean(d_normed * unit, axis=-1, keepdims=True)
    d_x = rstd * (d_normed - mean_d - unit * mean_dn) + g_tgt[...].astype(F32)
    d_tgt[every, :] = d_x.astype(BF16)
    ids = tid_row[...]
    high = lax.shift_right_logical(ids, 6)
    low = ids - high * 64
    d_tgt[tgt_rows:, :] = jnp.zeros((d_tgt.shape[0] - tgt_rows, feature), BF16)
    wide = (d_tgt.shape[0] - tgt_rows, tgt_rows)
    d_tgt[tgt_rows:, :tgt_rows] = jnp.broadcast_to(high.astype(F32), wide).astype(BF16)
    d_tgt[tgt_rows:, tgt_rows : 2 * tgt_rows] = jnp.broadcast_to(low.astype(F32), wide).astype(BF16)


def hist_kernel(
    core_ref,
    first_ref,
    lo,
    hi,
    w_out,
    g_hist,
    g_tgt,
    tgt_t,
    tgt_pre,
    acts_in,
    x_in,
    slopes_in,
    dv_in,
    dk_in,
    normed_t_in,
    out_hist,
    keep,
    give,
    d_pre_o,
    acts,
    x_s,
    d_pre,
    dv_t,
    dk_t,
    normed_t,
    mixed_t,
    sems,
    w_s,
    s_s,
    bias_s,
    a_acc,
    dq_acc,
    q_st,
    da_st,
    q_t,
    da_t,
):
    hist_rows, feature = out_hist.shape
    blocks = hist_rows // BLK
    part_cols = [slice(part * feature, (part + 1) * feature) for part in range(4)]
    later = slice(2 * feature, 4 * feature)
    copies = fetch(
        [
            (acts_in.at[:, later], acts.at[:, later]),
            (acts_in.at[:, part_cols[1]], acts.at[:, part_cols[1]]),
            (acts_in.at[:, part_cols[0]], acts.at[:, part_cols[0]]),
            (x_in, x_s),
            (slopes_in, d_pre),
            (dv_in, dv_t),
            (dk_in, dk_t),
            (normed_t_in, normed_t),
        ],
        sems,
    )
    k_ref, v_ref = acts.at[:, part_cols[3]], acts.at[:, part_cols[1]]
    q_t[...] = jnp.zeros_like(q_t)
    da_t[...] = jnp.zeros_like(da_t)
    for copy in copies[:2]:
        copy.wait()

    def hist_block(i, carry):
        r0 = pl.multiple_of(i * BLK, BLK)
        rows = pl.ds(r0, BLK)
        first = first_ref[i]
        a_acc[...] = jnp.zeros_like(a_acc)
        dq_acc[...] = jnp.zeros_like(dq_acc)

        qry = acts[rows, part_cols[2]].astype(F32)
        stack_heads(qry, q_st, BLK)
        stack_columns(qry.T, q_t, BLK)

        def fwd(j, c):
            k0 = pl.multiple_of(j * BLK, BLK)
            bias_s[...] = score_bias(lo[rows, :], hi[rows, :], k0)
            forward(q_st, k_ref, v_ref, pl.ds(k0, BLK), w_s, s_s, j, bias_s, a_acc)
            return c

        def bwd(j, c):
            keys = pl.ds(pl.multiple_of(j * BLK, BLK), BLK)
            backward(q_t, k_ref, v_ref, keys, BLK, w_s, s_s, j, da_st, da_t, dq_acc, dk_t, dv_t)
            return c

        lax.fori_loop(first, i + 1, fwd, 0)

        @pl.when(i == 0)
        def _():
            for copy in copies[2:]:
                copy.wait()

        out, mixed, d_gate, d_att = middle(
            merge_heads(a_acc, BLK),
            x_s[rows, :].astype(F32),
            acts[rows, part_cols[0]].astype(F32),
            g_hist[rows, :],
            w_out[...],
        )
        out_hist[rows, :] = out
        mixed_t[:, rows] = mixed.T.astype(BF16)
        d_pre[rows, part_cols[0]] = (d_gate * d_pre[rows, part_cols[0]].astype(F32)).astype(BF16)
        stack_heads(d_att, da_st, BLK)
        stack_columns(d_att.T, da_t, BLK)
        lax.fori_loop(first, i + 1, bwd, 0)
        d_q = merge_heads(dq_acc, BLK) * 0.125 * d_pre[rows, part_cols[2]].astype(F32)
        d_pre[rows, part_cols[2]] = d_q.astype(BF16)
        return carry

    lax.fori_loop(0, blocks, hist_block, 0)

    def spread(i, carry):
        rows = pl.ds(pl.multiple_of(i * BLK, BLK), BLK)
        vals, keys = part_cols[1], part_cols[3]
        d_pre[rows, vals] = (dv_t[:, rows].T * d_pre[rows, vals].astype(F32)).astype(BF16)
        d_pre[rows, keys] = (dk_t[:, rows].T * 2.0 * d_pre[rows, keys].astype(F32)).astype(BF16)
        return carry

    lax.fori_loop(0, blocks, spread, 0)
    sent = pltpu.make_async_copy(d_pre, d_pre_o, sems.at[len(copies)])
    sent.start()

    core = core_ref[0]
    half_rows = feature // 2
    for dest, half in ((give, 1 - core), (keep, core)):
        rows = pl.ds(pl.multiple_of(half * half_rows, half_rows), half_rows)
        for part in range(5):
            if part < 4:
                total = mm(normed_t[rows, :], d_pre[:, part_cols[part]])
                total = total + mm(tgt_t[0, rows, :], tgt_pre[:, part_cols[part]])
            else:
                total = mm(mixed_t[rows, :], g_hist[...]) + mm(tgt_t[1, rows, :], g_tgt[...])
            for group, dest_cols, cols in segments(part, feature):
                piece = total[:, cols].reshape(16, 16, cols.stop - cols.start)
                dest[:, group, :, dest_cols] = piece.astype(BF16)
    sent.wait()


def segments(part, feature):
    found, begin = [], part * feature
    while begin < (part + 1) * feature:
        group = begin // 640
        end = min((part + 1) * feature, (group + 1) * 640)
        found.append(
            (group, slice(begin - group * 640, end - group * 640), slice(begin - part * feature, end - part * feature))
        )
        begin = end
    return found


def rows_kernel(d_pre, w_proj, normed, rstd, g_hist, pos_col, slot_grads, d_hist):
    hist_rows, feature = g_hist.shape

    def back(i, carry):
        rows = pl.ds(pl.multiple_of(i * BLK, BLK), BLK)
        d_normed = mm(d_pre[rows, :], w_proj[...], NT)
        unit = normed[rows, :].astype(F32)
        mean_d = jnp.mean(d_normed, axis=-1, keepdims=True)
        mean_dn = jnp.mean(d_normed * unit, axis=-1, keepdims=True)
        d_x = rstd[rows, :] * (d_normed - mean_d - unit * mean_dn)
        d_hist[rows, :] = (d_x + g_hist[rows, :].astype(F32)).astype(BF16)
        return carry

    lax.fori_loop(0, hist_rows // BLK, back, 0)

    def pick(i, carry):
        rows = pl.ds(pl.multiple_of(i * BLK, BLK), BLK)
        row = lax.broadcasted_iota(jnp.int32, (1, hist_rows), 1)
        onehot = one_hot(pos_col[rows, :] == row)
        slot_grads[rows, :] = mm(onehot, d_hist[...]).astype(BF16)
        return carry

    lax.fori_loop(0, slot_grads.shape[0] // BLK, pick, 0)


def cand_kernel(first_ref, rows, out):
    count, feature = out.shape
    own = first_ref[0] + lax.broadcasted_iota(jnp.int32, (count, 1), 0)
    total = jnp.zeros((count, feature), F32)
    for peer in range(rows.shape[0]):
        high = rows[peer, count : count + 16, :count].astype(F32)[:1]
        low = rows[peer, count : count + 16, count : 2 * count].astype(F32)[:1]
        ids = (high * 64.0 + low).astype(jnp.int32)
        total = total + mm(one_hot(own == ids), rows[peer, :count, :])
    out[...] = total


def reduce_kernel(pieces, slot_grads, copies):
    del slot_grads
    total = jnp.sum(pieces[...].astype(F32), axis=0).astype(BF16)
    for peer in range(copies.shape[0]):
        copies[peer] = total


def sums_kernel(pieces, d_proj, d_out):
    feature = d_out.shape[1]
    quarter = d_out.shape[0] // 8
    for level in range(4):
        for core in range(2):
            first = (core * 4 + level) * quarter
            rows = slice(first, first + quarter)
            for part in range(5):
                for group, source_cols, cols in segments(part, feature):
                    piece = pieces[level * 2 + core, :, group, :, source_cols].astype(F32)
                    piece = piece.reshape(quarter, cols.stop - cols.start)
                    if part < 4:
                        base = part * feature
                        d_proj[rows, base + cols.start : base + cols.stop] = piece
                    else:
                        d_out[rows, cols] = piece


VMEM = pl.BlockSpec(memory_space=pltpu.VMEM)
SMEM = pl.BlockSpec(memory_space=pltpu.SMEM)
ANY = pl.BlockSpec(memory_space=pl.ANY)


def params(mib):
    return pltpu.CompilerParams(vmem_limit_bytes=mib << 20)


def cost(flops, nbytes):
    return pl.CostEstimate(flops=flops, bytes_accessed=nbytes, transcendentals=0)


def local(
    send_rows, slot_pos, lengths, candidates, target_ids, w_proj, w_out, g_hist, g_tgt
):
    peers, capacity, feature = send_rows.shape[1:]
    slots = peers * capacity
    hist_rows, tgt_rows = g_hist.shape[0], g_tgt.shape[0]
    blocks = hist_rows // BLK
    each = target_ids.shape[1]
    table = lax.all_gather(candidates, "mem", axis=0, tiled=True)
    arrived = lax.all_to_all(send_rows, BOTH, split_axis=1, concat_axis=0, tiled=True)
    arrived = arrived.reshape(slots, feature)

    pos_row = slot_pos.reshape(1, slots)
    pos_col = slot_pos.reshape(slots, 1)
    ends = jnp.cumsum(lengths[0])
    starts = ends - lengths[0]
    row = jnp.arange(hist_rows, dtype=jnp.int32)[:, None]
    hist_lo = jnp.max(jnp.where(row >= starts[None, :], starts[None, :], 0), axis=1)
    first = (hist_lo[::BLK] // BLK).astype(jnp.int32)
    tgt_lo = jnp.repeat(starts, each).astype(jnp.int32)[:, None]
    tgt_hi = jnp.repeat(ends - 1, each).astype(jnp.int32)[:, None]
    core = lax.rem(lax.axis_index("grp"), 2).astype(jnp.int32)[None]

    sds = jax.ShapeDtypeStruct

    def by_rows(width):
        return pl.BlockSpec((BLK, width), lambda i: (i, 0))

    def whole(*shape):
        return pl.BlockSpec(shape, lambda i: (0,) * len(shape))

    x_hist, normed, rstd, normed_t, acts, slopes = pl.pallas_call(
        project_kernel,
        grid=(blocks,),
        out_shape=(
            sds((hist_rows, feature), BF16),
            sds((hist_rows, feature), BF16),
            sds((hist_rows, 1), F32),
            sds((feature, hist_rows), BF16),
            sds((hist_rows, 4 * feature), BF16),
            sds((hist_rows, 4 * feature), BF16),
        ),
        in_specs=[whole(slots, feature), whole(1, slots), whole(feature, 4 * feature)],
        out_specs=(
            by_rows(feature),
            by_rows(feature),
            by_rows(1),
            pl.BlockSpec((feature, BLK), lambda i: (0, i)),
            by_rows(4 * feature),
            by_rows(4 * feature),
        ),
        compiler_params=params(56),
        cost_estimate=cost(5 << 30, 20 << 20),
        name="project",
    )(arrived, pos_row, w_proj)

    scratch = pltpu.VMEM
    out_tgt, d_tgt, dk_t, dv_t, tgt_t, tgt_pre = pl.pallas_call(
        tgt_kernel,
        out_shape=(
            sds((tgt_rows, feature), BF16),
            sds((tgt_rows + 16, feature), BF16),
            sds((feature, hist_rows), F32),
            sds((feature, hist_rows), F32),
            sds((2, feature, tgt_rows), BF16),
            sds((tgt_rows, 4 * feature), BF16),
        ),
        in_specs=[VMEM] * 8 + [ANY],
        out_specs=(VMEM,) * 6,
        scratch_shapes=[
            scratch((hist_rows, feature), BF16),
            scratch((hist_rows, feature), BF16),
            pltpu.SemaphoreType.DMA((2,)),
            scratch((tgt_rows, 4 * feature), BF16),
            scratch((blocks + 1, PAIRS, 2 * tgt_rows, BLK), BF16),
            scratch((blocks + 1, PAIRS, 2 * tgt_rows, BLK), BF16),
            scratch((tgt_rows, BLK), F32),
            scratch((tgt_rows, tgt_rows), F32),
            scratch((PAIRS, 2 * tgt_rows, 128), F32),
            scratch((PAIRS, 2 * tgt_rows, 128), F32),
            scratch((PAIRS, 2 * tgt_rows, 128), BF16),
            scratch((PAIRS, 2 * tgt_rows, 128), BF16),
            scratch((PAIRS, 128, 2 * tgt_rows), BF16),
            scratch((PAIRS, 128, 2 * tgt_rows), BF16),
            scratch((feature, tgt_rows), F32),
            scratch((feature, tgt_rows), F32),
        ],
        compiler_params=params(56),
        cost_estimate=cost(6 << 30, 16 << 20),
        name="tgt",
    )(
        table,
        target_ids.reshape(tgt_rows, 1),
        target_ids.reshape(1, tgt_rows),
        tgt_lo,
        tgt_hi,
        w_proj,
        w_out,
        g_tgt,
        acts,
    )
    tgt_grads = lax.all_gather(d_tgt, "mem", axis=0, tiled=False)

    pieces = (16, 4, 16, 640)
    out_hist, keep, give, d_pre = pl.pallas_call(
        hist_kernel,
        out_shape=(
            sds((hist_rows, feature), BF16),
            sds(pieces, BF16),
            sds(pieces, BF16),
            sds((hist_rows, 4 * feature), BF16),
        ),
        in_specs=[SMEM] * 2 + [VMEM] * 7 + [ANY] * 6,
        out_specs=(VMEM, VMEM, VMEM, ANY),
        scratch_shapes=[
            scratch((hist_rows, 4 * feature), BF16),
            scratch((hist_rows, feature), BF16),
            scratch((hist_rows, 4 * feature), BF16),
            scratch((feature, hist_rows), F32),
            scratch((feature, hist_rows), F32),
            scratch((feature, hist_rows), BF16),
            scratch((feature, hist_rows), BF16),
            pltpu.SemaphoreType.DMA((9,)),
            scratch((blocks, PAIRS, 2 * BLK, BLK), BF16),
            scratch((blocks, PAIRS, 2 * BLK, BLK), BF16),
            scratch((BLK, BLK), F32),
            scratch((PAIRS, 2 * BLK, 128), F32),
            scratch((PAIRS, 2 * BLK, 128), F32),
            scratch((PAIRS, 2 * BLK, 128), BF16),
            scratch((PAIRS, 2 * BLK, 128), BF16),
            scratch((PAIRS, 128, 2 * BLK), BF16),
            scratch((PAIRS, 128, 2 * BLK), BF16),
        ],
        compiler_params=params(56),
        cost_estimate=cost(18 << 30, 24 << 20),
        name="hist",
    )(
        core,
        first,
        hist_lo.astype(jnp.int32)[:, None],
        row,
        w_out,
        g_hist,
        g_tgt,
        tgt_t,
        tgt_pre,
        acts,
        x_hist,
        slopes,
        dv_t,
        dk_t,
        normed_t,
    )

    swapped = lax.ppermute(give, BOTH, core_swap())
    chip_sum = (keep.astype(F32) + swapped.astype(F32)).astype(BF16)
    chip_sum = chip_sum.reshape(64, 1, 16, 640)
    scattered = lax.all_to_all(
        chip_sum, BOTH, split_axis=0, concat_axis=1, tiled=True, axis_index_groups=same_core()
    )
    slot_grads = pl.pallas_call(
        rows_kernel,
        out_shape=sds((slots, feature), BF16),
        in_specs=[VMEM] * 6,
        out_specs=VMEM,
        scratch_shapes=[scratch((hist_rows, feature), BF16)],
        compiler_params=params(56),
        cost_estimate=cost(5 << 30, 16 << 20),
        name="rows",
    )(d_pre, w_proj, normed, rstd, g_hist, pos_col)
    copies = pl.pallas_call(
        reduce_kernel,
        out_shape=sds((16, 16, 640), BF16),
        in_specs=[VMEM, ANY],
        out_specs=VMEM,
        compiler_params=params(56),
        name="reduce",
    )(scattered.reshape(64, 16, 640), slot_grads)
    level = lax.all_to_all(
        copies.reshape(16, 1, 16, 640), "mem", split_axis=0, concat_axis=1, tiled=True
    ).reshape(256, 640)
    everything = lax.all_gather(level, "grp", axis=0, tiled=True)

    returned = lax.all_to_all(
        slot_grads.reshape(peers, 1, capacity, feature),
        BOTH,
        split_axis=0,
        concat_axis=1,
        tiled=True,
    )
    sum_proj, sum_out = pl.pallas_call(
        sums_kernel,
        out_shape=(sds(w_proj.shape, F32), sds(w_out.shape, F32)),
        in_specs=[VMEM],
        out_specs=(VMEM, VMEM),
        compiler_params=params(16),
        name="sums",
    )(everything.reshape(8, 4, 4, 16, 640))

    mine = (lax.axis_index("mem") * candidates.shape[0]).astype(jnp.int32)[None]
    d_cand = pl.pallas_call(
        cand_kernel,
        out_shape=sds(candidates.shape, F32),
        in_specs=[SMEM, VMEM],
        out_specs=VMEM,
        compiler_params=params(56),
        name="cand",
    )(mine, tgt_grads)
    return (out_hist, out_tgt, returned, d_cand, sum_proj, sum_out)


def core_swap():
    return [(i, i + 16 if (i // 16) % 2 == 0 else i - 16) for i in range(128)]


def same_core():
    return [[i for i in range(128) if (i // 16) % 2 == core] for core in (0, 1)]


def solution(mesh):
    placed = (
        P(BOTH, None, None, None),
        P(BOTH, None, None),
        P(BOTH, None),
        P(BOTH, None),
        P(BOTH, None),
        P(),
        P(),
        P(BOTH, None),
        P(BOTH, None),
    )
    return jax.shard_map(
        local,
        mesh=mesh,
        in_specs=placed,
        out_specs=(
            P(BOTH, None),
            P(BOTH, None),
            P(BOTH, None, None, None),
            P(BOTH, None),
            P(),
            P(),
        ),
        check_vma=False,
    )
```

```python
import jax
import jax.numpy as jnp
from jax import lax
from jax.experimental import pallas as pl
from jax.experimental.pallas import tpu as pltpu
from jax.sharding import PartitionSpec as P

HEADS = 8
PAIRS = HEADS // 2
EPS = 1e-05
BLK = 256
MASKED = -1e9
F32 = jnp.float32
BF16 = jnp.bfloat16
BOTH = ("grp", "mem")
NN = (((1,), (0,)), ((), ()))
NT = (((1,), (1,)), ((), ()))


def mm(left, right, dims=NN):
    return lax.dot_general(left, right, dims, preferred_element_type=F32)


def moments(values):
    centred = values - jnp.mean(values, axis=-1, keepdims=True)
    variance = jnp.mean(centred * centred, axis=-1, keepdims=True)
    return centred, lax.rsqrt(variance + EPS)


def head_masks():
    lane = lax.broadcasted_iota(jnp.int32, (1, 128), 1)
    low_half = jnp.where(lane < 64, 1.0, 0.0).astype(F32)
    return (low_half, 1.0 - low_half)


def silu_parts(half):
    t = jnp.tanh(half)
    u = 1.0 + t
    return half * u, 0.5 * u * (1.0 + half * (1.0 - t))


def one_hot(hits):
    return jnp.where(hits, 1.0, 0.0).astype(BF16)


def score_bias(lo, hi, k0):
    key = k0 + lax.broadcasted_iota(jnp.int32, (1, BLK), 1)
    allowed = (key >= lo) & (key <= hi)
    return jnp.where(allowed, 0.0, MASKED).astype(F32)


def stack_heads(rows, dest, size):
    for pair in range(PAIRS):
        both = rows[:, pair * 128 : (pair + 1) * 128]
        for place, keep in enumerate(head_masks()):
            dest[pair, place * size : (place + 1) * size, :] = (both * keep).astype(BF16)


def stack_columns(rows_t, dest, size):
    for head in range(HEADS):
        pair, place = head // 2, head % 2
        own = rows_t[head * 64 : (head + 1) * 64, :].astype(BF16)
        dest[pair, place * 64 : (place + 1) * 64, place * size : (place + 1) * size] = own


def merge_heads(acc, size):
    first, second = head_masks()
    return jnp.concatenate(
        [acc[pair, :size, :] * first + acc[pair, size:, :] * second for pair in range(PAIRS)],
        axis=1,
    )


def forward(q_st, k_ref, v_ref, keys, w_s, s_s, slot, bias, a_acc):
    size, width = bias.shape
    for pair in range(PAIRS):
        cols = slice(pair * 128, (pair + 1) * 128)
        half = mm(q_st[pair], k_ref[keys, cols], NT).reshape(2, size, width)
        weight, slope = silu_parts((half + bias[...][None]).reshape(2 * size, width))
        weight = weight.astype(BF16)
        w_s[slot, pair, :, :width] = weight
        s_s[slot, pair, :, :width] = slope.astype(BF16)
        a_acc[pair] += mm(weight, v_ref[keys, cols])


def backward(q_t, k_ref, v_ref, keys, width, w_s, s_s, slot, da_st, da_t, dq_acc, dk_t, dv_t):
    for pair in range(PAIRS):
        cols = slice(pair * 128, (pair + 1) * 128)
        d_weight = mm(da_st[pair], v_ref[keys, cols], NT)
        d_score = (d_weight * s_s[slot, pair, :, :width].astype(F32)).astype(BF16)
        dq_acc[pair] += mm(d_score, k_ref[keys, cols])
        dv_t[cols, keys] += mm(da_t[pair], w_s[slot, pair, :, :width])
        dk_t[cols, keys] += mm(q_t[pair], d_score)


def middle(attended, x, gate, g, w_out):
    centred, rstd = moments(attended)
    normed = centred * rstd
    mixed = normed * gate
    out = (x + mm(mixed.astype(BF16), w_out)).astype(BF16)
    d_mixed = mm(g, w_out, NT)
    d_normed = d_mixed * gate
    mean_d = jnp.mean(d_normed, axis=-1, keepdims=True)
    mean_dn = jnp.mean(d_normed * normed, axis=-1, keepdims=True)
    d_att = rstd * (d_normed - mean_d - normed * mean_dn)
    return out, mixed, d_mixed * normed, d_att


def project_kernel(
    arrived, pos_row, w_proj, x_o, normed_o, rstd_o, normed_t, acts, slopes
):
    size, feature = x_o.shape
    row = pl.program_id(0) * size + lax.broadcasted_iota(jnp.int32, (size, 1), 0)
    x = mm(one_hot(pos_row[...] == row), arrived[...])
    x_o[...] = x.astype(BF16)
    centred, rstd = moments(x)
    normed = centred * rstd
    rstd_o[...] = rstd
    normed_t[...] = normed.T.astype(BF16)
    normed = normed.astype(BF16)
    normed_o[...] = normed
    for part in range(4):
        cols = slice(part * feature, (part + 1) * feature)
        act, slope = silu_parts(mm(normed, w_proj[:, cols]) * 0.5)
        slopes[:, cols] = slope.astype(BF16)
        act = act.astype(BF16)
        acts[:, cols] = (act * 0.0625).astype(BF16) if part == 2 else act


def fetch(pairs, sems):
    copies = [pltpu.make_async_copy(src, dst, sems.at[i]) for i, (src, dst) in enumerate(pairs)]
    for copy in copies:
        copy.start()
    return copies


def tgt_kernel(
    cand,
    tid_col,
    tid_row,
    lo,
    hi,
    w_proj,
    w_out,
    g_tgt,
    acts_in,
    out_tgt,
    d_tgt,
    dk_o,
    dv_o,
    tgt_t,
    d_pre,
    dk_t,
    dv_t,
    k_s,
    v_s,
    sems,
    acts,
    w_s,
    s_s,
    bias_s,
    own_bias,
    a_acc,
    dq_acc,
    q_st,
    da_st,
    q_t,
    da_t,
    dk_own,
    dv_own,
):
    feature = out_tgt.shape[1]
    copies = fetch(
        [(acts_in.at[:, 3 * feature :], k_s), (acts_in.at[:, feature : 2 * feature], v_s)], sems
    )
    tgt_rows = out_tgt.shape[0]
    blocks = k_s.shape[0] // BLK
    every = slice(0, tgt_rows)
    part_cols = [slice(part * feature, (part + 1) * feature) for part in range(4)]
    col = lax.broadcasted_iota(jnp.int32, (1, cand.shape[0]), 1)
    x = mm(one_hot(tid_col[...] == col), cand[...])
    centred, rstd = moments(x)
    unit = centred * rstd
    normed = unit.astype(BF16)
    tgt_t[0] = unit.T.astype(BF16)
    for part in range(4):
        half = mm(normed, w_proj[:, part_cols[part]]) * 0.5
        act, slope = silu_parts(half)
        d_pre[:, part_cols[part]] = slope.astype(BF16)
        act = act.astype(BF16)
        acts[:, part_cols[part]] = (act * 0.0625).astype(BF16) if part == 2 else act
    qry = acts[:, part_cols[2]].astype(F32)
    q_t[...] = jnp.zeros_like(q_t)
    da_t[...] = jnp.zeros_like(da_t)
    stack_heads(qry, q_st, tgt_rows)
    stack_columns(qry.T, q_t, tgt_rows)

    a_acc[...] = jnp.zeros_like(a_acc)
    dq_acc[...] = jnp.zeros_like(dq_acc)
    dk_own[...] = jnp.zeros_like(dk_own)
    dv_own[...] = jnp.zeros_like(dv_own)
    dk_t[...] = jnp.zeros_like(dk_t)
    dv_t[...] = jnp.zeros_like(dv_t)
    for copy in copies:
        copy.wait()

    def fwd(j, c):
        k0 = pl.multiple_of(j * BLK, BLK)
        bias_s[...] = score_bias(lo[...], hi[...], k0)
        forward(q_st, k_s, v_s, pl.ds(k0, BLK), w_s, s_s, j, bias_s, a_acc)
        return c

    def bwd(j, c):
        keys = pl.ds(pl.multiple_of(j * BLK, BLK), BLK)
        backward(q_t, k_s, v_s, keys, BLK, w_s, s_s, j, da_st, da_t, dq_acc, dk_t, dv_t)
        return c

    lax.fori_loop(0, blocks, fwd, 0)
    same = lax.broadcasted_iota(jnp.int32, (tgt_rows, tgt_rows), 0) == lax.broadcasted_iota(
        jnp.int32, (tgt_rows, tgt_rows), 1
    )
    own_bias[...] = jnp.where(same, 0.0, MASKED).astype(F32)
    k_own, v_own = acts.at[:, part_cols[3]], acts.at[:, part_cols[1]]
    forward(q_st, k_own, v_own, every, w_s, s_s, blocks, own_bias, a_acc)
    gate = acts[:, part_cols[0]].astype(F32)
    out, mixed, d_gate, d_att = middle(merge_heads(a_acc, tgt_rows), x, gate, g_tgt[...], w_out[...])
    out_tgt[...] = out
    tgt_t[1] = mixed.T.astype(BF16)
    d_pre[:, part_cols[0]] = (d_gate * d_pre[:, part_cols[0]].astype(F32)).astype(BF16)
    stack_heads(d_att, da_st, tgt_rows)
    stack_columns(d_att.T, da_t, tgt_rows)
    lax.fori_loop(0, blocks, bwd, 0)
    backward(
        q_t, k_own, v_own, every, tgt_rows, w_s, s_s, blocks, da_st, da_t, dq_acc, dk_own, dv_own
    )
    dk_o[...] = dk_t[...].astype(BF16)
    dv_o[...] = dv_t[...].astype(BF16)
    d_q = merge_heads(dq_acc, tgt_rows) * 0.125
    grads = (None, dv_own[...].T, d_q, dk_own[...].T * 2.0)
    for part in (1, 2, 3):
        d_part = grads[part] * d_pre[:, part_cols[part]].astype(F32)
        d_pre[:, part_cols[part]] = d_part.astype(BF16)

    d_normed = mm(d_pre[...], w_proj[...], NT)
    mean_d = jnp.mean(d_normed, axis=-1, keepdims=True)
    mean_dn = jnp.mean(d_normed * unit, axis=-1, keepdims=True)
    d_x = rstd * (d_normed - mean_d - unit * mean_dn) + g_tgt[...].astype(F32)
    d_tgt[every, :] = d_x.astype(BF16)
    ids = tid_row[...]
    high = lax.shift_right_logical(ids, 6)
    low = ids - high * 64
    d_tgt[tgt_rows:, :] = jnp.zeros((d_tgt.shape[0] - tgt_rows, feature), BF16)
    wide = (d_tgt.shape[0] - tgt_rows, tgt_rows)
    d_tgt[tgt_rows:, :tgt_rows] = jnp.broadcast_to(high.astype(F32), wide).astype(BF16)
    d_tgt[tgt_rows:, tgt_rows : 2 * tgt_rows] = jnp.broadcast_to(low.astype(F32), wide).astype(BF16)


def hist_kernel(
    core_ref,
    first_ref,
    starts_ref,
    w_out,
    g_hist,
    g_tgt,
    tgt_t,
    tgt_pre,
    acts_in,
    x_in,
    slopes_in,
    dv_in,
    dk_in,
    normed_t_in,
    out_hist,
    keep,
    give,
    d_pre_o,
    acts,
    x_s,
    d_pre,
    dv_add,
    dk_add,
    dv_t,
    dk_t,
    normed_t,
    mixed_t,
    out_s,
    give_s,
    sems,
    w_s,
    s_s,
    bias_s,
    a_acc,
    dq_acc,
    q_st,
    da_st,
    q_t,
    da_t,
):
    hist_rows, feature = g_hist.shape
    blocks = hist_rows // BLK
    part_cols = [slice(part * feature, (part + 1) * feature) for part in range(4)]
    gates, vals, qrys, ids = part_cols
    later = slice(2 * feature, 4 * feature)
    copies = fetch(
        [
            (acts_in.at[:, later], acts.at[:, later]),
            (acts_in.at[:, vals], acts.at[:, vals]),
            (acts_in.at[:, gates], acts.at[:, gates]),
            (x_in, x_s),
            (slopes_in.at[:, gates], d_pre.at[:, gates]),
            (slopes_in.at[:, qrys], d_pre.at[:, qrys]),
            (slopes_in.at[:, vals], d_pre.at[:, vals]),
            (slopes_in.at[:, ids], d_pre.at[:, ids]),
            (dv_in, dv_add),
            (dk_in, dk_add),
            (normed_t_in, normed_t),
        ],
        sems,
    )
    k_ref, v_ref = acts.at[:, part_cols[3]], acts.at[:, part_cols[1]]
    q_t[...] = jnp.zeros_like(q_t)
    da_t[...] = jnp.zeros_like(da_t)
    dk_t[...] = jnp.zeros_like(dk_t)
    dv_t[...] = jnp.zeros_like(dv_t)
    for copy in copies[:2]:
        copy.wait()

    def hist_block(n, carry):
        i = blocks - 1 - n
        r0 = pl.multiple_of(i * BLK, BLK)
        rows = pl.ds(r0, BLK)
        first = first_ref[i]
        row = r0 + lax.broadcasted_iota(jnp.int32, (BLK, 1), 0)
        lo = jnp.zeros((BLK, 1), jnp.int32)
        for user in range(starts_ref.shape[0]):
            lo = jnp.where(row >= starts_ref[user], starts_ref[user], lo)
        a_acc[...] = jnp.zeros_like(a_acc)
        dq_acc[...] = jnp.zeros_like(dq_acc)
        qry = acts[rows, part_cols[2]].astype(F32)
        stack_heads(qry, q_st, BLK)
        stack_columns(qry.T, q_t, BLK)

        def fwd(j, c):
            k0 = pl.multiple_of(j * BLK, BLK)
            bias_s[...] = score_bias(lo, row, k0)
            forward(q_st, k_ref, v_ref, pl.ds(k0, BLK), w_s, s_s, j, bias_s, a_acc)
            return c

        def bwd(j, c):
            keys = pl.ds(pl.multiple_of(j * BLK, BLK), BLK)
            backward(q_t, k_ref, v_ref, keys, BLK, w_s, s_s, j, da_st, da_t, dq_acc, dk_t, dv_t)
            return c

        lax.fori_loop(first, i + 1, fwd, 0)

        @pl.when(n == 0)
        def _():
            for copy in copies[2:5]:
                copy.wait()

        out, mixed, d_gate, d_att = middle(
            merge_heads(a_acc, BLK),
            x_s[rows, :].astype(F32),
            acts[rows, part_cols[0]].astype(F32),
            g_hist[rows, :],
            w_out[...],
        )
        out_s[rows, :] = out
        mixed_t[:, rows] = mixed.T.astype(BF16)
        d_pre[rows, part_cols[0]] = (d_gate * d_pre[rows, part_cols[0]].astype(F32)).astype(BF16)
        stack_heads(d_att, da_st, BLK)
        stack_columns(d_att.T, da_t, BLK)
        lax.fori_loop(first, i + 1, bwd, 0)

        @pl.when(n == 0)
        def _():
            copies[5].wait()

        d_q = merge_heads(dq_acc, BLK) * 0.125 * d_pre[rows, part_cols[2]].astype(F32)
        d_pre[rows, part_cols[2]] = d_q.astype(BF16)
        return carry

    lax.fori_loop(0, blocks, hist_block, 0)
    count = len(copies)
    sent_out = pltpu.make_async_copy(out_s, out_hist, sems.at[count])
    sent_out.start()
    for copy in copies[6:]:
        copy.wait()

    def spread(i, carry):
        rows = pl.ds(pl.multiple_of(i * BLK, BLK), BLK)
        vals, keys = part_cols[1], part_cols[3]
        d_pre[rows, vals] = ((dv_t[:, rows] + dv_add[:, rows].astype(F32)).T * d_pre[rows, vals].astype(F32)).astype(BF16)
        d_pre[rows, keys] = ((dk_t[:, rows] + dk_add[:, rows].astype(F32)).T * 2.0 * d_pre[rows, keys].astype(F32)).astype(BF16)
        return carry

    lax.fori_loop(0, blocks, spread, 0)
    sent = pltpu.make_async_copy(d_pre, d_pre_o, sems.at[count + 1])
    sent.start()

    core = core_ref[0]
    half_rows = feature // 2
    sent_give = pltpu.make_async_copy(give_s, give, sems.at[count + 2])
    for dest, half in ((give_s, 1 - core), (keep, core)):
        rows = pl.ds(pl.multiple_of(half * half_rows, half_rows), half_rows)
        for part in range(5):
            if part < 4:
                total = mm(normed_t[rows, :], d_pre[:, part_cols[part]])
                total = total + mm(tgt_t[0, rows, :], tgt_pre[:, part_cols[part]])
            else:
                total = mm(mixed_t[rows, :], g_hist[...]) + mm(tgt_t[1, rows, :], g_tgt[...])
            for group, dest_cols, cols in segments(part, feature):
                piece = total[:, cols].reshape(16, 16, cols.stop - cols.start)
                dest[:, group, :, dest_cols] = piece.astype(BF16)
        if dest is give_s:
            sent_give.start()
    sent_out.wait()
    sent.wait()
    sent_give.wait()


def segments(part, feature):
    found, begin = [], part * feature
    while begin < (part + 1) * feature:
        group = begin // 640
        end = min((part + 1) * feature, (group + 1) * 640)
        found.append(
            (group, slice(begin - group * 640, end - group * 640), slice(begin - part * feature, end - part * feature))
        )
        begin = end
    return found


def rows_kernel(d_pre, w_proj, normed, rstd, g_hist, pos_col, slot_grads, d_hist):
    hist_rows, feature = g_hist.shape

    def back(i, carry):
        rows = pl.ds(pl.multiple_of(i * BLK, BLK), BLK)
        d_normed = mm(d_pre[rows, :], w_proj[...], NT)
        unit = normed[rows, :].astype(F32)
        mean_d = jnp.mean(d_normed, axis=-1, keepdims=True)
        mean_dn = jnp.mean(d_normed * unit, axis=-1, keepdims=True)
        d_x = rstd[rows, :] * (d_normed - mean_d - unit * mean_dn)
        d_hist[rows, :] = (d_x + g_hist[rows, :].astype(F32)).astype(BF16)
        return carry

    lax.fori_loop(0, hist_rows // BLK, back, 0)

    def pick(i, carry):
        rows = pl.ds(pl.multiple_of(i * BLK, BLK), BLK)
        row = lax.broadcasted_iota(jnp.int32, (1, hist_rows), 1)
        onehot = one_hot(pos_col[rows, :] == row)
        slot_grads[rows, :] = mm(onehot, d_hist[...]).astype(BF16)
        return carry

    lax.fori_loop(0, slot_grads.shape[0] // BLK, pick, 0)


def cand_kernel(first_ref, rows, out):
    count, feature = out.shape
    own = first_ref[0] + lax.broadcasted_iota(jnp.int32, (count, 1), 0)
    total = jnp.zeros((count, feature), F32)
    for peer in range(rows.shape[0]):
        high = rows[peer, count : count + 16, :count].astype(F32)[:1]
        low = rows[peer, count : count + 16, count : 2 * count].astype(F32)[:1]
        ids = (high * 64.0 + low).astype(jnp.int32)
        total = total + mm(one_hot(own == ids), rows[peer, :count, :])
    out[...] = total


def reduce_kernel(pieces, slot_grads, copies):
    del slot_grads
    total = jnp.sum(pieces[...].astype(F32), axis=0).astype(BF16)
    for peer in range(copies.shape[0]):
        copies[peer] = total


def sums_kernel(pieces, d_proj, d_out):
    feature = d_out.shape[1]
    quarter = d_out.shape[0] // 8
    for level in range(4):
        for core in range(2):
            first = (core * 4 + level) * quarter
            rows = slice(first, first + quarter)
            for part in range(5):
                for group, source_cols, cols in segments(part, feature):
                    piece = pieces[level * 2 + core, :, group, :, source_cols].astype(F32)
                    piece = piece.reshape(quarter, cols.stop - cols.start)
                    if part < 4:
                        base = part * feature
                        d_proj[rows, base + cols.start : base + cols.stop] = piece
                    else:
                        d_out[rows, cols] = piece


VMEM = pl.BlockSpec(memory_space=pltpu.VMEM)
SMEM = pl.BlockSpec(memory_space=pltpu.SMEM)
ANY = pl.BlockSpec(memory_space=pl.ANY)


def params(mib):
    return pltpu.CompilerParams(vmem_limit_bytes=mib << 20)


def cost(flops, nbytes):
    return pl.CostEstimate(flops=flops, bytes_accessed=nbytes, transcendentals=0)


def local(
    send_rows, slot_pos, lengths, candidates, target_ids, w_proj, w_out, g_hist, g_tgt
):
    peers, capacity, feature = send_rows.shape[1:]
    slots = peers * capacity
    hist_rows, tgt_rows = g_hist.shape[0], g_tgt.shape[0]
    blocks = hist_rows // BLK
    each = target_ids.shape[1]
    table = lax.all_gather(candidates, "mem", axis=0, tiled=True)
    arrived = lax.all_to_all(send_rows, BOTH, split_axis=1, concat_axis=0, tiled=True)
    arrived = arrived.reshape(slots, feature)

    pos_row = slot_pos.reshape(1, slots)
    pos_col = slot_pos.reshape(slots, 1)
    ends = jnp.cumsum(lengths[0])
    starts = ends - lengths[0]
    row = jnp.arange(0, hist_rows, BLK, dtype=jnp.int32)[:, None]
    first = jnp.max(jnp.where(row >= starts[None, :], starts[None, :], 0), axis=1) // BLK
    first = first.astype(jnp.int32)
    tgt_lo = jnp.repeat(starts, each).astype(jnp.int32)[:, None]
    tgt_hi = jnp.repeat(ends - 1, each).astype(jnp.int32)[:, None]
    core = lax.rem(lax.axis_index("grp"), 2).astype(jnp.int32)[None]

    sds = jax.ShapeDtypeStruct

    def by_rows(width):
        return pl.BlockSpec((BLK, width), lambda i: (i, 0))

    def whole(*shape):
        return pl.BlockSpec(shape, lambda i: (0,) * len(shape))

    x_hist, normed, rstd, normed_t, acts, slopes = pl.pallas_call(
        project_kernel,
        grid=(blocks,),
        out_shape=(
            sds((hist_rows, feature), BF16),
            sds((hist_rows, feature), BF16),
            sds((hist_rows, 1), F32),
            sds((feature, hist_rows), BF16),
            sds((hist_rows, 4 * feature), BF16),
            sds((hist_rows, 4 * feature), BF16),
        ),
        in_specs=[whole(slots, feature), whole(1, slots), whole(feature, 4 * feature)],
        out_specs=(
            by_rows(feature),
            by_rows(feature),
            by_rows(1),
            pl.BlockSpec((feature, BLK), lambda i: (0, i)),
            by_rows(4 * feature),
            by_rows(4 * feature),
        ),
        compiler_params=params(56),
        cost_estimate=cost(5 << 30, 20 << 20),
        name="project",
    )(arrived, pos_row, w_proj)

    scratch = pltpu.VMEM
    out_tgt, d_tgt, dk_t, dv_t, tgt_t, tgt_pre = pl.pallas_call(
        tgt_kernel,
        out_shape=(
            sds((tgt_rows, feature), BF16),
            sds((tgt_rows + 16, feature), BF16),
            sds((feature, hist_rows), BF16),
            sds((feature, hist_rows), BF16),
            sds((2, feature, tgt_rows), BF16),
            sds((tgt_rows, 4 * feature), BF16),
        ),
        in_specs=[VMEM] * 8 + [ANY],
        out_specs=(VMEM,) * 6,
        scratch_shapes=[
            scratch((feature, hist_rows), F32),
            scratch((feature, hist_rows), F32),
            scratch((hist_rows, feature), BF16),
            scratch((hist_rows, feature), BF16),
            pltpu.SemaphoreType.DMA((2,)),
            scratch((tgt_rows, 4 * feature), BF16),
            scratch((blocks + 1, PAIRS, 2 * tgt_rows, BLK), BF16),
            scratch((blocks + 1, PAIRS, 2 * tgt_rows, BLK), BF16),
            scratch((tgt_rows, BLK), F32),
            scratch((tgt_rows, tgt_rows), F32),
            scratch((PAIRS, 2 * tgt_rows, 128), F32),
            scratch((PAIRS, 2 * tgt_rows, 128), F32),
            scratch((PAIRS, 2 * tgt_rows, 128), BF16),
            scratch((PAIRS, 2 * tgt_rows, 128), BF16),
            scratch((PAIRS, 128, 2 * tgt_rows), BF16),
            scratch((PAIRS, 128, 2 * tgt_rows), BF16),
            scratch((feature, tgt_rows), F32),
            scratch((feature, tgt_rows), F32),
        ],
        compiler_params=params(56),
        cost_estimate=cost(6 << 30, 16 << 20),
        name="tgt",
    )(
        table,
        target_ids.reshape(tgt_rows, 1),
        target_ids.reshape(1, tgt_rows),
        tgt_lo,
        tgt_hi,
        w_proj,
        w_out,
        g_tgt,
        acts,
    )
    tgt_grads = lax.all_gather(d_tgt, "mem", axis=0, tiled=False)

    pieces = (16, 4, 16, 640)
    out_hist, keep, give, d_pre = pl.pallas_call(
        hist_kernel,
        out_shape=(
            sds((hist_rows, feature), BF16),
            sds(pieces, BF16),
            sds(pieces, BF16),
            sds((hist_rows, 4 * feature), BF16),
        ),
        in_specs=[SMEM] * 3 + [VMEM] * 5 + [ANY] * 6,
        out_specs=(ANY, VMEM, ANY, ANY),
        scratch_shapes=[
            scratch((hist_rows, 4 * feature), BF16),
            scratch((hist_rows, feature), BF16),
            scratch((hist_rows, 4 * feature), BF16),
            scratch((feature, hist_rows), BF16),
            scratch((feature, hist_rows), BF16),
            scratch((feature, hist_rows), F32),
            scratch((feature, hist_rows), F32),
            scratch((feature, hist_rows), BF16),
            scratch((feature, hist_rows), BF16),
            scratch((hist_rows, feature), BF16),
            scratch(pieces, BF16),
            pltpu.SemaphoreType.DMA((14,)),
            scratch((blocks, PAIRS, 2 * BLK, BLK), BF16),
            scratch((blocks, PAIRS, 2 * BLK, BLK), BF16),
            scratch((BLK, BLK), F32),
            scratch((PAIRS, 2 * BLK, 128), F32),
            scratch((PAIRS, 2 * BLK, 128), F32),
            scratch((PAIRS, 2 * BLK, 128), BF16),
            scratch((PAIRS, 2 * BLK, 128), BF16),
            scratch((PAIRS, 128, 2 * BLK), BF16),
            scratch((PAIRS, 128, 2 * BLK), BF16),
        ],
        compiler_params=params(56),
        cost_estimate=cost(18 << 30, 24 << 20),
        name="hist",
    )(
        core,
        first,
        starts.astype(jnp.int32),
        w_out,
        g_hist,
        g_tgt,
        tgt_t,
        tgt_pre,
        acts,
        x_hist,
        slopes,
        dv_t,
        dk_t,
        normed_t,
    )

    swapped = lax.ppermute(give, BOTH, core_swap())
    chip_sum = (keep.astype(F32) + swapped.astype(F32)).astype(BF16)
    chip_sum = chip_sum.reshape(64, 1, 16, 640)
    scattered = lax.all_to_all(
        chip_sum, BOTH, split_axis=0, concat_axis=1, tiled=True, axis_index_groups=same_core()
    )
    slot_grads = pl.pallas_call(
        rows_kernel,
        out_shape=sds((slots, feature), BF16),
        in_specs=[VMEM] * 6,
        out_specs=VMEM,
        scratch_shapes=[scratch((hist_rows, feature), BF16)],
        compiler_params=params(56),
        cost_estimate=cost(5 << 30, 16 << 20),
        name="rows",
    )(d_pre, w_proj, normed, rstd, g_hist, pos_col)
    copies = pl.pallas_call(
        reduce_kernel,
        out_shape=sds((16, 16, 640), BF16),
        in_specs=[VMEM, ANY],
        out_specs=VMEM,
        compiler_params=params(56),
        name="reduce",
    )(scattered.reshape(64, 16, 640), slot_grads)
    level = lax.all_to_all(
        copies.reshape(16, 1, 16, 640), "mem", split_axis=0, concat_axis=1, tiled=True
    ).reshape(256, 640)
    everything = lax.all_gather(level, "grp", axis=0, tiled=True)

    returned = lax.all_to_all(
        slot_grads.reshape(peers, 1, capacity, feature),
        BOTH,
        split_axis=0,
        concat_axis=1,
        tiled=True,
    )
    sum_proj, sum_out = pl.pallas_call(
        sums_kernel,
        out_shape=(sds(w_proj.shape, F32), sds(w_out.shape, F32)),
        in_specs=[VMEM],
        out_specs=(VMEM, VMEM),
        compiler_params=params(16),
        name="sums",
    )(everything.reshape(8, 4, 4, 16, 640))

    mine = (lax.axis_index("mem") * candidates.shape[0]).astype(jnp.int32)[None]
    d_cand = pl.pallas_call(
        cand_kernel,
        out_shape=sds(candidates.shape, F32),
        in_specs=[SMEM, VMEM],
        out_specs=VMEM,
        compiler_params=params(56),
        name="cand",
    )(mine, tgt_grads)
    return (out_hist, out_tgt, returned, d_cand, sum_proj, sum_out)


def core_swap():
    return [(i, i + 16 if (i // 16) % 2 == 0 else i - 16) for i in range(128)]


def same_core():
    return [[i for i in range(128) if (i // 16) % 2 == core] for core in (0, 1)]


def solution(mesh):
    placed = (
        P(BOTH, None, None, None),
        P(BOTH, None, None),
        P(BOTH, None),
        P(BOTH, None),
        P(BOTH, None),
        P(),
        P(),
        P(BOTH, None),
        P(BOTH, None),
    )
    return jax.shard_map(
        local,
        mesh=mesh,
        in_specs=placed,
        out_specs=(
            P(BOTH, None),
            P(BOTH, None),
            P(BOTH, None, None, None),
            P(BOTH, None),
            P(),
            P(),
        ),
        check_vma=False,
    )
```

```python
import jax
import jax.numpy as jnp
from jax import lax
from jax.experimental import pallas as pl
from jax.experimental.pallas import tpu as pltpu
from jax.sharding import PartitionSpec as P

HEADS = 8
PAIRS = HEADS // 2
EPS = 1e-05
BLK = 256
MASKED = -1e9
F32 = jnp.float32
BF16 = jnp.bfloat16
BOTH = ("grp", "mem")
NN = (((1,), (0,)), ((), ()))
NT = (((1,), (1,)), ((), ()))


def mm(left, right, dims=NN):
    return lax.dot_general(left, right, dims, preferred_element_type=F32)


def moments(values):
    centred = values - jnp.mean(values, axis=-1, keepdims=True)
    variance = jnp.mean(centred * centred, axis=-1, keepdims=True)
    return centred, lax.rsqrt(variance + EPS)


def head_masks():
    lane = lax.broadcasted_iota(jnp.int32, (1, 128), 1)
    low_half = jnp.where(lane < 64, 1.0, 0.0).astype(F32)
    return (low_half, 1.0 - low_half)


def silu_parts(half):
    t = jnp.tanh(half)
    u = 1.0 + t
    return half * u, 0.5 * u * (1.0 + half * (1.0 - t))


def one_hot(hits):
    return jnp.where(hits, 1.0, 0.0).astype(BF16)


def score_bias(lo, hi, k0):
    key = k0 + lax.broadcasted_iota(jnp.int32, (1, BLK), 1)
    allowed = (key >= lo) & (key <= hi)
    return jnp.where(allowed, 0.0, MASKED).astype(F32)


def stack_heads(rows, dest, size):
    for pair in range(PAIRS):
        both = rows[:, pair * 128 : (pair + 1) * 128]
        for place, keep in enumerate(head_masks()):
            dest[pair, place * size : (place + 1) * size, :] = (both * keep).astype(BF16)


def stack_columns(rows_t, dest, size):
    for head in range(HEADS):
        pair, place = head // 2, head % 2
        own = rows_t[head * 64 : (head + 1) * 64, :].astype(BF16)
        dest[pair, place * 64 : (place + 1) * 64, place * size : (place + 1) * size] = own


def merge_heads(acc, size):
    first, second = head_masks()
    return jnp.concatenate(
        [acc[pair, :size, :] * first + acc[pair, size:, :] * second for pair in range(PAIRS)],
        axis=1,
    )


def forward(q_st, k_ref, v_ref, keys, w_s, s_s, slot, bias, a_acc):
    size, width = bias.shape
    for pair in range(PAIRS):
        cols = slice(pair * 128, (pair + 1) * 128)
        half = mm(q_st[pair], k_ref[keys, cols], NT).reshape(2, size, width)
        weight, slope = silu_parts((half + bias[...][None]).reshape(2 * size, width))
        weight = weight.astype(BF16)
        w_s[slot, pair, :, :width] = weight
        s_s[slot, pair, :, :width] = slope.astype(BF16)
        a_acc[pair] += mm(weight, v_ref[keys, cols])


def backward(q_t, k_ref, v_ref, keys, width, w_s, s_s, slot, da_st, da_t, dq_acc, dk_t, dv_t, add):
    for pair in range(PAIRS):
        cols = slice(pair * 128, (pair + 1) * 128)
        d_weight = mm(da_st[pair], v_ref[keys, cols], NT)
        d_score = (d_weight * s_s[slot, pair, :, :width].astype(F32)).astype(BF16)
        dq_acc[pair] += mm(d_score, k_ref[keys, cols])
        d_val = mm(da_t[pair], w_s[slot, pair, :, :width])
        d_key = mm(q_t[pair], d_score)
        if add:
            dv_t[cols, keys] += d_val
            dk_t[cols, keys] += d_key
        else:
            dv_t[cols, keys] = d_val.astype(dv_t.dtype)
            dk_t[cols, keys] = d_key.astype(dk_t.dtype)


def middle(attended, x, gate, g, w_out):
    centred, rstd = moments(attended)
    normed = centred * rstd
    mixed = normed * gate
    out = (x + mm(mixed.astype(BF16), w_out)).astype(BF16)
    d_mixed = mm(g, w_out, NT)
    d_normed = d_mixed * gate
    mean_d = jnp.mean(d_normed, axis=-1, keepdims=True)
    mean_dn = jnp.mean(d_normed * normed, axis=-1, keepdims=True)
    d_att = rstd * (d_normed - mean_d - normed * mean_dn)
    return out, mixed, d_mixed * normed, d_att


def project_kernel(
    arrived, pos_row, w_proj, x_o, normed_o, rstd_o, normed_t, acts, slopes
):
    size, feature = x_o.shape
    row = pl.program_id(0) * size + lax.broadcasted_iota(jnp.int32, (size, 1), 0)
    x = mm(one_hot(pos_row[...] == row), arrived[...])
    x_o[...] = x.astype(BF16)
    centred, rstd = moments(x)
    normed = centred * rstd
    rstd_o[...] = rstd
    normed_t[...] = normed.T.astype(BF16)
    normed = normed.astype(BF16)
    normed_o[...] = normed
    for part in range(4):
        cols = slice(part * feature, (part + 1) * feature)
        act, slope = silu_parts(mm(normed, w_proj[:, cols]) * 0.5)
        slopes[:, cols] = slope.astype(BF16)
        act = act.astype(BF16)
        acts[:, cols] = (act * 0.0625).astype(BF16) if part == 2 else act


def fetch(pairs, sems):
    copies = [pltpu.make_async_copy(src, dst, sems.at[i]) for i, (src, dst) in enumerate(pairs)]
    for copy in copies:
        copy.start()
    return copies


def tgt_kernel(
    cand,
    tid_col,
    tid_row,
    lo,
    hi,
    w_proj,
    w_out,
    g_tgt,
    acts_in,
    out_tgt,
    d_tgt,
    dk_o,
    dv_o,
    tgt_t,
    d_pre,
    k_s,
    v_s,
    sems,
    acts,
    w_s,
    s_s,
    bias_s,
    own_bias,
    a_acc,
    dq_acc,
    q_st,
    da_st,
    q_t,
    da_t,
    dk_own,
    dv_own,
):
    feature = out_tgt.shape[1]
    copies = fetch(
        [(acts_in.at[:, 3 * feature :], k_s), (acts_in.at[:, feature : 2 * feature], v_s)], sems
    )
    tgt_rows = out_tgt.shape[0]
    blocks = k_s.shape[0] // BLK
    every = slice(0, tgt_rows)
    part_cols = [slice(part * feature, (part + 1) * feature) for part in range(4)]
    col = lax.broadcasted_iota(jnp.int32, (1, cand.shape[0]), 1)
    x = mm(one_hot(tid_col[...] == col), cand[...])
    centred, rstd = moments(x)
    unit = centred * rstd
    normed = unit.astype(BF16)
    tgt_t[0] = unit.T.astype(BF16)
    for part in range(4):
        half = mm(normed, w_proj[:, part_cols[part]]) * 0.5
        act, slope = silu_parts(half)
        d_pre[:, part_cols[part]] = slope.astype(BF16)
        act = act.astype(BF16)
        acts[:, part_cols[part]] = (act * 0.0625).astype(BF16) if part == 2 else act
    qry = acts[:, part_cols[2]].astype(F32)
    q_t[...] = jnp.zeros_like(q_t)
    da_t[...] = jnp.zeros_like(da_t)
    stack_heads(qry, q_st, tgt_rows)
    stack_columns(qry.T, q_t, tgt_rows)

    a_acc[...] = jnp.zeros_like(a_acc)
    dq_acc[...] = jnp.zeros_like(dq_acc)
    for copy in copies:
        copy.wait()

    def fwd(j, c):
        k0 = pl.multiple_of(j * BLK, BLK)
        bias_s[...] = score_bias(lo[...], hi[...], k0)
        forward(q_st, k_s, v_s, pl.ds(k0, BLK), w_s, s_s, j, bias_s, a_acc)
        return c

    def bwd(j, c):
        keys = pl.ds(pl.multiple_of(j * BLK, BLK), BLK)
        backward(q_t, k_s, v_s, keys, BLK, w_s, s_s, j, da_st, da_t, dq_acc, dk_o, dv_o, False)
        return c

    lax.fori_loop(0, blocks, fwd, 0)
    same = lax.broadcasted_iota(jnp.int32, (tgt_rows, tgt_rows), 0) == lax.broadcasted_iota(
        jnp.int32, (tgt_rows, tgt_rows), 1
    )
    own_bias[...] = jnp.where(same, 0.0, MASKED).astype(F32)
    k_own, v_own = acts.at[:, part_cols[3]], acts.at[:, part_cols[1]]
    forward(q_st, k_own, v_own, every, w_s, s_s, blocks, own_bias, a_acc)
    gate = acts[:, part_cols[0]].astype(F32)
    out, mixed, d_gate, d_att = middle(merge_heads(a_acc, tgt_rows), x, gate, g_tgt[...], w_out[...])
    out_tgt[...] = out
    tgt_t[1] = mixed.T.astype(BF16)
    d_pre[:, part_cols[0]] = (d_gate * d_pre[:, part_cols[0]].astype(F32)).astype(BF16)
    stack_heads(d_att, da_st, tgt_rows)
    stack_columns(d_att.T, da_t, tgt_rows)
    lax.fori_loop(0, blocks, bwd, 0)
    backward(
        q_t, k_own, v_own, every, tgt_rows, w_s, s_s, blocks, da_st, da_t, dq_acc, dk_own, dv_own,
        False,
    )
    d_q = merge_heads(dq_acc, tgt_rows) * 0.125
    grads = (None, dv_own[...].T, d_q, dk_own[...].T * 2.0)
    for part in (1, 2, 3):
        d_part = grads[part] * d_pre[:, part_cols[part]].astype(F32)
        d_pre[:, part_cols[part]] = d_part.astype(BF16)

    d_normed = mm(d_pre[...], w_proj[...], NT)
    mean_d = jnp.mean(d_normed, axis=-1, keepdims=True)
    mean_dn = jnp.mean(d_normed * unit, axis=-1, keepdims=True)
    d_x = rstd * (d_normed - mean_d - unit * mean_dn) + g_tgt[...].astype(F32)
    d_tgt[every, :] = d_x.astype(BF16)
    ids = tid_row[...]
    high = lax.shift_right_logical(ids, 6)
    low = ids - high * 64
    d_tgt[tgt_rows:, :] = jnp.zeros((d_tgt.shape[0] - tgt_rows, feature), BF16)
    wide = (d_tgt.shape[0] - tgt_rows, tgt_rows)
    d_tgt[tgt_rows:, :tgt_rows] = jnp.broadcast_to(high.astype(F32), wide).astype(BF16)
    d_tgt[tgt_rows:, tgt_rows : 2 * tgt_rows] = jnp.broadcast_to(low.astype(F32), wide).astype(BF16)


def hist_kernel(
    core_ref,
    first_ref,
    starts_ref,
    w_out,
    g_hist,
    g_tgt,
    tgt_t,
    tgt_pre,
    acts_in,
    x_in,
    slopes_in,
    dv_in,
    dk_in,
    normed_t_in,
    out_hist,
    keep,
    give,
    d_pre_o,
    acts,
    x_s,
    d_pre,
    dv_add,
    dk_add,
    dv_t,
    dk_t,
    normed_t,
    mixed_t,
    out_s,
    give_s,
    sems,
    w_s,
    s_s,
    bias_s,
    a_acc,
    dq_acc,
    q_st,
    da_st,
    q_t,
    da_t,
):
    hist_rows, feature = g_hist.shape
    blocks = hist_rows // BLK
    part_cols = [slice(part * feature, (part + 1) * feature) for part in range(4)]
    gates, vals, qrys, ids = part_cols
    later = slice(2 * feature, 4 * feature)
    copies = fetch(
        [
            (acts_in.at[:, later], acts.at[:, later]),
            (acts_in.at[:, vals], acts.at[:, vals]),
            (acts_in.at[:, gates], acts.at[:, gates]),
            (x_in, x_s),
            (slopes_in.at[:, gates], d_pre.at[:, gates]),
            (slopes_in.at[:, qrys], d_pre.at[:, qrys]),
            (slopes_in.at[:, vals], d_pre.at[:, vals]),
            (slopes_in.at[:, ids], d_pre.at[:, ids]),
            (dv_in, dv_add),
            (dk_in, dk_add),
            (normed_t_in, normed_t),
        ],
        sems,
    )
    k_ref, v_ref = acts.at[:, part_cols[3]], acts.at[:, part_cols[1]]
    q_t[...] = jnp.zeros_like(q_t)
    da_t[...] = jnp.zeros_like(da_t)
    dk_t[...] = jnp.zeros_like(dk_t)
    dv_t[...] = jnp.zeros_like(dv_t)
    for copy in copies[:2]:
        copy.wait()

    def hist_block(n, carry):
        i = blocks - 1 - n
        r0 = pl.multiple_of(i * BLK, BLK)
        rows = pl.ds(r0, BLK)
        first = first_ref[i]
        row = r0 + lax.broadcasted_iota(jnp.int32, (BLK, 1), 0)
        lo = jnp.zeros((BLK, 1), jnp.int32)
        for user in range(starts_ref.shape[0]):
            lo = jnp.where(row >= starts_ref[user], starts_ref[user], lo)
        a_acc[...] = jnp.zeros_like(a_acc)
        dq_acc[...] = jnp.zeros_like(dq_acc)
        qry = acts[rows, part_cols[2]].astype(F32)
        stack_heads(qry, q_st, BLK)
        stack_columns(qry.T, q_t, BLK)

        def fwd(j, c):
            k0 = pl.multiple_of(j * BLK, BLK)
            bias_s[...] = score_bias(lo, row, k0)
            forward(q_st, k_ref, v_ref, pl.ds(k0, BLK), w_s, s_s, j, bias_s, a_acc)
            return c

        def bwd(j, c):
            keys = pl.ds(pl.multiple_of(j * BLK, BLK), BLK)
            backward(
                q_t, k_ref, v_ref, keys, BLK, w_s, s_s, j, da_st, da_t, dq_acc, dk_t, dv_t, True
            )
            return c

        lax.fori_loop(first, i + 1, fwd, 0)

        @pl.when(n == 0)
        def _():
            for copy in copies[2:5]:
                copy.wait()

        out, mixed, d_gate, d_att = middle(
            merge_heads(a_acc, BLK),
            x_s[rows, :].astype(F32),
            acts[rows, part_cols[0]].astype(F32),
            g_hist[rows, :],
            w_out[...],
        )
        out_s[rows, :] = out
        mixed_t[:, rows] = mixed.T.astype(BF16)
        d_pre[rows, part_cols[0]] = (d_gate * d_pre[rows, part_cols[0]].astype(F32)).astype(BF16)
        stack_heads(d_att, da_st, BLK)
        stack_columns(d_att.T, da_t, BLK)
        lax.fori_loop(first, i + 1, bwd, 0)

        @pl.when(n == 0)
        def _():
            copies[5].wait()

        d_q = merge_heads(dq_acc, BLK) * 0.125 * d_pre[rows, part_cols[2]].astype(F32)
        d_pre[rows, part_cols[2]] = d_q.astype(BF16)
        return carry

    lax.fori_loop(0, blocks, hist_block, 0)
    count = len(copies)
    sent_out = pltpu.make_async_copy(out_s, out_hist, sems.at[count])
    sent_out.start()
    for copy in copies[6:]:
        copy.wait()

    def spread(i, carry):
        rows = pl.ds(pl.multiple_of(i * BLK, BLK), BLK)
        vals, keys = part_cols[1], part_cols[3]
        d_pre[rows, vals] = ((dv_t[:, rows] + dv_add[:, rows].astype(F32)).T * d_pre[rows, vals].astype(F32)).astype(BF16)
        d_pre[rows, keys] = ((dk_t[:, rows] + dk_add[:, rows].astype(F32)).T * 2.0 * d_pre[rows, keys].astype(F32)).astype(BF16)
        return carry

    lax.fori_loop(0, blocks, spread, 0)
    sent = pltpu.make_async_copy(d_pre, d_pre_o, sems.at[count + 1])
    sent.start()

    core = core_ref[0]
    half_rows = feature // 2
    sent_give = pltpu.make_async_copy(give_s, give, sems.at[count + 2])
    for dest, half in ((give_s, 1 - core), (keep, core)):
        rows = pl.ds(pl.multiple_of(half * half_rows, half_rows), half_rows)
        for part in range(5):
            if part < 4:
                total = mm(normed_t[rows, :], d_pre[:, part_cols[part]])
                total = total + mm(tgt_t[0, rows, :], tgt_pre[:, part_cols[part]])
            else:
                total = mm(mixed_t[rows, :], g_hist[...]) + mm(tgt_t[1, rows, :], g_tgt[...])
            for group, dest_cols, cols in segments(part, feature):
                piece = total[:, cols].reshape(16, 16, cols.stop - cols.start)
                dest[:, group, :, dest_cols] = piece.astype(BF16)
        if dest is give_s:
            sent_give.start()
    sent_out.wait()
    sent.wait()
    sent_give.wait()


def segments(part, feature):
    found, begin = [], part * feature
    while begin < (part + 1) * feature:
        group = begin // 640
        end = min((part + 1) * feature, (group + 1) * 640)
        found.append(
            (group, slice(begin - group * 640, end - group * 640), slice(begin - part * feature, end - part * feature))
        )
        begin = end
    return found


def rows_kernel(d_pre, w_proj, normed, rstd, g_hist, pos_col, slot_grads, d_hist):
    hist_rows, feature = g_hist.shape

    def back(i, carry):
        rows = pl.ds(pl.multiple_of(i * BLK, BLK), BLK)
        d_normed = mm(d_pre[rows, :], w_proj[...], NT)
        unit = normed[rows, :].astype(F32)
        mean_d = jnp.mean(d_normed, axis=-1, keepdims=True)
        mean_dn = jnp.mean(d_normed * unit, axis=-1, keepdims=True)
        d_x = rstd[rows, :] * (d_normed - mean_d - unit * mean_dn)
        d_hist[rows, :] = (d_x + g_hist[rows, :].astype(F32)).astype(BF16)
        return carry

    lax.fori_loop(0, hist_rows // BLK, back, 0)

    def pick(i, carry):
        rows = pl.ds(pl.multiple_of(i * BLK, BLK), BLK)
        row = lax.broadcasted_iota(jnp.int32, (1, hist_rows), 1)
        onehot = one_hot(pos_col[rows, :] == row)
        slot_grads[rows, :] = mm(onehot, d_hist[...]).astype(BF16)
        return carry

    lax.fori_loop(0, slot_grads.shape[0] // BLK, pick, 0)


def cand_kernel(first_ref, rows, out):
    count, feature = out.shape
    own = first_ref[0] + lax.broadcasted_iota(jnp.int32, (count, 1), 0)
    total = jnp.zeros((count, feature), F32)
    for peer in range(rows.shape[0]):
        high = rows[peer, count : count + 16, :count].astype(F32)[:1]
        low = rows[peer, count : count + 16, count : 2 * count].astype(F32)[:1]
        ids = (high * 64.0 + low).astype(jnp.int32)
        total = total + mm(one_hot(own == ids), rows[peer, :count, :])
    out[...] = total


def reduce_kernel(pieces_in, slot_grads, copies, pieces, sems):
    del slot_grads
    count = pieces.shape[0] // 4
    chunks = [pl.ds(k * count, count) for k in range(4)]
    parts = fetch([(pieces_in.at[chunk], pieces.at[chunk]) for chunk in chunks], sems)
    total = jnp.zeros(pieces.shape[1:], F32)
    for chunk, part in zip(chunks, parts):
        part.wait()
        total = total + jnp.sum(pieces[chunk].astype(F32), axis=0)
    total = total.astype(BF16)
    for peer in range(copies.shape[0]):
        copies[peer] = total


def sums_kernel(pieces_in, d_proj_o, d_out_o, pieces, d_proj, d_out, sems, sent):
    feature = d_out.shape[1]
    quarter = d_out.shape[0] // 8
    count = pieces.shape[0]
    parts = fetch([(pieces_in.at[k], pieces.at[k]) for k in range(count)], sems)
    leaving = []
    for k in range(count):
        parts[k].wait()
        first = ((k % 2) * 4 + k // 2) * quarter
        rows = slice(first, first + quarter)
        for part in range(5):
            for group, source_cols, cols in segments(part, feature):
                piece = pieces[k, :, group, :, source_cols].astype(F32)
                piece = piece.reshape(quarter, cols.stop - cols.start)
                if part < 4:
                    base = part * feature
                    d_proj[rows, base + cols.start : base + cols.stop] = piece
                else:
                    d_out[rows, cols] = piece
        own = pl.ds(first, quarter)
        leaving.append(pltpu.make_async_copy(d_proj.at[own], d_proj_o.at[own], sent.at[2 * k]))
        leaving.append(pltpu.make_async_copy(d_out.at[own], d_out_o.at[own], sent.at[2 * k + 1]))
        leaving[-2].start()
        leaving[-1].start()
    for copy in leaving:
        copy.wait()


VMEM = pl.BlockSpec(memory_space=pltpu.VMEM)
SMEM = pl.BlockSpec(memory_space=pltpu.SMEM)
ANY = pl.BlockSpec(memory_space=pl.ANY)


def params(mib):
    return pltpu.CompilerParams(vmem_limit_bytes=mib << 20)


def cost(flops, nbytes):
    return pl.CostEstimate(flops=flops, bytes_accessed=nbytes, transcendentals=0)


def local(
    send_rows, slot_pos, lengths, candidates, target_ids, w_proj, w_out, g_hist, g_tgt
):
    peers, capacity, feature = send_rows.shape[1:]
    slots = peers * capacity
    hist_rows, tgt_rows = g_hist.shape[0], g_tgt.shape[0]
    blocks = hist_rows // BLK
    each = target_ids.shape[1]
    table = lax.all_gather(candidates, "mem", axis=0, tiled=True)
    arrived = lax.all_to_all(send_rows, BOTH, split_axis=1, concat_axis=0, tiled=True)
    arrived = arrived.reshape(slots, feature)

    pos_row = slot_pos.reshape(1, slots)
    pos_col = slot_pos.reshape(slots, 1)
    ends = jnp.cumsum(lengths[0])
    starts = ends - lengths[0]
    row = jnp.arange(0, hist_rows, BLK, dtype=jnp.int32)[:, None]
    first = jnp.max(jnp.where(row >= starts[None, :], starts[None, :], 0), axis=1) // BLK
    first = first.astype(jnp.int32)
    tgt_lo = jnp.repeat(starts, each).astype(jnp.int32)[:, None]
    tgt_hi = jnp.repeat(ends - 1, each).astype(jnp.int32)[:, None]
    core = lax.rem(lax.axis_index("grp"), 2).astype(jnp.int32)[None]

    sds = jax.ShapeDtypeStruct

    def by_rows(width):
        return pl.BlockSpec((BLK, width), lambda i: (i, 0))

    def whole(*shape):
        return pl.BlockSpec(shape, lambda i: (0,) * len(shape))

    x_hist, normed, rstd, normed_t, acts, slopes = pl.pallas_call(
        project_kernel,
        grid=(blocks,),
        out_shape=(
            sds((hist_rows, feature), BF16),
            sds((hist_rows, feature), BF16),
            sds((hist_rows, 1), F32),
            sds((feature, hist_rows), BF16),
            sds((hist_rows, 4 * feature), BF16),
            sds((hist_rows, 4 * feature), BF16),
        ),
        in_specs=[whole(slots, feature), whole(1, slots), whole(feature, 4 * feature)],
        out_specs=(
            by_rows(feature),
            by_rows(feature),
            by_rows(1),
            pl.BlockSpec((feature, BLK), lambda i: (0, i)),
            by_rows(4 * feature),
            by_rows(4 * feature),
        ),
        compiler_params=params(56),
        cost_estimate=cost(5 << 30, 20 << 20),
        name="project",
    )(arrived, pos_row, w_proj)

    scratch = pltpu.VMEM
    out_tgt, d_tgt, dk_t, dv_t, tgt_t, tgt_pre = pl.pallas_call(
        tgt_kernel,
        out_shape=(
            sds((tgt_rows, feature), BF16),
            sds((tgt_rows + 16, feature), BF16),
            sds((feature, hist_rows), BF16),
            sds((feature, hist_rows), BF16),
            sds((2, feature, tgt_rows), BF16),
            sds((tgt_rows, 4 * feature), BF16),
        ),
        in_specs=[VMEM] * 8 + [ANY],
        out_specs=(VMEM,) * 6,
        scratch_shapes=[
            scratch((hist_rows, feature), BF16),
            scratch((hist_rows, feature), BF16),
            pltpu.SemaphoreType.DMA((2,)),
            scratch((tgt_rows, 4 * feature), BF16),
            scratch((blocks + 1, PAIRS, 2 * tgt_rows, BLK), BF16),
            scratch((blocks + 1, PAIRS, 2 * tgt_rows, BLK), BF16),
            scratch((tgt_rows, BLK), F32),
            scratch((tgt_rows, tgt_rows), F32),
            scratch((PAIRS, 2 * tgt_rows, 128), F32),
            scratch((PAIRS, 2 * tgt_rows, 128), F32),
            scratch((PAIRS, 2 * tgt_rows, 128), BF16),
            scratch((PAIRS, 2 * tgt_rows, 128), BF16),
            scratch((PAIRS, 128, 2 * tgt_rows), BF16),
            scratch((PAIRS, 128, 2 * tgt_rows), BF16),
            scratch((feature, tgt_rows), F32),
            scratch((feature, tgt_rows), F32),
        ],
        compiler_params=params(56),
        cost_estimate=cost(6 << 30, 16 << 20),
        name="tgt",
    )(
        table,
        target_ids.reshape(tgt_rows, 1),
        target_ids.reshape(1, tgt_rows),
        tgt_lo,
        tgt_hi,
        w_proj,
        w_out,
        g_tgt,
        acts,
    )
    tgt_grads = lax.all_gather(d_tgt, "mem", axis=0, tiled=False)

    pieces = (16, 4, 16, 640)
    out_hist, keep, give, d_pre = pl.pallas_call(
        hist_kernel,
        out_shape=(
            sds((hist_rows, feature), BF16),
            sds(pieces, BF16),
            sds(pieces, BF16),
            sds((hist_rows, 4 * feature), BF16),
        ),
        in_specs=[SMEM] * 3 + [VMEM] * 5 + [ANY] * 6,
        out_specs=(ANY, VMEM, ANY, ANY),
        scratch_shapes=[
            scratch((hist_rows, 4 * feature), BF16),
            scratch((hist_rows, feature), BF16),
            scratch((hist_rows, 4 * feature), BF16),
            scratch((feature, hist_rows), BF16),
            scratch((feature, hist_rows), BF16),
            scratch((feature, hist_rows), F32),
            scratch((feature, hist_rows), F32),
            scratch((feature, hist_rows), BF16),
            scratch((feature, hist_rows), BF16),
            scratch((hist_rows, feature), BF16),
            scratch(pieces, BF16),
            pltpu.SemaphoreType.DMA((14,)),
            scratch((blocks, PAIRS, 2 * BLK, BLK), BF16),
            scratch((blocks, PAIRS, 2 * BLK, BLK), BF16),
            scratch((BLK, BLK), F32),
            scratch((PAIRS, 2 * BLK, 128), F32),
            scratch((PAIRS, 2 * BLK, 128), F32),
            scratch((PAIRS, 2 * BLK, 128), BF16),
            scratch((PAIRS, 2 * BLK, 128), BF16),
            scratch((PAIRS, 128, 2 * BLK), BF16),
            scratch((PAIRS, 128, 2 * BLK), BF16),
        ],
        compiler_params=params(56),
        cost_estimate=cost(18 << 30, 24 << 20),
        name="hist",
    )(
        core,
        first,
        starts.astype(jnp.int32),
        w_out,
        g_hist,
        g_tgt,
        tgt_t,
        tgt_pre,
        acts,
        x_hist,
        slopes,
        dv_t,
        dk_t,
        normed_t,
    )

    swapped = lax.ppermute(give, BOTH, core_swap())
    chip_sum = (keep.astype(F32) + swapped.astype(F32)).astype(BF16)
    chip_sum = chip_sum.reshape(64, 1, 16, 640)
    scattered = lax.all_to_all(
        chip_sum, BOTH, split_axis=0, concat_axis=1, tiled=True, axis_index_groups=same_core()
    )
    slot_grads = pl.pallas_call(
        rows_kernel,
        out_shape=sds((slots, feature), BF16),
        in_specs=[VMEM] * 6,
        out_specs=VMEM,
        scratch_shapes=[scratch((hist_rows, feature), BF16)],
        compiler_params=params(56),
        cost_estimate=cost(5 << 30, 16 << 20),
        name="rows",
    )(d_pre, w_proj, normed, rstd, g_hist, pos_col)
    copies = pl.pallas_call(
        reduce_kernel,
        out_shape=sds((16, 16, 640), BF16),
        in_specs=[ANY, ANY],
        out_specs=VMEM,
        scratch_shapes=[scratch((64, 16, 640), BF16), pltpu.SemaphoreType.DMA((4,))],
        compiler_params=params(60),
        name="reduce",
    )(scattered.reshape(64, 16, 640), slot_grads)
    level = lax.all_to_all(
        copies.reshape(16, 1, 16, 640), "mem", split_axis=0, concat_axis=1, tiled=True
    ).reshape(256, 640)
    everything = lax.all_gather(level, "grp", axis=0, tiled=True)

    returned = lax.all_to_all(
        slot_grads.reshape(peers, 1, capacity, feature),
        BOTH,
        split_axis=0,
        concat_axis=1,
        tiled=True,
    )
    sum_proj, sum_out = pl.pallas_call(
        sums_kernel,
        out_shape=(sds(w_proj.shape, F32), sds(w_out.shape, F32)),
        in_specs=[ANY],
        out_specs=(ANY, ANY),
        scratch_shapes=[
            scratch((8, 4, 4, 16, 640), BF16),
            scratch(w_proj.shape, F32),
            scratch(w_out.shape, F32),
            pltpu.SemaphoreType.DMA((8,)),
            pltpu.SemaphoreType.DMA((16,)),
        ],
        compiler_params=params(60),
        name="sums",
    )(everything.reshape(8, 4, 4, 16, 640))

    mine = (lax.axis_index("mem") * candidates.shape[0]).astype(jnp.int32)[None]
    d_cand = pl.pallas_call(
        cand_kernel,
        out_shape=sds(candidates.shape, F32),
        in_specs=[SMEM, VMEM],
        out_specs=VMEM,
        compiler_params=params(56),
        name="cand",
    )(mine, tgt_grads)
    return (out_hist, out_tgt, returned, d_cand, sum_proj, sum_out)


def core_swap():
    return [(i, i + 16 if (i // 16) % 2 == 0 else i - 16) for i in range(128)]


def same_core():
    return [[i for i in range(128) if (i // 16) % 2 == core] for core in (0, 1)]


def solution(mesh):
    placed = (
        P(BOTH, None, None, None),
        P(BOTH, None, None),
        P(BOTH, None),
        P(BOTH, None),
        P(BOTH, None),
        P(),
        P(),
        P(BOTH, None),
        P(BOTH, None),
    )
    return jax.shard_map(
        local,
        mesh=mesh,
        in_specs=placed,
        out_specs=(
            P(BOTH, None),
            P(BOTH, None),
            P(BOTH, None, None, None),
            P(BOTH, None),
            P(),
            P(),
        ),
        check_vma=False,
    )
```

```python
import jax
import jax.numpy as jnp
from jax import lax
from jax.experimental import pallas as pl
from jax.experimental.pallas import tpu as pltpu
from jax.sharding import PartitionSpec as P

HEADS = 8
PAIRS = HEADS // 2
EPS = 1e-05
BLK = 256
MASKED = -1e9
F32 = jnp.float32
BF16 = jnp.bfloat16
BOTH = ("grp", "mem")
NN = (((1,), (0,)), ((), ()))
NT = (((1,), (1,)), ((), ()))


def mm(left, right, dims=NN):
    return lax.dot_general(left, right, dims, preferred_element_type=F32)


def moments(values):
    centred = values - jnp.mean(values, axis=-1, keepdims=True)
    variance = jnp.mean(centred * centred, axis=-1, keepdims=True)
    return centred, lax.rsqrt(variance + EPS)


def head_masks():
    lane = lax.broadcasted_iota(jnp.int32, (1, 128), 1)
    low_half = jnp.where(lane < 64, 1.0, 0.0).astype(F32)
    return (low_half, 1.0 - low_half)


def silu_parts(half):
    t = jnp.tanh(half)
    u = 1.0 + t
    return half * u, 0.5 * u * (1.0 + half * (1.0 - t))


def one_hot(hits):
    return jnp.where(hits, 1.0, 0.0).astype(BF16)


def score_bias(lo, hi, k0):
    key = k0 + lax.broadcasted_iota(jnp.int32, (1, BLK), 1)
    allowed = (key >= lo) & (key <= hi)
    return jnp.where(allowed, 0.0, MASKED).astype(F32)


def stack_heads(rows, dest, size):
    for pair in range(PAIRS):
        both = rows[:, pair * 128 : (pair + 1) * 128]
        for place, keep in enumerate(head_masks()):
            dest[pair, place * size : (place + 1) * size, :] = (both * keep).astype(BF16)


def stack_columns(rows_t, dest, size):
    for head in range(HEADS):
        pair, place = head // 2, head % 2
        own = rows_t[head * 64 : (head + 1) * 64, :].astype(BF16)
        dest[pair, place * 64 : (place + 1) * 64, place * size : (place + 1) * size] = own


def merge_heads(acc, size):
    first, second = head_masks()
    return jnp.concatenate(
        [acc[pair, :size, :] * first + acc[pair, size:, :] * second for pair in range(PAIRS)],
        axis=1,
    )


def forward(q_st, k_ref, v_ref, keys, w_s, s_s, slot, bias, a_acc):
    size, width = bias.shape
    for pair in range(PAIRS):
        cols = slice(pair * 128, (pair + 1) * 128)
        half = mm(q_st[pair], k_ref[keys, cols], NT).reshape(2, size, width)
        weight, slope = silu_parts((half + bias[...][None]).reshape(2 * size, width))
        weight = weight.astype(BF16)
        w_s[slot, pair, :, :width] = weight
        s_s[slot, pair, :, :width] = slope.astype(BF16)
        a_acc[pair] += mm(weight, v_ref[keys, cols])


def backward(q_t, k_ref, v_ref, keys, width, w_s, s_s, slot, da_st, da_t, dq_acc, dk_t, dv_t, add):
    for pair in range(PAIRS):
        cols = slice(pair * 128, (pair + 1) * 128)
        d_weight = mm(da_st[pair], v_ref[keys, cols], NT)
        d_score = (d_weight * s_s[slot, pair, :, :width].astype(F32)).astype(BF16)
        dq_acc[pair] += mm(d_score, k_ref[keys, cols])
        d_val = mm(da_t[pair], w_s[slot, pair, :, :width])
        d_key = mm(q_t[pair], d_score)
        if add:
            dv_t[cols, keys] += d_val
            dk_t[cols, keys] += d_key
        else:
            dv_t[cols, keys] = d_val.astype(dv_t.dtype)
            dk_t[cols, keys] = d_key.astype(dk_t.dtype)


def middle(attended, x, gate, g, w_out):
    centred, rstd = moments(attended)
    normed = centred * rstd
    mixed = normed * gate
    out = (x + mm(mixed.astype(BF16), w_out)).astype(BF16)
    d_mixed = mm(g, w_out, NT)
    d_normed = d_mixed * gate
    mean_d = jnp.mean(d_normed, axis=-1, keepdims=True)
    mean_dn = jnp.mean(d_normed * normed, axis=-1, keepdims=True)
    d_att = rstd * (d_normed - mean_d - normed * mean_dn)
    return out, mixed, d_mixed * normed, d_att


def project_kernel(
    arrived, pos_row, w_proj, x_o, normed_o, rstd_o, normed_t, acts, slopes
):
    size, feature = x_o.shape
    row = pl.program_id(0) * size + lax.broadcasted_iota(jnp.int32, (size, 1), 0)
    x = mm(one_hot(pos_row[...] == row), arrived[...])
    x_o[...] = x.astype(BF16)
    centred, rstd = moments(x)
    normed = centred * rstd
    rstd_o[...] = rstd
    normed_t[...] = normed.T.astype(BF16)
    normed = normed.astype(BF16)
    normed_o[...] = normed
    for part in range(4):
        cols = slice(part * feature, (part + 1) * feature)
        act, slope = silu_parts(mm(normed, w_proj[:, cols]) * 0.5)
        slopes[:, cols] = slope.astype(BF16)
        act = act.astype(BF16)
        acts[:, cols] = (act * 0.0625).astype(BF16) if part == 2 else act


def fetch(pairs, sems):
    copies = [pltpu.make_async_copy(src, dst, sems.at[i]) for i, (src, dst) in enumerate(pairs)]
    for copy in copies:
        copy.start()
    return copies


def tgt_kernel(
    cand,
    tid_col,
    tid_row,
    lo,
    hi,
    w_proj,
    w_out,
    g_tgt,
    acts_in,
    out_tgt,
    d_tgt,
    dk_o,
    dv_o,
    tgt_t,
    d_pre,
    k_s,
    v_s,
    sems,
    acts,
    w_s,
    s_s,
    bias_s,
    own_bias,
    a_acc,
    dq_acc,
    q_st,
    da_st,
    q_t,
    da_t,
    dk_own,
    dv_own,
):
    feature = out_tgt.shape[1]
    copies = fetch(
        [(acts_in.at[:, 3 * feature :], k_s), (acts_in.at[:, feature : 2 * feature], v_s)], sems
    )
    tgt_rows = out_tgt.shape[0]
    blocks = k_s.shape[0] // BLK
    every = slice(0, tgt_rows)
    part_cols = [slice(part * feature, (part + 1) * feature) for part in range(4)]
    col = lax.broadcasted_iota(jnp.int32, (1, cand.shape[0]), 1)
    x = mm(one_hot(tid_col[...] == col), cand[...])
    centred, rstd = moments(x)
    unit = centred * rstd
    normed = unit.astype(BF16)
    tgt_t[0] = unit.T.astype(BF16)
    for part in range(4):
        half = mm(normed, w_proj[:, part_cols[part]]) * 0.5
        act, slope = silu_parts(half)
        d_pre[:, part_cols[part]] = slope.astype(BF16)
        act = act.astype(BF16)
        acts[:, part_cols[part]] = (act * 0.0625).astype(BF16) if part == 2 else act
    qry = acts[:, part_cols[2]].astype(F32)
    q_t[...] = jnp.zeros_like(q_t)
    da_t[...] = jnp.zeros_like(da_t)
    stack_heads(qry, q_st, tgt_rows)
    stack_columns(qry.T, q_t, tgt_rows)

    a_acc[...] = jnp.zeros_like(a_acc)
    dq_acc[...] = jnp.zeros_like(dq_acc)
    for copy in copies:
        copy.wait()

    def fwd(j, c):
        k0 = pl.multiple_of(j * BLK, BLK)
        bias_s[...] = score_bias(lo[...], hi[...], k0)
        forward(q_st, k_s, v_s, pl.ds(k0, BLK), w_s, s_s, j, bias_s, a_acc)
        return c

    def bwd(j, c):
        keys = pl.ds(pl.multiple_of(j * BLK, BLK), BLK)
        backward(q_t, k_s, v_s, keys, BLK, w_s, s_s, j, da_st, da_t, dq_acc, dk_o, dv_o, False)
        return c

    lax.fori_loop(0, blocks, fwd, 0)
    same = lax.broadcasted_iota(jnp.int32, (tgt_rows, tgt_rows), 0) == lax.broadcasted_iota(
        jnp.int32, (tgt_rows, tgt_rows), 1
    )
    own_bias[...] = jnp.where(same, 0.0, MASKED).astype(F32)
    k_own, v_own = acts.at[:, part_cols[3]], acts.at[:, part_cols[1]]
    forward(q_st, k_own, v_own, every, w_s, s_s, blocks, own_bias, a_acc)
    gate = acts[:, part_cols[0]].astype(F32)
    out, mixed, d_gate, d_att = middle(merge_heads(a_acc, tgt_rows), x, gate, g_tgt[...], w_out[...])
    out_tgt[...] = out
    tgt_t[1] = mixed.T.astype(BF16)
    d_pre[:, part_cols[0]] = (d_gate * d_pre[:, part_cols[0]].astype(F32)).astype(BF16)
    stack_heads(d_att, da_st, tgt_rows)
    stack_columns(d_att.T, da_t, tgt_rows)
    lax.fori_loop(0, blocks, bwd, 0)
    backward(
        q_t, k_own, v_own, every, tgt_rows, w_s, s_s, blocks, da_st, da_t, dq_acc, dk_own, dv_own,
        False,
    )
    d_q = merge_heads(dq_acc, tgt_rows) * 0.125
    grads = (None, dv_own[...].T, d_q, dk_own[...].T * 2.0)
    for part in (1, 2, 3):
        d_part = grads[part] * d_pre[:, part_cols[part]].astype(F32)
        d_pre[:, part_cols[part]] = d_part.astype(BF16)

    d_normed = mm(d_pre[...], w_proj[...], NT)
    mean_d = jnp.mean(d_normed, axis=-1, keepdims=True)
    mean_dn = jnp.mean(d_normed * unit, axis=-1, keepdims=True)
    d_x = rstd * (d_normed - mean_d - unit * mean_dn) + g_tgt[...].astype(F32)
    d_tgt[every, :] = d_x.astype(BF16)
    ids = tid_row[...]
    high = lax.shift_right_logical(ids, 6)
    low = ids - high * 64
    d_tgt[tgt_rows:, :] = jnp.zeros((d_tgt.shape[0] - tgt_rows, feature), BF16)
    wide = (d_tgt.shape[0] - tgt_rows, tgt_rows)
    d_tgt[tgt_rows:, :tgt_rows] = jnp.broadcast_to(high.astype(F32), wide).astype(BF16)
    d_tgt[tgt_rows:, tgt_rows : 2 * tgt_rows] = jnp.broadcast_to(low.astype(F32), wide).astype(BF16)


def hist_kernel(
    core_ref,
    first_ref,
    starts_ref,
    w_out,
    g_hist,
    g_tgt,
    tgt_t,
    tgt_pre,
    acts_in,
    x_in,
    slopes_in,
    dv_in,
    dk_in,
    normed_t_in,
    out_hist,
    keep,
    give,
    d_pre_o,
    acts,
    x_s,
    d_pre,
    dv_add,
    dk_add,
    dv_t,
    dk_t,
    normed_t,
    mixed_t,
    out_s,
    give_s,
    sems,
    w_s,
    s_s,
    bias_s,
    a_acc,
    dq_acc,
    q_st,
    da_st,
    q_t,
    da_t,
):
    hist_rows, feature = g_hist.shape
    blocks = hist_rows // BLK
    part_cols = [slice(part * feature, (part + 1) * feature) for part in range(4)]
    gates, vals, qrys, ids = part_cols
    later = slice(2 * feature, 4 * feature)
    copies = fetch(
        [
            (acts_in.at[:, later], acts.at[:, later]),
            (acts_in.at[:, vals], acts.at[:, vals]),
            (acts_in.at[:, gates], acts.at[:, gates]),
            (x_in, x_s),
            (slopes_in.at[:, gates], d_pre.at[:, gates]),
            (slopes_in.at[:, qrys], d_pre.at[:, qrys]),
            (slopes_in.at[:, vals], d_pre.at[:, vals]),
            (slopes_in.at[:, ids], d_pre.at[:, ids]),
            (dv_in, dv_add),
            (dk_in, dk_add),
            (normed_t_in, normed_t),
        ],
        sems,
    )
    k_ref, v_ref = acts.at[:, part_cols[3]], acts.at[:, part_cols[1]]
    q_t[...] = jnp.zeros_like(q_t)
    da_t[...] = jnp.zeros_like(da_t)
    dk_t[...] = jnp.zeros_like(dk_t)
    dv_t[...] = jnp.zeros_like(dv_t)
    for copy in copies[:2]:
        copy.wait()

    def hist_block(n, carry):
        i = blocks - 1 - n
        r0 = pl.multiple_of(i * BLK, BLK)
        rows = pl.ds(r0, BLK)
        first = first_ref[i]
        row = r0 + lax.broadcasted_iota(jnp.int32, (BLK, 1), 0)
        lo = jnp.zeros((BLK, 1), jnp.int32)
        for user in range(starts_ref.shape[0]):
            lo = jnp.where(row >= starts_ref[user], starts_ref[user], lo)
        a_acc[...] = jnp.zeros_like(a_acc)
        dq_acc[...] = jnp.zeros_like(dq_acc)
        qry = acts[rows, part_cols[2]].astype(F32)
        stack_heads(qry, q_st, BLK)
        stack_columns(qry.T, q_t, BLK)

        def fwd(j, c):
            k0 = pl.multiple_of(j * BLK, BLK)
            bias_s[...] = score_bias(lo, row, k0)
            forward(q_st, k_ref, v_ref, pl.ds(k0, BLK), w_s, s_s, j, bias_s, a_acc)
            return c

        def bwd(j, c):
            keys = pl.ds(pl.multiple_of(j * BLK, BLK), BLK)
            backward(
                q_t, k_ref, v_ref, keys, BLK, w_s, s_s, j, da_st, da_t, dq_acc, dk_t, dv_t, True
            )
            return c

        lax.fori_loop(first, i + 1, fwd, 0)

        @pl.when(n == 0)
        def _():
            for copy in copies[2:5]:
                copy.wait()

        out, mixed, d_gate, d_att = middle(
            merge_heads(a_acc, BLK),
            x_s[rows, :].astype(F32),
            acts[rows, part_cols[0]].astype(F32),
            g_hist[rows, :],
            w_out[...],
        )
        out_s[rows, :] = out
        mixed_t[:, rows] = mixed.T.astype(BF16)
        d_pre[rows, part_cols[0]] = (d_gate * d_pre[rows, part_cols[0]].astype(F32)).astype(BF16)
        stack_heads(d_att, da_st, BLK)
        stack_columns(d_att.T, da_t, BLK)
        lax.fori_loop(first, i + 1, bwd, 0)

        @pl.when(n == 0)
        def _():
            copies[5].wait()

        d_q = merge_heads(dq_acc, BLK) * 0.125 * d_pre[rows, part_cols[2]].astype(F32)
        d_pre[rows, part_cols[2]] = d_q.astype(BF16)
        return carry

    lax.fori_loop(0, blocks, hist_block, 0)
    count = len(copies)
    sent_out = pltpu.make_async_copy(out_s, out_hist, sems.at[count])
    sent_out.start()
    for copy in copies[6:]:
        copy.wait()

    def spread(i, carry):
        rows = pl.ds(pl.multiple_of(i * BLK, BLK), BLK)
        vals, keys = part_cols[1], part_cols[3]
        d_pre[rows, vals] = ((dv_t[:, rows] + dv_add[:, rows].astype(F32)).T * d_pre[rows, vals].astype(F32)).astype(BF16)
        d_pre[rows, keys] = ((dk_t[:, rows] + dk_add[:, rows].astype(F32)).T * 2.0 * d_pre[rows, keys].astype(F32)).astype(BF16)
        return carry

    lax.fori_loop(0, blocks, spread, 0)
    sent = pltpu.make_async_copy(d_pre, d_pre_o, sems.at[count + 1])
    sent.start()

    core = core_ref[0]
    half_rows = feature // 2
    sent_give = pltpu.make_async_copy(give_s, give, sems.at[count + 2])
    for dest, half in ((give_s, 1 - core), (keep, core)):
        rows = pl.ds(pl.multiple_of(half * half_rows, half_rows), half_rows)
        for part in range(5):
            if part < 4:
                total = mm(normed_t[rows, :], d_pre[:, part_cols[part]])
                total = total + mm(tgt_t[0, rows, :], tgt_pre[:, part_cols[part]])
            else:
                total = mm(mixed_t[rows, :], g_hist[...]) + mm(tgt_t[1, rows, :], g_tgt[...])
            for group, dest_cols, cols in segments(part, feature):
                piece = total[:, cols].reshape(16, 16, cols.stop - cols.start)
                dest[:, group, :, dest_cols] = piece.astype(BF16)
        if dest is give_s:
            sent_give.start()
    sent_out.wait()
    sent.wait()
    sent_give.wait()


def segments(part, feature):
    found, begin = [], part * feature
    while begin < (part + 1) * feature:
        group = begin // 640
        end = min((part + 1) * feature, (group + 1) * 640)
        found.append(
            (group, slice(begin - group * 640, end - group * 640), slice(begin - part * feature, end - part * feature))
        )
        begin = end
    return found


def rows_kernel(d_pre, w_proj, normed, rstd, g_hist, pos_col, slot_grads, d_hist):
    hist_rows, feature = g_hist.shape

    def back(i, carry):
        rows = pl.ds(pl.multiple_of(i * BLK, BLK), BLK)
        d_normed = mm(d_pre[rows, :], w_proj[...], NT)
        unit = normed[rows, :].astype(F32)
        mean_d = jnp.mean(d_normed, axis=-1, keepdims=True)
        mean_dn = jnp.mean(d_normed * unit, axis=-1, keepdims=True)
        d_x = rstd[rows, :] * (d_normed - mean_d - unit * mean_dn)
        d_hist[rows, :] = (d_x + g_hist[rows, :].astype(F32)).astype(BF16)
        return carry

    lax.fori_loop(0, hist_rows // BLK, back, 0)

    def pick(i, carry):
        rows = pl.ds(pl.multiple_of(i * BLK, BLK), BLK)
        row = lax.broadcasted_iota(jnp.int32, (1, hist_rows), 1)
        onehot = one_hot(pos_col[rows, :] == row)
        slot_grads[rows, :] = mm(onehot, d_hist[...]).astype(BF16)
        return carry

    lax.fori_loop(0, slot_grads.shape[0] // BLK, pick, 0)


def cand_kernel(first_ref, rows, out):
    count, feature = out.shape
    own = first_ref[0] + lax.broadcasted_iota(jnp.int32, (count, 1), 0)
    total = jnp.zeros((count, feature), F32)
    for peer in range(rows.shape[0]):
        high = rows[peer, count : count + 16, :count].astype(F32)[:1]
        low = rows[peer, count : count + 16, count : 2 * count].astype(F32)[:1]
        ids = (high * 64.0 + low).astype(jnp.int32)
        total = total + mm(one_hot(own == ids), rows[peer, :count, :])
    out[...] = total


def reduce_kernel(pieces, slot_grads, copies):
    del slot_grads
    total = jnp.sum(pieces[...].astype(F32), axis=0).astype(BF16)
    for peer in range(copies.shape[0]):
        copies[peer] = total


def sums_kernel(pieces_in, d_proj_o, d_out_o, pieces, d_proj, d_out, sems, sent):
    feature = d_out.shape[1]
    quarter = d_out.shape[0] // 8
    count = pieces.shape[0]
    parts = fetch([(pieces_in.at[k], pieces.at[k]) for k in range(count)], sems)
    leaving = []
    for k in range(count):
        parts[k].wait()
        first = ((k % 2) * 4 + k // 2) * quarter
        rows = slice(first, first + quarter)
        for part in range(5):
            for group, source_cols, cols in segments(part, feature):
                piece = pieces[k, :, group, :, source_cols].astype(F32)
                piece = piece.reshape(quarter, cols.stop - cols.start)
                if part < 4:
                    base = part * feature
                    d_proj[rows, base + cols.start : base + cols.stop] = piece
                else:
                    d_out[rows, cols] = piece
        own = pl.ds(first, quarter)
        leaving.append(pltpu.make_async_copy(d_proj.at[own], d_proj_o.at[own], sent.at[2 * k]))
        leaving.append(pltpu.make_async_copy(d_out.at[own], d_out_o.at[own], sent.at[2 * k + 1]))
        leaving[-2].start()
        leaving[-1].start()
    for copy in leaving:
        copy.wait()


VMEM = pl.BlockSpec(memory_space=pltpu.VMEM)
SMEM = pl.BlockSpec(memory_space=pltpu.SMEM)
ANY = pl.BlockSpec(memory_space=pl.ANY)


def params(mib):
    return pltpu.CompilerParams(vmem_limit_bytes=mib << 20)


def cost(flops, nbytes):
    return pl.CostEstimate(flops=flops, bytes_accessed=nbytes, transcendentals=0)


def local(
    send_rows, slot_pos, lengths, candidates, target_ids, w_proj, w_out, g_hist, g_tgt
):
    peers, capacity, feature = send_rows.shape[1:]
    slots = peers * capacity
    hist_rows, tgt_rows = g_hist.shape[0], g_tgt.shape[0]
    blocks = hist_rows // BLK
    each = target_ids.shape[1]
    table = lax.all_gather(candidates, "mem", axis=0, tiled=True)
    arrived = lax.all_to_all(send_rows, BOTH, split_axis=1, concat_axis=0, tiled=True)
    arrived = arrived.reshape(slots, feature)

    pos_row = slot_pos.reshape(1, slots)
    pos_col = slot_pos.reshape(slots, 1)
    ends = jnp.cumsum(lengths[0])
    starts = ends - lengths[0]
    row = jnp.arange(0, hist_rows, BLK, dtype=jnp.int32)[:, None]
    first = jnp.max(jnp.where(row >= starts[None, :], starts[None, :], 0), axis=1) // BLK
    first = first.astype(jnp.int32)
    tgt_lo = jnp.repeat(starts, each).astype(jnp.int32)[:, None]
    tgt_hi = jnp.repeat(ends - 1, each).astype(jnp.int32)[:, None]
    core = lax.rem(lax.axis_index("grp"), 2).astype(jnp.int32)[None]

    sds = jax.ShapeDtypeStruct

    def by_rows(width):
        return pl.BlockSpec((BLK, width), lambda i: (i, 0))

    def whole(*shape):
        return pl.BlockSpec(shape, lambda i: (0,) * len(shape))

    x_hist, normed, rstd, normed_t, acts, slopes = pl.pallas_call(
        project_kernel,
        grid=(blocks,),
        out_shape=(
            sds((hist_rows, feature), BF16),
            sds((hist_rows, feature), BF16),
            sds((hist_rows, 1), F32),
            sds((feature, hist_rows), BF16),
            sds((hist_rows, 4 * feature), BF16),
            sds((hist_rows, 4 * feature), BF16),
        ),
        in_specs=[whole(slots, feature), whole(1, slots), whole(feature, 4 * feature)],
        out_specs=(
            by_rows(feature),
            by_rows(feature),
            by_rows(1),
            pl.BlockSpec((feature, BLK), lambda i: (0, i)),
            by_rows(4 * feature),
            by_rows(4 * feature),
        ),
        compiler_params=params(56),
        cost_estimate=cost(5 << 30, 20 << 20),
        name="project",
    )(arrived, pos_row, w_proj)

    scratch = pltpu.VMEM
    out_tgt, d_tgt, dk_t, dv_t, tgt_t, tgt_pre = pl.pallas_call(
        tgt_kernel,
        out_shape=(
            sds((tgt_rows, feature), BF16),
            sds((tgt_rows + 16, feature), BF16),
            sds((feature, hist_rows), BF16),
            sds((feature, hist_rows), BF16),
            sds((2, feature, tgt_rows), BF16),
            sds((tgt_rows, 4 * feature), BF16),
        ),
        in_specs=[VMEM] * 8 + [ANY],
        out_specs=(VMEM,) * 6,
        scratch_shapes=[
            scratch((hist_rows, feature), BF16),
            scratch((hist_rows, feature), BF16),
            pltpu.SemaphoreType.DMA((2,)),
            scratch((tgt_rows, 4 * feature), BF16),
            scratch((blocks + 1, PAIRS, 2 * tgt_rows, BLK), BF16),
            scratch((blocks + 1, PAIRS, 2 * tgt_rows, BLK), BF16),
            scratch((tgt_rows, BLK), F32),
            scratch((tgt_rows, tgt_rows), F32),
            scratch((PAIRS, 2 * tgt_rows, 128), F32),
            scratch((PAIRS, 2 * tgt_rows, 128), F32),
            scratch((PAIRS, 2 * tgt_rows, 128), BF16),
            scratch((PAIRS, 2 * tgt_rows, 128), BF16),
            scratch((PAIRS, 128, 2 * tgt_rows), BF16),
            scratch((PAIRS, 128, 2 * tgt_rows), BF16),
            scratch((feature, tgt_rows), F32),
            scratch((feature, tgt_rows), F32),
        ],
        compiler_params=params(56),
        cost_estimate=cost(6 << 30, 16 << 20),
        name="tgt",
    )(
        table,
        target_ids.reshape(tgt_rows, 1),
        target_ids.reshape(1, tgt_rows),
        tgt_lo,
        tgt_hi,
        w_proj,
        w_out,
        g_tgt,
        acts,
    )
    tgt_grads = lax.all_gather(d_tgt, "mem", axis=0, tiled=False)

    pieces = (16, 4, 16, 640)
    out_hist, keep, give, d_pre = pl.pallas_call(
        hist_kernel,
        out_shape=(
            sds((hist_rows, feature), BF16),
            sds(pieces, BF16),
            sds(pieces, BF16),
            sds((hist_rows, 4 * feature), BF16),
        ),
        in_specs=[SMEM] * 3 + [VMEM] * 5 + [ANY] * 6,
        out_specs=(ANY, VMEM, ANY, ANY),
        scratch_shapes=[
            scratch((hist_rows, 4 * feature), BF16),
            scratch((hist_rows, feature), BF16),
            scratch((hist_rows, 4 * feature), BF16),
            scratch((feature, hist_rows), BF16),
            scratch((feature, hist_rows), BF16),
            scratch((feature, hist_rows), F32),
            scratch((feature, hist_rows), F32),
            scratch((feature, hist_rows), BF16),
            scratch((feature, hist_rows), BF16),
            scratch((hist_rows, feature), BF16),
            scratch(pieces, BF16),
            pltpu.SemaphoreType.DMA((14,)),
            scratch((blocks, PAIRS, 2 * BLK, BLK), BF16),
            scratch((blocks, PAIRS, 2 * BLK, BLK), BF16),
            scratch((BLK, BLK), F32),
            scratch((PAIRS, 2 * BLK, 128), F32),
            scratch((PAIRS, 2 * BLK, 128), F32),
            scratch((PAIRS, 2 * BLK, 128), BF16),
            scratch((PAIRS, 2 * BLK, 128), BF16),
            scratch((PAIRS, 128, 2 * BLK), BF16),
            scratch((PAIRS, 128, 2 * BLK), BF16),
        ],
        compiler_params=params(56),
        cost_estimate=cost(18 << 30, 24 << 20),
        name="hist",
    )(
        core,
        first,
        starts.astype(jnp.int32),
        w_out,
        g_hist,
        g_tgt,
        tgt_t,
        tgt_pre,
        acts,
        x_hist,
        slopes,
        dv_t,
        dk_t,
        normed_t,
    )

    swapped = lax.ppermute(give, BOTH, core_swap())
    chip_sum = (keep.astype(F32) + swapped.astype(F32)).astype(BF16)
    chip_sum = chip_sum.reshape(64, 1, 16, 640)
    scattered = lax.all_to_all(
        chip_sum, BOTH, split_axis=0, concat_axis=1, tiled=True, axis_index_groups=same_core()
    )
    slot_grads = pl.pallas_call(
        rows_kernel,
        out_shape=sds((slots, feature), BF16),
        in_specs=[VMEM] * 6,
        out_specs=VMEM,
        scratch_shapes=[scratch((hist_rows, feature), BF16)],
        compiler_params=params(56),
        cost_estimate=cost(5 << 30, 16 << 20),
        name="rows",
    )(d_pre, w_proj, normed, rstd, g_hist, pos_col)
    copies = pl.pallas_call(
        reduce_kernel,
        out_shape=sds((16, 16, 640), BF16),
        in_specs=[VMEM, ANY],
        out_specs=VMEM,
        compiler_params=params(16),
        name="reduce",
    )(scattered.reshape(64, 16, 640), slot_grads)
    level = lax.all_to_all(
        copies.reshape(16, 1, 16, 640), "mem", split_axis=0, concat_axis=1, tiled=True
    ).reshape(256, 640)
    everything = lax.all_gather(level, "grp", axis=0, tiled=True)

    returned = lax.all_to_all(
        slot_grads.reshape(peers, 1, capacity, feature),
        BOTH,
        split_axis=0,
        concat_axis=1,
        tiled=True,
    )
    sum_proj, sum_out = pl.pallas_call(
        sums_kernel,
        out_shape=(sds(w_proj.shape, F32), sds(w_out.shape, F32)),
        in_specs=[ANY],
        out_specs=(ANY, ANY),
        scratch_shapes=[
            scratch((8, 4, 4, 16, 640), BF16),
            scratch(w_proj.shape, F32),
            scratch(w_out.shape, F32),
            pltpu.SemaphoreType.DMA((8,)),
            pltpu.SemaphoreType.DMA((16,)),
        ],
        compiler_params=params(60),
        name="sums",
    )(everything.reshape(8, 4, 4, 16, 640))

    mine = (lax.axis_index("mem") * candidates.shape[0]).astype(jnp.int32)[None]
    d_cand = pl.pallas_call(
        cand_kernel,
        out_shape=sds(candidates.shape, F32),
        in_specs=[SMEM, VMEM],
        out_specs=VMEM,
        compiler_params=params(56),
        name="cand",
    )(mine, tgt_grads)
    return (out_hist, out_tgt, returned, d_cand, sum_proj, sum_out)


def core_swap():
    return [(i, i + 16 if (i // 16) % 2 == 0 else i - 16) for i in range(128)]


def same_core():
    return [[i for i in range(128) if (i // 16) % 2 == core] for core in (0, 1)]


def solution(mesh):
    placed = (
        P(BOTH, None, None, None),
        P(BOTH, None, None),
        P(BOTH, None),
        P(BOTH, None),
        P(BOTH, None),
        P(),
        P(),
        P(BOTH, None),
        P(BOTH, None),
    )
    return jax.shard_map(
        local,
        mesh=mesh,
        in_specs=placed,
        out_specs=(
            P(BOTH, None),
            P(BOTH, None),
            P(BOTH, None, None, None),
            P(BOTH, None),
            P(),
            P(),
        ),
        check_vma=False,
    )
```

```python
import jax
import jax.numpy as jnp
from jax import lax
from jax.experimental import pallas as pl
from jax.experimental.pallas import tpu as pltpu
from jax.sharding import PartitionSpec as P

HEADS = 8
PAIRS = HEADS // 2
EPS = 1e-05
BLK = 256
MASKED = -1e9
F32 = jnp.float32
BF16 = jnp.bfloat16
BOTH = ("grp", "mem")
NN = (((1,), (0,)), ((), ()))
NT = (((1,), (1,)), ((), ()))


def mm(left, right, dims=NN):
    return lax.dot_general(left, right, dims, preferred_element_type=F32)


def moments(values):
    centred = values - jnp.mean(values, axis=-1, keepdims=True)
    variance = jnp.mean(centred * centred, axis=-1, keepdims=True)
    return centred, lax.rsqrt(variance + EPS)


def head_masks():
    lane = lax.broadcasted_iota(jnp.int32, (1, 128), 1)
    low_half = jnp.where(lane < 64, 1.0, 0.0).astype(F32)
    return (low_half, 1.0 - low_half)


def silu_parts(half):
    t = jnp.tanh(half)
    u = 1.0 + t
    return half * u, 0.5 * u * (1.0 + half * (1.0 - t))


def one_hot(hits):
    return jnp.where(hits, 1.0, 0.0).astype(BF16)


def score_bias(lo, hi, k0):
    key = k0 + lax.broadcasted_iota(jnp.int32, (1, BLK), 1)
    allowed = (key >= lo) & (key <= hi)
    return jnp.where(allowed, 0.0, MASKED).astype(F32)


def stack_heads(rows, dest, size):
    for pair in range(PAIRS):
        both = rows[:, pair * 128 : (pair + 1) * 128]
        for place, keep in enumerate(head_masks()):
            dest[pair, place * size : (place + 1) * size, :] = (both * keep).astype(BF16)


def stack_columns(rows_t, dest, size):
    for head in range(HEADS):
        pair, place = head // 2, head % 2
        own = rows_t[head * 64 : (head + 1) * 64, :].astype(BF16)
        dest[pair, place * 64 : (place + 1) * 64, place * size : (place + 1) * size] = own


def merge_heads(acc, size):
    first, second = head_masks()
    return jnp.concatenate(
        [acc[pair, :size, :] * first + acc[pair, size:, :] * second for pair in range(PAIRS)],
        axis=1,
    )


def forward(q_st, k_ref, v_ref, keys, w_s, s_s, slot, bias, a_acc):
    size, width = bias.shape
    for pair in range(PAIRS):
        cols = slice(pair * 128, (pair + 1) * 128)
        half = mm(q_st[pair], k_ref[keys, cols], NT).reshape(2, size, width)
        weight, slope = silu_parts((half + bias[...][None]).reshape(2 * size, width))
        weight = weight.astype(BF16)
        w_s[slot, pair, :, :width] = weight
        s_s[slot, pair, :, :width] = slope.astype(BF16)
        a_acc[pair] += mm(weight, v_ref[keys, cols])


def backward(q_t, k_ref, v_ref, keys, width, w_s, s_s, slot, da_st, da_t, dq_acc, dk_t, dv_t, add):
    for pair in range(PAIRS):
        cols = slice(pair * 128, (pair + 1) * 128)
        d_weight = mm(da_st[pair], v_ref[keys, cols], NT)
        d_score = (d_weight * s_s[slot, pair, :, :width].astype(F32)).astype(BF16)
        dq_acc[pair] += mm(d_score, k_ref[keys, cols])
        d_val = mm(da_t[pair], w_s[slot, pair, :, :width])
        d_key = mm(q_t[pair], d_score)
        if add:
            dv_t[cols, keys] += d_val
            dk_t[cols, keys] += d_key
        else:
            dv_t[cols, keys] = d_val.astype(dv_t.dtype)
            dk_t[cols, keys] = d_key.astype(dk_t.dtype)


def middle(attended, x, gate, g, w_out):
    centred, rstd = moments(attended)
    normed = centred * rstd
    mixed = normed * gate
    out = (x + mm(mixed.astype(BF16), w_out)).astype(BF16)
    d_mixed = mm(g, w_out, NT)
    d_normed = d_mixed * gate
    mean_d = jnp.mean(d_normed, axis=-1, keepdims=True)
    mean_dn = jnp.mean(d_normed * normed, axis=-1, keepdims=True)
    d_att = rstd * (d_normed - mean_d - normed * mean_dn)
    return out, mixed, d_mixed * normed, d_att


def project_kernel(
    arrived, pos_row, w_proj, x_o, normed_o, rstd_o, normed_t, acts, slopes
):
    size, feature = x_o.shape
    row = pl.program_id(0) * size + lax.broadcasted_iota(jnp.int32, (size, 1), 0)
    x = mm(one_hot(pos_row[...] == row), arrived[...])
    x_o[...] = x.astype(BF16)
    centred, rstd = moments(x)
    normed = centred * rstd
    rstd_o[...] = rstd
    normed_t[...] = normed.T.astype(BF16)
    normed = normed.astype(BF16)
    normed_o[...] = normed
    for part in range(4):
        cols = slice(part * feature, (part + 1) * feature)
        act, slope = silu_parts(mm(normed, w_proj[:, cols]) * 0.5)
        slopes[:, cols] = slope.astype(BF16)
        act = act.astype(BF16)
        acts[:, cols] = (act * 0.0625).astype(BF16) if part == 2 else act


def fetch(pairs, sems):
    copies = [pltpu.make_async_copy(src, dst, sems.at[i]) for i, (src, dst) in enumerate(pairs)]
    for copy in copies:
        copy.start()
    return copies


def tgt_kernel(
    cand,
    tid_col,
    tid_row,
    lo,
    hi,
    w_proj,
    w_out,
    g_tgt,
    acts_in,
    out_tgt,
    d_tgt,
    dk_o,
    dv_o,
    tgt_t,
    d_pre,
    k_s,
    v_s,
    sems,
    acts,
    w_s,
    s_s,
    bias_s,
    own_bias,
    a_acc,
    dq_acc,
    q_st,
    da_st,
    q_t,
    da_t,
    dk_own,
    dv_own,
):
    feature = out_tgt.shape[1]
    copies = fetch(
        [(acts_in.at[:, 3 * feature :], k_s), (acts_in.at[:, feature : 2 * feature], v_s)], sems
    )
    tgt_rows = out_tgt.shape[0]
    blocks = k_s.shape[0] // BLK
    every = slice(0, tgt_rows)
    part_cols = [slice(part * feature, (part + 1) * feature) for part in range(4)]
    col = lax.broadcasted_iota(jnp.int32, (1, cand.shape[0]), 1)
    x = mm(one_hot(tid_col[...] == col), cand[...])
    centred, rstd = moments(x)
    unit = centred * rstd
    normed = unit.astype(BF16)
    tgt_t[0] = unit.T.astype(BF16)
    for part in range(4):
        half = mm(normed, w_proj[:, part_cols[part]]) * 0.5
        act, slope = silu_parts(half)
        d_pre[:, part_cols[part]] = slope.astype(BF16)
        act = act.astype(BF16)
        acts[:, part_cols[part]] = (act * 0.0625).astype(BF16) if part == 2 else act
    qry = acts[:, part_cols[2]].astype(F32)
    q_t[...] = jnp.zeros_like(q_t)
    da_t[...] = jnp.zeros_like(da_t)
    stack_heads(qry, q_st, tgt_rows)
    stack_columns(qry.T, q_t, tgt_rows)

    a_acc[...] = jnp.zeros_like(a_acc)
    dq_acc[...] = jnp.zeros_like(dq_acc)
    for copy in copies:
        copy.wait()

    def fwd(j, c):
        k0 = pl.multiple_of(j * BLK, BLK)
        bias_s[...] = score_bias(lo[...], hi[...], k0)
        forward(q_st, k_s, v_s, pl.ds(k0, BLK), w_s, s_s, j, bias_s, a_acc)
        return c

    def bwd(j, c):
        keys = pl.ds(pl.multiple_of(j * BLK, BLK), BLK)
        backward(q_t, k_s, v_s, keys, BLK, w_s, s_s, j, da_st, da_t, dq_acc, dk_o, dv_o, False)
        return c

    lax.fori_loop(0, blocks, fwd, 0)
    same = lax.broadcasted_iota(jnp.int32, (tgt_rows, tgt_rows), 0) == lax.broadcasted_iota(
        jnp.int32, (tgt_rows, tgt_rows), 1
    )
    own_bias[...] = jnp.where(same, 0.0, MASKED).astype(F32)
    k_own, v_own = acts.at[:, part_cols[3]], acts.at[:, part_cols[1]]
    forward(q_st, k_own, v_own, every, w_s, s_s, blocks, own_bias, a_acc)
    gate = acts[:, part_cols[0]].astype(F32)
    out, mixed, d_gate, d_att = middle(merge_heads(a_acc, tgt_rows), x, gate, g_tgt[...], w_out[...])
    out_tgt[...] = out
    tgt_t[1] = mixed.T.astype(BF16)
    d_pre[:, part_cols[0]] = (d_gate * d_pre[:, part_cols[0]].astype(F32)).astype(BF16)
    stack_heads(d_att, da_st, tgt_rows)
    stack_columns(d_att.T, da_t, tgt_rows)
    lax.fori_loop(0, blocks, bwd, 0)
    backward(
        q_t, k_own, v_own, every, tgt_rows, w_s, s_s, blocks, da_st, da_t, dq_acc, dk_own, dv_own,
        False,
    )
    d_q = merge_heads(dq_acc, tgt_rows) * 0.125
    grads = (None, dv_own[...].T, d_q, dk_own[...].T * 2.0)
    for part in (1, 2, 3):
        d_part = grads[part] * d_pre[:, part_cols[part]].astype(F32)
        d_pre[:, part_cols[part]] = d_part.astype(BF16)

    d_normed = mm(d_pre[...], w_proj[...], NT)
    mean_d = jnp.mean(d_normed, axis=-1, keepdims=True)
    mean_dn = jnp.mean(d_normed * unit, axis=-1, keepdims=True)
    d_x = rstd * (d_normed - mean_d - unit * mean_dn) + g_tgt[...].astype(F32)
    d_tgt[every, :] = d_x.astype(BF16)
    ids = tid_row[...]
    high = lax.shift_right_logical(ids, 6)
    low = ids - high * 64
    d_tgt[tgt_rows:, :] = jnp.zeros((d_tgt.shape[0] - tgt_rows, feature), BF16)
    wide = (d_tgt.shape[0] - tgt_rows, tgt_rows)
    d_tgt[tgt_rows:, :tgt_rows] = jnp.broadcast_to(high.astype(F32), wide).astype(BF16)
    d_tgt[tgt_rows:, tgt_rows : 2 * tgt_rows] = jnp.broadcast_to(low.astype(F32), wide).astype(BF16)


def hist_kernel(
    core_ref,
    first_ref,
    starts_ref,
    w_out,
    g_hist,
    g_tgt,
    tgt_t,
    tgt_pre,
    acts_in,
    x_in,
    slopes_in,
    dv_in,
    dk_in,
    normed_t_in,
    out_hist,
    keep,
    give,
    d_pre_o,
    acts,
    x_s,
    d_pre,
    dv_add,
    dk_add,
    dv_t,
    dk_t,
    normed_t,
    mixed_t,
    out_s,
    give_s,
    sems,
    w_s,
    s_s,
    bias_s,
    a_acc,
    dq_acc,
    q_st,
    da_st,
    q_t,
    da_t,
):
    hist_rows, feature = g_hist.shape
    blocks = hist_rows // BLK
    part_cols = [slice(part * feature, (part + 1) * feature) for part in range(4)]
    gates, vals, qrys, ids = part_cols
    later = slice(2 * feature, 4 * feature)
    copies = fetch(
        [
            (acts_in.at[:, later], acts.at[:, later]),
            (acts_in.at[:, vals], acts.at[:, vals]),
            (acts_in.at[:, gates], acts.at[:, gates]),
            (x_in, x_s),
            (slopes_in.at[:, gates], d_pre.at[:, gates]),
            (slopes_in.at[:, qrys], d_pre.at[:, qrys]),
            (slopes_in.at[:, vals], d_pre.at[:, vals]),
            (slopes_in.at[:, ids], d_pre.at[:, ids]),
            (dv_in, dv_add),
            (dk_in, dk_add),
            (normed_t_in, normed_t),
        ],
        sems,
    )
    k_ref, v_ref = acts.at[:, part_cols[3]], acts.at[:, part_cols[1]]
    q_t[...] = jnp.zeros_like(q_t)
    da_t[...] = jnp.zeros_like(da_t)
    dk_t[...] = jnp.zeros_like(dk_t)
    dv_t[...] = jnp.zeros_like(dv_t)
    for copy in copies[:2]:
        copy.wait()

    def hist_block(n, carry):
        i = blocks - 1 - n
        r0 = pl.multiple_of(i * BLK, BLK)
        rows = pl.ds(r0, BLK)
        first = first_ref[i]
        row = r0 + lax.broadcasted_iota(jnp.int32, (BLK, 1), 0)
        lo = jnp.zeros((BLK, 1), jnp.int32)
        for user in range(starts_ref.shape[0]):
            lo = jnp.where(row >= starts_ref[user], starts_ref[user], lo)
        a_acc[...] = jnp.zeros_like(a_acc)
        dq_acc[...] = jnp.zeros_like(dq_acc)
        qry = acts[rows, part_cols[2]].astype(F32)
        stack_heads(qry, q_st, BLK)
        stack_columns(qry.T, q_t, BLK)

        def fwd(j, c):
            k0 = pl.multiple_of(j * BLK, BLK)
            bias_s[...] = score_bias(lo, row, k0)
            forward(q_st, k_ref, v_ref, pl.ds(k0, BLK), w_s, s_s, j, bias_s, a_acc)
            return c

        def bwd(j, c):
            keys = pl.ds(pl.multiple_of(j * BLK, BLK), BLK)
            backward(
                q_t, k_ref, v_ref, keys, BLK, w_s, s_s, j, da_st, da_t, dq_acc, dk_t, dv_t, True
            )
            return c

        lax.fori_loop(first, i + 1, fwd, 0)

        @pl.when(n == 0)
        def _():
            for copy in copies[2:5]:
                copy.wait()

        out, mixed, d_gate, d_att = middle(
            merge_heads(a_acc, BLK),
            x_s[rows, :].astype(F32),
            acts[rows, part_cols[0]].astype(F32),
            g_hist[rows, :],
            w_out[...],
        )
        out_s[rows, :] = out
        mixed_t[:, rows] = mixed.T.astype(BF16)
        d_pre[rows, part_cols[0]] = (d_gate * d_pre[rows, part_cols[0]].astype(F32)).astype(BF16)
        stack_heads(d_att, da_st, BLK)
        stack_columns(d_att.T, da_t, BLK)
        lax.fori_loop(first, i + 1, bwd, 0)

        @pl.when(n == 0)
        def _():
            copies[5].wait()

        d_q = merge_heads(dq_acc, BLK) * 0.125 * d_pre[rows, part_cols[2]].astype(F32)
        d_pre[rows, part_cols[2]] = d_q.astype(BF16)
        return carry

    lax.fori_loop(0, blocks, hist_block, 0)
    count = len(copies)
    sent_out = pltpu.make_async_copy(out_s, out_hist, sems.at[count])
    sent_out.start()
    for copy in copies[6:]:
        copy.wait()

    def spread(i, carry):
        rows = pl.ds(pl.multiple_of(i * BLK, BLK), BLK)
        vals, keys = part_cols[1], part_cols[3]
        d_pre[rows, vals] = ((dv_t[:, rows] + dv_add[:, rows].astype(F32)).T * d_pre[rows, vals].astype(F32)).astype(BF16)
        d_pre[rows, keys] = ((dk_t[:, rows] + dk_add[:, rows].astype(F32)).T * 2.0 * d_pre[rows, keys].astype(F32)).astype(BF16)
        return carry

    lax.fori_loop(0, blocks, spread, 0)
    sent = pltpu.make_async_copy(d_pre, d_pre_o, sems.at[count + 1])
    sent.start()

    core = core_ref[0]
    half_rows = feature // 2
    sent_give = pltpu.make_async_copy(give_s, give, sems.at[count + 2])
    for dest, half in ((give_s, 1 - core), (keep, core)):
        rows = pl.ds(pl.multiple_of(half * half_rows, half_rows), half_rows)
        for part in range(5):
            if part < 4:
                total = mm(normed_t[rows, :], d_pre[:, part_cols[part]])
                total = total + mm(tgt_t[0, rows, :], tgt_pre[:, part_cols[part]])
            else:
                total = mm(mixed_t[rows, :], g_hist[...]) + mm(tgt_t[1, rows, :], g_tgt[...])
            for group, dest_cols, cols in segments(part, feature):
                piece = total[:, cols].reshape(16, 16, cols.stop - cols.start)
                dest[:, group, :, dest_cols] = piece.astype(BF16)
        if dest is give_s:
            sent_give.start()
    sent_out.wait()
    sent.wait()
    sent_give.wait()


def segments(part, feature):
    found, begin = [], part * feature
    while begin < (part + 1) * feature:
        group = begin // 640
        end = min((part + 1) * feature, (group + 1) * 640)
        found.append(
            (group, slice(begin - group * 640, end - group * 640), slice(begin - part * feature, end - part * feature))
        )
        begin = end
    return found


def rows_kernel(d_pre, w_proj, normed, rstd, g_hist, pos_col, slot_grads, d_hist):
    hist_rows, feature = g_hist.shape

    def back(i, carry):
        rows = pl.ds(pl.multiple_of(i * BLK, BLK), BLK)
        d_normed = mm(d_pre[rows, :], w_proj[...], NT)
        unit = normed[rows, :].astype(F32)
        mean_d = jnp.mean(d_normed, axis=-1, keepdims=True)
        mean_dn = jnp.mean(d_normed * unit, axis=-1, keepdims=True)
        d_x = rstd[rows, :] * (d_normed - mean_d - unit * mean_dn)
        d_hist[rows, :] = (d_x + g_hist[rows, :].astype(F32)).astype(BF16)
        return carry

    lax.fori_loop(0, hist_rows // BLK, back, 0)

    def pick(i, carry):
        rows = pl.ds(pl.multiple_of(i * BLK, BLK), BLK)
        row = lax.broadcasted_iota(jnp.int32, (1, hist_rows), 1)
        onehot = one_hot(pos_col[rows, :] == row)
        slot_grads[rows, :] = mm(onehot, d_hist[...]).astype(BF16)
        return carry

    lax.fori_loop(0, slot_grads.shape[0] // BLK, pick, 0)


def cand_kernel(first_ref, rows, out):
    count, feature = out.shape
    own = first_ref[0] + lax.broadcasted_iota(jnp.int32, (count, 1), 0)
    total = jnp.zeros((count, feature), F32)
    for peer in range(rows.shape[0]):
        high = rows[peer, count : count + 16, :count].astype(F32)[:1]
        low = rows[peer, count : count + 16, count : 2 * count].astype(F32)[:1]
        ids = (high * 64.0 + low).astype(jnp.int32)
        total = total + mm(one_hot(own == ids), rows[peer, :count, :])
    out[...] = total


def reduce_kernel(pieces, slot_grads, copies):
    del slot_grads
    total = jnp.sum(pieces[...].astype(F32), axis=0).astype(BF16)
    for peer in range(copies.shape[0]):
        copies[peer] = total


def sums_kernel(pieces_in, d_proj_o, d_out_o, pieces, d_proj, d_out, sems, sent):
    feature = d_out.shape[1]
    quarter = d_out.shape[0] // 8
    count = pieces.shape[0]
    parts = fetch([(pieces_in.at[k], pieces.at[k]) for k in range(count)], sems)
    leaving = []
    for k in range(count):
        parts[k].wait()
        first = ((k % 2) * 4 + k // 2) * quarter
        rows = slice(first, first + quarter)
        for part in range(5):
            for group, source_cols, cols in segments(part, feature):
                piece = pieces[k, :, group, :, source_cols].astype(F32)
                piece = piece.reshape(quarter, cols.stop - cols.start)
                if part < 4:
                    base = part * feature
                    d_proj[rows, base + cols.start : base + cols.stop] = piece
                else:
                    d_out[rows, cols] = piece
        own = pl.ds(first, quarter)
        leaving.append(pltpu.make_async_copy(d_proj.at[own], d_proj_o.at[own], sent.at[2 * k]))
        leaving.append(pltpu.make_async_copy(d_out.at[own], d_out_o.at[own], sent.at[2 * k + 1]))
        leaving[-2].start()
        leaving[-1].start()
    for copy in leaving:
        copy.wait()


VMEM = pl.BlockSpec(memory_space=pltpu.VMEM)
SMEM = pl.BlockSpec(memory_space=pltpu.SMEM)
ANY = pl.BlockSpec(memory_space=pl.ANY)


def params(mib):
    return pltpu.CompilerParams(vmem_limit_bytes=mib << 20)


def cost(flops, nbytes):
    return pl.CostEstimate(flops=flops, bytes_accessed=nbytes, transcendentals=0)


def local(
    send_rows, slot_pos, lengths, candidates, target_ids, w_proj, w_out, g_hist, g_tgt
):
    peers, capacity, feature = send_rows.shape[1:]
    slots = peers * capacity
    hist_rows, tgt_rows = g_hist.shape[0], g_tgt.shape[0]
    blocks = hist_rows // BLK
    each = target_ids.shape[1]
    table = lax.all_gather(candidates, "mem", axis=0, tiled=True)
    arrived = lax.all_to_all(send_rows, BOTH, split_axis=1, concat_axis=0, tiled=True)
    arrived = arrived.reshape(slots, feature)

    pos_row = slot_pos.reshape(1, slots)
    pos_col = slot_pos.reshape(slots, 1)
    ends = jnp.cumsum(lengths[0])
    starts = ends - lengths[0]
    row = jnp.arange(0, hist_rows, BLK, dtype=jnp.int32)[:, None]
    first = jnp.max(jnp.where(row >= starts[None, :], starts[None, :], 0), axis=1) // BLK
    first = first.astype(jnp.int32)
    tgt_lo = jnp.repeat(starts, each).astype(jnp.int32)[:, None]
    tgt_hi = jnp.repeat(ends - 1, each).astype(jnp.int32)[:, None]
    core = lax.rem(lax.axis_index("grp"), 2).astype(jnp.int32)[None]

    sds = jax.ShapeDtypeStruct

    def by_rows(width):
        return pl.BlockSpec((BLK, width), lambda i: (i, 0))

    def whole(*shape):
        return pl.BlockSpec(shape, lambda i: (0,) * len(shape))

    x_hist, normed, rstd, normed_t, acts, slopes = pl.pallas_call(
        project_kernel,
        grid=(blocks,),
        out_shape=(
            sds((hist_rows, feature), BF16),
            sds((hist_rows, feature), BF16),
            sds((hist_rows, 1), F32),
            sds((feature, hist_rows), BF16),
            sds((hist_rows, 4 * feature), BF16),
            sds((hist_rows, 4 * feature), BF16),
        ),
        in_specs=[whole(slots, feature), whole(1, slots), whole(feature, 4 * feature)],
        out_specs=(
            by_rows(feature),
            by_rows(feature),
            by_rows(1),
            pl.BlockSpec((feature, BLK), lambda i: (0, i)),
            by_rows(4 * feature),
            by_rows(4 * feature),
        ),
        compiler_params=params(56),
        cost_estimate=cost(5 << 30, 20 << 20),
        name="project",
    )(arrived, pos_row, w_proj)

    scratch = pltpu.VMEM
    out_tgt, d_tgt, dk_t, dv_t, tgt_t, tgt_pre = pl.pallas_call(
        tgt_kernel,
        out_shape=(
            sds((tgt_rows, feature), BF16),
            sds((tgt_rows + 16, feature), BF16),
            sds((feature, hist_rows), BF16),
            sds((feature, hist_rows), BF16),
            sds((2, feature, tgt_rows), BF16),
            sds((tgt_rows, 4 * feature), BF16),
        ),
        in_specs=[VMEM] * 8 + [ANY],
        out_specs=(VMEM,) * 6,
        scratch_shapes=[
            scratch((hist_rows, feature), BF16),
            scratch((hist_rows, feature), BF16),
            pltpu.SemaphoreType.DMA((2,)),
            scratch((tgt_rows, 4 * feature), BF16),
            scratch((blocks + 1, PAIRS, 2 * tgt_rows, BLK), BF16),
            scratch((blocks + 1, PAIRS, 2 * tgt_rows, BLK), BF16),
            scratch((tgt_rows, BLK), F32),
            scratch((tgt_rows, tgt_rows), F32),
            scratch((PAIRS, 2 * tgt_rows, 128), F32),
            scratch((PAIRS, 2 * tgt_rows, 128), F32),
            scratch((PAIRS, 2 * tgt_rows, 128), BF16),
            scratch((PAIRS, 2 * tgt_rows, 128), BF16),
            scratch((PAIRS, 128, 2 * tgt_rows), BF16),
            scratch((PAIRS, 128, 2 * tgt_rows), BF16),
            scratch((feature, tgt_rows), F32),
            scratch((feature, tgt_rows), F32),
        ],
        compiler_params=params(56),
        cost_estimate=cost(6 << 30, 16 << 20),
        name="tgt",
    )(
        table,
        target_ids.reshape(tgt_rows, 1),
        target_ids.reshape(1, tgt_rows),
        tgt_lo,
        tgt_hi,
        w_proj,
        w_out,
        g_tgt,
        acts,
    )
    tgt_grads = lax.all_gather(d_tgt, "mem", axis=0, tiled=False)

    pieces = (16, 4, 16, 640)
    out_hist, keep, give, d_pre = pl.pallas_call(
        hist_kernel,
        out_shape=(
            sds((hist_rows, feature), BF16),
            sds(pieces, BF16),
            sds(pieces, BF16),
            sds((hist_rows, 4 * feature), BF16),
        ),
        in_specs=[SMEM] * 3 + [VMEM] * 5 + [ANY] * 6,
        out_specs=(ANY, VMEM, ANY, ANY),
        scratch_shapes=[
            scratch((hist_rows, 4 * feature), BF16),
            scratch((hist_rows, feature), BF16),
            scratch((hist_rows, 4 * feature), BF16),
            scratch((feature, hist_rows), BF16),
            scratch((feature, hist_rows), BF16),
            scratch((feature, hist_rows), F32),
            scratch((feature, hist_rows), F32),
            scratch((feature, hist_rows), BF16),
            scratch((feature, hist_rows), BF16),
            scratch((hist_rows, feature), BF16),
            scratch(pieces, BF16),
            pltpu.SemaphoreType.DMA((14,)),
            scratch((blocks, PAIRS, 2 * BLK, BLK), BF16),
            scratch((blocks, PAIRS, 2 * BLK, BLK), BF16),
            scratch((BLK, BLK), F32),
            scratch((PAIRS, 2 * BLK, 128), F32),
            scratch((PAIRS, 2 * BLK, 128), F32),
            scratch((PAIRS, 2 * BLK, 128), BF16),
            scratch((PAIRS, 2 * BLK, 128), BF16),
            scratch((PAIRS, 128, 2 * BLK), BF16),
            scratch((PAIRS, 128, 2 * BLK), BF16),
        ],
        compiler_params=params(44),
        cost_estimate=cost(18 << 30, 24 << 20),
        name="hist",
    )(
        core,
        first,
        starts.astype(jnp.int32),
        w_out,
        g_hist,
        g_tgt,
        tgt_t,
        tgt_pre,
        acts,
        x_hist,
        slopes,
        dv_t,
        dk_t,
        normed_t,
    )

    swapped = lax.ppermute(give, BOTH, core_swap())
    chip_sum = (keep.astype(F32) + swapped.astype(F32)).astype(BF16)
    chip_sum = chip_sum.reshape(64, 1, 16, 640)
    scattered = lax.all_to_all(
        chip_sum, BOTH, split_axis=0, concat_axis=1, tiled=True, axis_index_groups=same_core()
    )
    slot_grads = pl.pallas_call(
        rows_kernel,
        out_shape=sds((slots, feature), BF16),
        in_specs=[VMEM] * 6,
        out_specs=VMEM,
        scratch_shapes=[scratch((hist_rows, feature), BF16)],
        compiler_params=params(56),
        cost_estimate=cost(5 << 30, 16 << 20),
        name="rows",
    )(d_pre, w_proj, normed, rstd, g_hist, pos_col)
    copies = pl.pallas_call(
        reduce_kernel,
        out_shape=sds((16, 16, 640), BF16),
        in_specs=[VMEM, ANY],
        out_specs=VMEM,
        compiler_params=params(16),
        name="reduce",
    )(scattered.reshape(64, 16, 640), slot_grads)
    level = lax.all_to_all(
        copies.reshape(16, 1, 16, 640), "mem", split_axis=0, concat_axis=1, tiled=True
    ).reshape(256, 640)
    everything = lax.all_gather(level, "grp", axis=0, tiled=True)

    returned = lax.all_to_all(
        slot_grads.reshape(peers, 1, capacity, feature),
        BOTH,
        split_axis=0,
        concat_axis=1,
        tiled=True,
    )
    sum_proj, sum_out = pl.pallas_call(
        sums_kernel,
        out_shape=(sds(w_proj.shape, F32), sds(w_out.shape, F32)),
        in_specs=[ANY],
        out_specs=(ANY, ANY),
        scratch_shapes=[
            scratch((8, 4, 4, 16, 640), BF16),
            scratch(w_proj.shape, F32),
            scratch(w_out.shape, F32),
            pltpu.SemaphoreType.DMA((8,)),
            pltpu.SemaphoreType.DMA((16,)),
        ],
        compiler_params=params(60),
        name="sums",
    )(everything.reshape(8, 4, 4, 16, 640))

    mine = (lax.axis_index("mem") * candidates.shape[0]).astype(jnp.int32)[None]
    d_cand = pl.pallas_call(
        cand_kernel,
        out_shape=sds(candidates.shape, F32),
        in_specs=[SMEM, VMEM],
        out_specs=VMEM,
        compiler_params=params(56),
        name="cand",
    )(mine, tgt_grads)
    return (out_hist, out_tgt, returned, d_cand, sum_proj, sum_out)


def core_swap():
    return [(i, i + 16 if (i // 16) % 2 == 0 else i - 16) for i in range(128)]


def same_core():
    return [[i for i in range(128) if (i // 16) % 2 == core] for core in (0, 1)]


def solution(mesh):
    placed = (
        P(BOTH, None, None, None),
        P(BOTH, None, None),
        P(BOTH, None),
        P(BOTH, None),
        P(BOTH, None),
        P(),
        P(),
        P(BOTH, None),
        P(BOTH, None),
    )
    return jax.shard_map(
        local,
        mesh=mesh,
        in_specs=placed,
        out_specs=(
            P(BOTH, None),
            P(BOTH, None),
            P(BOTH, None, None, None),
            P(BOTH, None),
            P(),
            P(),
        ),
        check_vma=False,
    )
```
